32 devices in a mesh: modes: 16 (over z, y, x), rows: 2 (over core).
Axes of the slice: x: 2, y: 2, z: 4, core: 2. Of those that a mesh axis runs over, the one named last changes fastest.
Arguments:
- forward: bfloat16 [16, 768, 1536], P('modes', 'rows'), may hold values from -6 to 6
- backward: bfloat16 [16, 768, 1536], P('modes', 'rows'), may hold values from -6 to 6
- targets: bfloat16 [2, 16, 768, 768], P(None, None, ('rows', 'modes')), may hold values from -0.0078125 to 0.0078125
Outputs:
- phase_plane: bfloat16 [768, 1536], P('rows')
- output_fields: bfloat16 [16, 768, 1536], P('modes', 'rows')
- coupling: float32 [32, 16], P(('modes', 'rows'))
The draws below stay inside these ranges and needn't reach their ends.
All inputs are finite; a program needn't handle non-finite values.
Results may differ from the reference program's by a relative error of at most 0.012.
Values may be sent and summed in bfloat16 or wider, within the bound.
No kernel may reach another device: no remote copies, remote signals or barrier semaphores. Data moves between devices by JAX's collectives and lax.ppermute only.
A program may use at most 64 MiB of HBM per device.

```python
import math
import jax
import jax.numpy as jnp
from jax import lax

GRID = 768
MODES = 16


def level_of(key, shape, shards, low, largest):
    def one(axis_at, shards_of):
        draws = jax.random.uniform(jax.random.fold_in(jax.random.fold_in(key, 6), axis_at), (shards_of,), jnp.float32, low / len(shards), largest / len(shards))
        return jnp.repeat(jnp.exp(draws), shape[axis_at] // shards_of).reshape((-1,) + (1,) * (len(shape) - axis_at - 1))

    factor_of = one(*shards[0])
    for cut in shards[1:]:
        factor_of = factor_of * one(*cut)
    return factor_of


def scatter_about(rng, shape, scale, limit, shards=(), kind=jnp.bfloat16):
    values = jax.random.normal(rng, shape, jnp.float32) * scale
    if len(shards) > 0:
        values = level_of(rng, shape, shards, -0.22, 0.18) * values
    return jnp.clip(values, min=-limit, max=limit).astype(kind)


def setup_inputs(seed: int = 0) -> dict:
    key_list = jax.random.split(jax.random.key(seed), 4)
    return {
        "forward": scatter_about(key_list[0], (MODES, GRID, 2 * GRID), 1.0, 6.0, ((0, 16), (1, 2))),
        "backward": scatter_about(key_list[1], (MODES, GRID, 2 * GRID), 1.0, 6.0, ((0, 16), (1, 2))),
        "targets": scatter_about(key_list[2], (2, MODES, GRID, GRID), (GRID * GRID) ** -0.5, 0.0078125, ((2, 32),)),
    }


two_pi = 2.0 * math.pi

def fourier_pair(row_index, col_index, grid_size):
    product = row_index[:, None] * col_index[None, :] % grid_size
    angles = product.astype(jnp.float32) * (two_pi / grid_size)
    factor = 1.0 / math.sqrt(grid_size)
    return (jnp.cos(angles) * factor, jnp.sin(angles) * factor)

def column_matrices(grid_size):
    index_all = jnp.arange(grid_size, dtype=jnp.int32)
    cosine, sine_part = fourier_pair(index_all, index_all, grid_size)
    forward_cols = jnp.concatenate([jnp.concatenate([cosine, -sine_part], 1), jnp.concatenate([sine_part, cosine], 1)], 0)
    inverse_cols = jnp.concatenate([jnp.concatenate([cosine, sine_part], 1), jnp.concatenate([-sine_part, cosine], 1)], 0)
    return (forward_cols.astype(jnp.bfloat16), inverse_cols.astype(jnp.bfloat16))

def spectral_phase(row_freq, col_freq, grid_size):

    def squared(freq):
        centred = (freq + grid_size // 2) % grid_size - grid_size // 2
        return centred * centred % (4 * grid_size)
    summed = (squared(row_freq)[:, None] + squared(col_freq)[None, :]) % (4 * grid_size)
    theta = summed.astype(jnp.float32) * (-two_pi / (4 * grid_size))
    return (jnp.cos(theta), jnp.sin(theta))

def swap_parts(values):
    half_width = values.shape[-1] // 2
    return jnp.concatenate([values[..., half_width:], -values[..., :half_width]], -1)

def apply_phase(values, phase_re, phase_im):
    half_width = values.shape[-1] // 2
    real_part = values[..., :half_width]
    imag_part = values[..., half_width:]
    return jnp.concatenate([real_part * phase_re - imag_part * phase_im, real_part * phase_im + imag_part * phase_re], -1)

def reference(forward, backward, targets):

    def add_mode(running, fields):
        forward32 = fields[0].astype(jnp.float32)
        backward32 = fields[1].astype(jnp.float32)
        fore_re = forward32[:, :GRID]
        fore_im = forward32[:, GRID:]
        back_re = backward32[:, :GRID]
        back_im = backward32[:, GRID:]
        term = jnp.concatenate([back_re * fore_re + back_im * fore_im, back_re * fore_im - back_im * fore_re], -1)
        return (running + term, None)
    intersection, ignored = lax.scan(add_mode, jnp.zeros((GRID, 2 * GRID), jnp.float32), (forward, backward))
    over_re = intersection[:, :GRID]
    over_im = intersection[:, GRID:]
    scale = lax.rsqrt(over_re * over_re + over_im * over_im + MODES)
    phase_plane = jnp.concatenate([over_re * scale, over_im * scale], -1).astype(jnp.bfloat16)
    index_all = jnp.arange(GRID, dtype=jnp.int32)
    cosine, sine_part = fourier_pair(index_all, index_all, GRID)
    cos_full = cosine.astype(jnp.bfloat16)
    sin_full = sine_part.astype(jnp.bfloat16)
    neg_full = (-sine_part).astype(jnp.bfloat16)
    forward_cols, inverse_cols = column_matrices(GRID)
    phase_re, phase_im = spectral_phase(index_all, index_all, GRID)
    plane32 = phase_plane.astype(jnp.float32)
    plane_re = plane32[:, :GRID]
    plane_im = plane32[:, GRID:]

    def along_rows(values, table_sin):
        return jnp.dot(cos_full, values, preferred_element_type=jnp.float32) + jnp.dot(table_sin, swap_parts(values), preferred_element_type=jnp.float32)

    def propagate(field):
        shaped = apply_phase(field.astype(jnp.float32), plane_re, plane_im).astype(jnp.bfloat16)
        across = jnp.dot(shaped, forward_cols, preferred_element_type=jnp.float32).astype(jnp.bfloat16)
        spectrum = apply_phase(along_rows(across, sin_full), phase_re, phase_im).astype(jnp.bfloat16)
        returned = along_rows(spectrum, neg_full).astype(jnp.bfloat16)
        return jnp.dot(returned, inverse_cols, preferred_element_type=jnp.float32).astype(jnp.bfloat16)
    output_fields = lax.map(propagate, forward)
    split_fields = output_fields.reshape(MODES, GRID, 2, GRID)
    out_re = split_fields[:, :, 0, :].reshape(MODES, GRID * GRID)
    out_im = split_fields[:, :, 1, :].reshape(MODES, GRID * GRID)
    target_re = targets[0].reshape(MODES, GRID * GRID)
    target_im = targets[1].reshape(MODES, GRID * GRID)
    real_part = jnp.dot(out_re, target_re.T, preferred_element_type=jnp.float32) + jnp.dot(out_im, target_im.T, preferred_element_type=jnp.float32)
    imag_part = jnp.dot(out_im, target_re.T, preferred_element_type=jnp.float32) - jnp.dot(out_re, target_im.T, preferred_element_type=jnp.float32)
    coupling = jnp.concatenate([real_part, imag_part], 0)
    return (phase_plane, output_fields, coupling)
```

```python
import numpy as np

import jax
import jax.numpy as jnp
from jax import lax
from jax.experimental import pallas as pl
from jax.experimental.pallas import tpu as pltpu
from jax.sharding import PartitionSpec as P

bf16 = jnp.bfloat16
f32 = jnp.float32


def propagator(grid_size):
    index = np.arange(grid_size)
    centred = (index + grid_size // 2) % grid_size - grid_size // 2
    squared = centred * centred % (4 * grid_size)
    column = np.fft.ifft(np.exp(-2j * np.pi * squared / (4 * grid_size)))
    matrix = column[(index[:, None] - index[None, :]) % grid_size]
    return matrix.real, matrix.imag


def stages(count):
    digits, stride = [], 1
    while count // stride > 4:
        digits.append((stride, 2))
        stride *= 2
    digits.append((stride, count // stride))
    return digits


def exchange(values, offset, count):
    return lax.ppermute(values, "modes", [(i, i ^ offset) for i in range(count)])


def pick(values, index, axis):
    return lax.dynamic_index_in_dim(values, index, axis, keepdims=False)


def reduce_part(partial, digits, order, count):
    me = lax.axis_index("modes")
    axes = [len(digits) - 1 - d for d in range(len(digits))]
    for d in order:
        stride, size = digits[d]
        own = me // stride % size
        axis = axes[d]
        got = [
            exchange(pick(partial, own ^ e, axis).astype(bf16), e * stride, count)
            for e in range(1, size)
        ]
        partial = pick(partial, own, axis)
        for g in got:
            partial = partial + g.astype(f32)
        axes = [a - (a > axis) for a in axes]
    return partial


def gather_part(block, digits, order, count):
    me = lax.axis_index("modes")
    done = []
    for d in reversed(order):
        stride, size = digits[d]
        own = me // stride % size
        got = [block] + [exchange(block, e * stride, count) for e in range(1, size)]
        axis = sum(1 for other in done if other > d)
        stacked = jnp.stack(got, axis)
        if size == 2:
            block = jnp.where(own == 0, stacked, jnp.flip(stacked, axis))
        else:
            block = jnp.stack([pick(stacked, own ^ at, axis) for at in range(size)], axis)
        done.append(d)
    return block


def columns_kernel(own_ref, other_ref, re_ref, im_ref, out_ref):
    half = own_ref.shape[1] // 2
    rows = own_ref.shape[0]

    def times(table, values):
        return jnp.dot(table, values, preferred_element_type=f32)

    def both(table, part):
        cols = pl.ds(part * half, half)
        return times(table[:, :rows], own_ref[:, cols]) + times(table[:, rows:], other_ref[:, cols])

    c_re, c_im = re_ref[...], im_ref[...]
    out_ref[:, :half] = (both(c_re, 0) - both(c_im, 1)).astype(bf16)
    out_ref[:, half:] = (both(c_im, 0) + both(c_re, 1)).astype(bf16)


def coupling_kernel(mode_rows, fields_ref, targets_ref, out_ref):
    product = lax.dot_general(
        fields_ref[...], targets_ref[...], (((1,), (1,)), ((), ())), preferred_element_type=f32
    )
    left, right = product.shape
    row = lax.broadcasted_iota(jnp.int32, (left, right), 0) % mode_rows
    col = lax.broadcasted_iota(jnp.int32, (left, right), 1) % mode_rows
    product = jnp.where(row == col, product, 0.0)

    def groups(size):
        member = lax.broadcasted_iota(jnp.int32, (size // mode_rows, size), 1) // mode_rows
        group = lax.broadcasted_iota(jnp.int32, (size // mode_rows, size), 0)
        return jnp.where(member == group, 1.0, 0.0).astype(f32)

    narrow = lax.dot_general(
        groups(left),
        product,
        (((1,), (0,)), ((), ())),
        precision=lax.Precision.HIGHEST,
        preferred_element_type=f32,
    )
    out_ref[...] = lax.dot_general(
        narrow,
        groups(right),
        (((1,), (1,)), ((), ())),
        precision=lax.Precision.HIGHEST,
        preferred_element_type=f32,
    )


def kernel_call(kernel, shape, dtype, flops, operands):
    return pl.pallas_call(
        kernel,
        out_shape=jax.ShapeDtypeStruct(shape, dtype),
        in_specs=[pl.BlockSpec(memory_space=pltpu.VMEM)] * len(operands),
        out_specs=pl.BlockSpec(memory_space=pltpu.VMEM),
        compiler_params=pltpu.CompilerParams(vmem_limit_bytes=32 * 1024 * 1024),
        cost_estimate=pl.CostEstimate(flops=flops, bytes_accessed=4 << 20, transcendentals=0),
    )(*operands)


def local(forward, backward, targets):
    modes_here, local_rows, double_width = forward.shape
    grid_size = double_width // 2
    count = lax.axis_size("modes")
    mode_total = modes_here * count
    block_rows = local_rows // count
    digits = stages(count)
    sizes = [size for _, size in reversed(digits)]
    half = grid_size // 2

    fore = forward[0].astype(f32)
    back = backward[0].astype(f32)
    fore_re, fore_im = fore[:, :grid_size], fore[:, grid_size:]
    back_re, back_im = back[:, :grid_size], back[:, grid_size:]
    partial_re = back_re * fore_re + back_im * fore_im
    partial_im = back_re * fore_im - back_im * fore_re
    first = list(range(len(digits)))
    orders = [first, [1, 0] + first[2:]]
    planes = []
    for part, order in enumerate(orders):
        cols = slice(part * half, (part + 1) * half)
        partial = jnp.concatenate([partial_re[:, cols], partial_im[:, cols]], -1)
        summed = reduce_part(partial.reshape(*sizes, block_rows, grid_size), digits, order, count)
        over_re, over_im = summed[:, :half], summed[:, half:]
        scale = lax.rsqrt(over_re * over_re + over_im * over_im + mode_total)
        block = jnp.concatenate([over_re * scale, over_im * scale], -1).astype(bf16)
        planes.append(gather_part(block, digits, order, count).reshape(local_rows, grid_size))
    plane_re = jnp.concatenate([p[:, :half] for p in planes], -1)
    plane_im = jnp.concatenate([p[:, half:] for p in planes], -1)
    phase_plane = jnp.concatenate([plane_re, plane_im], -1)

    plane_re, plane_im = plane_re.astype(f32), plane_im.astype(f32)
    shaped = jnp.concatenate(
        [fore_re * plane_re - fore_im * plane_im, fore_re * plane_im + fore_im * plane_re], -1
    ).astype(bf16)
    other = lax.ppermute(shaped, "rows", [(0, 1), (1, 0)])

    c_re, c_im = propagator(grid_size)
    own_re = jnp.asarray(c_re[:local_rows], bf16)
    own_im = jnp.asarray(c_im[:local_rows], bf16)
    columns = kernel_call(
        columns_kernel,
        (local_rows, double_width),
        bf16,
        2 * local_rows * double_width * double_width,
        (shaped, other, own_re, own_im),
    )

    back_table = jnp.asarray(np.block([[c_re, -c_im], [c_im, c_re]]), bf16)
    rows_table = jnp.asarray(np.block([[c_re, c_im], [-c_im, c_re]]), bf16)
    flat = jnp.concatenate([targets[0], targets[1]], -1).reshape(-1, double_width)
    seen = jnp.dot(flat, back_table, preferred_element_type=f32).astype(bf16)
    turned = jnp.concatenate([-seen[:, grid_size:], seen[:, :grid_size]], -1)
    target_pair = jnp.concatenate([seen, turned], 0)

    pixels = lax.all_to_all(
        columns.reshape(count, block_rows, double_width), "modes", 0, 0, tiled=True
    )
    output_fields = jnp.dot(columns, rows_table, preferred_element_type=f32).astype(bf16)

    term = kernel_call(
        lambda *refs: coupling_kernel(block_rows, *refs),
        (mode_total, 2 * mode_total),
        f32,
        4 * local_rows * local_rows * double_width,
        (pixels.reshape(local_rows, double_width), target_pair),
    )
    term = jnp.concatenate([term[:, :mode_total], term[:, mode_total:]], 0)
    pieces = lax.all_to_all(term, ("modes", "rows"), 0, 0, tiled=True)
    coupling = jnp.sum(pieces, 0, keepdims=True)
    return (phase_plane, output_fields[None], coupling)


def solution(mesh):
    return jax.shard_map(
        local,
        mesh=mesh,
        in_specs=(
            P("modes", "rows", None),
            P("modes", "rows", None),
            P(None, None, ("rows", "modes"), None),
        ),
        out_specs=(P("rows", None), P("modes", "rows", None), P(("modes", "rows"), None)),
        check_vma=False,
    )
```

```python
import numpy as np

import jax
import jax.numpy as jnp
from jax import lax
from jax.experimental import pallas as pl
from jax.experimental.pallas import tpu as pltpu
from jax.sharding import PartitionSpec as P

bf16 = jnp.bfloat16
f32 = jnp.float32


def propagator(grid_size):
    index = np.arange(grid_size)
    centred = (index + grid_size // 2) % grid_size - grid_size // 2
    squared = centred * centred % (4 * grid_size)
    column = np.fft.ifft(np.exp(-2j * np.pi * squared / (4 * grid_size)))
    matrix = column[(index[:, None] - index[None, :]) % grid_size]
    return matrix.real, matrix.imag


def stages(count):
    digits, stride = [], 1
    while count // stride > 4:
        digits.append((stride, 2))
        stride *= 2
    digits.append((stride, count // stride))
    return digits


def exchange(values, offset, count):
    return lax.ppermute(values, "modes", [(i, i ^ offset) for i in range(count)])


def pick(values, index, axis):
    return lax.dynamic_index_in_dim(values, index, axis, keepdims=False)


def reduce_digit(keep, got):
    for g in got:
        keep = keep + g.astype(f32)
    return keep


def gather_digit(block, own, stride, size, axis, count):
    got = [block] + [exchange(block, e * stride, count) for e in range(1, size)]
    stacked = jnp.stack(got, axis)
    if size == 2:
        return jnp.where(own == 0, stacked, jnp.flip(stacked, axis))
    return jnp.stack([pick(stacked, own ^ at, axis) for at in range(size)], axis)


def split_digit(partial, own, size, axis):
    send = [pick(partial, own ^ e, axis).astype(bf16) for e in range(1, size)]
    return send, pick(partial, own, axis)


def product_of(fore, back):
    half = fore.shape[-1] // 2
    fore, back = fore.astype(f32), back.astype(f32)
    fore_re, fore_im = fore[..., :half], fore[..., half:]
    back_re, back_im = back[..., :half], back[..., half:]
    return back_re * fore_re + back_im * fore_im, back_re * fore_im - back_im * fore_re


def products_kernel(rows, fore_ref, back_ref, send_a, keep_a, send_b, keep_b):
    me = lax.axis_index("modes")
    low, high = me % 2 == 1, me // 2 % 2 == 1
    grid_size = fore_ref.shape[1] // 2
    half = grid_size // 2
    pair = 2 * rows
    for group in range(fore_ref.shape[0] // (4 * rows)):
        at = pl.ds(group * 4 * rows, 4 * rows)
        out = pl.ds(group * pair, pair)
        for part in range(2):
            cols = [pl.ds(part * half, half), pl.ds(grid_size + part * half, half)]
            fore_re, fore_im = [fore_ref[at, c].astype(f32) for c in cols]
            back_re, back_im = [back_ref[at, c].astype(f32) for c in cols]
            values = (back_re * fore_re + back_im * fore_im, back_re * fore_im - back_im * fore_re)
            for k, v in enumerate(values):
                into = pl.ds(k * half, half)
                if part == 0:
                    first = jnp.concatenate([v[:rows], v[pair : pair + rows]], 0)
                    second = jnp.concatenate([v[rows:pair], v[pair + rows :]], 0)
                    send_a[out, into] = jnp.where(low, first, second).astype(bf16)
                    keep_a[out, into] = jnp.where(low, second, first)
                else:
                    first, second = v[:pair], v[pair:]
                    send_b[out, into] = jnp.where(high, first, second).astype(bf16)
                    keep_b[out, into] = jnp.where(high, second, first)


def columns_kernel(own_ref, other_ref, re_ref, im_ref, out_ref):
    half = own_ref.shape[1] // 2
    rows = own_ref.shape[0]

    def times(table, values):
        return jnp.dot(table, values, preferred_element_type=f32)

    def both(table, part):
        cols = pl.ds(part * half, half)
        return times(table[:, :rows], own_ref[:, cols]) + times(table[:, rows:], other_ref[:, cols])

    c_re, c_im = re_ref[...], im_ref[...]
    out_ref[:, :half] = (both(c_re, 0) - both(c_im, 1)).astype(bf16)
    out_ref[:, half:] = (both(c_im, 0) + both(c_re, 1)).astype(bf16)


def coupling_kernel(mode_rows, fields_ref, targets_ref, out_ref):
    product = lax.dot_general(
        fields_ref[...], targets_ref[...], (((1,), (1,)), ((), ())), preferred_element_type=f32
    )
    left, right = product.shape
    row = lax.broadcasted_iota(jnp.int32, (left, right), 0) % mode_rows
    col = lax.broadcasted_iota(jnp.int32, (left, right), 1) % mode_rows
    product = jnp.where(row == col, product, 0.0)

    def groups(size):
        member = lax.broadcasted_iota(jnp.int32, (size // mode_rows, size), 1) // mode_rows
        group = lax.broadcasted_iota(jnp.int32, (size // mode_rows, size), 0)
        return jnp.where(member == group, 1.0, 0.0).astype(f32)

    narrow = lax.dot_general(
        groups(left),
        product,
        (((1,), (0,)), ((), ())),
        precision=lax.Precision.HIGHEST,
        preferred_element_type=f32,
    )
    out_ref[...] = lax.dot_general(
        narrow,
        groups(right),
        (((1,), (1,)), ((), ())),
        precision=lax.Precision.HIGHEST,
        preferred_element_type=f32,
    )


def kernel_call(kernel, shape, dtype, flops, operands):
    place = pl.BlockSpec(memory_space=pltpu.VMEM)
    several = isinstance(dtype, list)
    if several:
        out_shape = [jax.ShapeDtypeStruct(s, d) for s, d in zip(shape, dtype)]
    else:
        out_shape = jax.ShapeDtypeStruct(shape, dtype)
    return pl.pallas_call(
        kernel,
        out_shape=out_shape,
        in_specs=[place] * len(operands),
        out_specs=[place] * len(shape) if several else place,
        compiler_params=pltpu.CompilerParams(vmem_limit_bytes=32 * 1024 * 1024),
        cost_estimate=pl.CostEstimate(flops=flops, bytes_accessed=4 << 20, transcendentals=0),
    )(*operands)


def local(forward, backward, targets):
    modes_here, local_rows, double_width = forward.shape
    grid_size = double_width // 2
    count = lax.axis_size("modes")
    mode_total = modes_here * count
    block_rows = local_rows // count
    digits = stages(count)
    sizes = [size for _, size in reversed(digits)]
    half = grid_size // 2

    me = lax.axis_index("modes")
    owns = [me // stride % size for stride, size in digits]
    last = len(digits) - 1
    first = list(range(last))
    orders = [first, [1, 0] + first[2:]]
    kernel_first = block_rows % 8 == 0 and local_rows % (4 * block_rows) == 0
    if kernel_first:
        halves = kernel_call(
            lambda *refs: products_kernel(block_rows, *refs),
            [(local_rows // 2, grid_size)] * 4,
            [bf16, f32, bf16, f32],
            8 * local_rows * double_width,
            (forward[0], backward[0]),
        )
    else:
        product = product_of(forward[0], backward[0])
    kept = []
    for part, order in enumerate(orders):
        cols = slice(part * half, (part + 1) * half)
        axes = [last - d for d in range(len(digits))]
        if not kernel_first:
            partial = jnp.concatenate([p[:, cols] for p in product], -1)
            partial = partial.reshape(*sizes, block_rows, grid_size)
        for at, d in enumerate(order):
            stride, size = digits[d]
            left = sizes[: axes[d]] + sizes[axes[d] + 1 :] if at == 0 else None
            if at == 0 and kernel_first:
                send = [halves[2 * part].reshape(*left, block_rows, grid_size)]
                keep = halves[2 * part + 1].reshape(*left, block_rows, grid_size)
            else:
                send, keep = split_digit(partial, owns[d], size, axes[d])
            got = [exchange(v, (e + 1) * stride, count) for e, v in enumerate(send)]
            partial = reduce_digit(keep, got)
            axes = [a - (a > axes[d]) for a in axes]
        kept.append(partial)
    stride, size = digits[last]
    send, keep = split_digit(jnp.concatenate(kept, -1), owns[last], size, 0)
    got = [exchange(v, (e + 1) * stride, count) for e, v in enumerate(send)]
    summed = reduce_digit(keep, got).reshape(block_rows, 2, 2, half)
    over_re, over_im = summed[:, :, 0], summed[:, :, 1]
    scale = lax.rsqrt(over_re * over_re + over_im * over_im + mode_total)
    block = jnp.stack([over_re * scale, over_im * scale], 2).astype(bf16)
    block = block.reshape(block_rows, double_width)

    block = gather_digit(block, owns[last], stride, size, 0, count)
    planes = []
    for part, order in enumerate(orders):
        piece = block[..., part * grid_size : (part + 1) * grid_size]
        done = [last]
        for d in reversed(order):
            axis = sum(1 for other in done if other > d)
            piece = gather_digit(piece, owns[d], *digits[d], axis, count)
            done.append(d)
        planes.append(piece.reshape(local_rows, grid_size))
    plane_re = jnp.concatenate([p[:, :half] for p in planes], -1)
    plane_im = jnp.concatenate([p[:, half:] for p in planes], -1)
    phase_plane = jnp.concatenate([plane_re, plane_im], -1)

    fore = forward[0].astype(f32)
    fore_re, fore_im = fore[:, :grid_size], fore[:, grid_size:]
    plane_re, plane_im = plane_re.astype(f32), plane_im.astype(f32)
    shaped = jnp.concatenate(
        [fore_re * plane_re - fore_im * plane_im, fore_re * plane_im + fore_im * plane_re], -1
    ).astype(bf16)
    other = lax.ppermute(shaped, "rows", [(0, 1), (1, 0)])

    c_re, c_im = propagator(grid_size)
    own_re = jnp.asarray(c_re[:local_rows], bf16)
    own_im = jnp.asarray(c_im[:local_rows], bf16)
    columns = kernel_call(
        columns_kernel,
        (local_rows, double_width),
        bf16,
        2 * local_rows * double_width * double_width,
        (shaped, other, own_re, own_im),
    )

    back_table = jnp.asarray(np.block([[c_re, -c_im], [c_im, c_re]]), bf16)
    rows_table = jnp.asarray(np.block([[c_re, c_im], [-c_im, c_re]]), bf16)
    flat = jnp.concatenate([targets[0], targets[1]], -1).reshape(-1, double_width)
    seen = jnp.dot(flat, back_table, preferred_element_type=f32).astype(bf16)
    turned = jnp.concatenate([-seen[:, grid_size:], seen[:, :grid_size]], -1)
    target_pair = jnp.concatenate([seen, turned], 0)

    pixels = lax.all_to_all(
        columns.reshape(count, block_rows, double_width), "modes", 0, 0, tiled=True
    )
    output_fields = jnp.dot(columns, rows_table, preferred_element_type=f32).astype(bf16)
    pixels, output_fields = lax.optimization_barrier((pixels, output_fields))

    term = kernel_call(
        lambda *refs: coupling_kernel(block_rows, *refs),
        (mode_total, 2 * mode_total),
        f32,
        4 * local_rows * local_rows * double_width,
        (pixels.reshape(local_rows, double_width), target_pair),
    )
    term = jnp.concatenate([term[:, :mode_total], term[:, mode_total:]], 0)
    pieces = lax.all_to_all(term, ("modes", "rows"), 0, 0, tiled=True)
    coupling = jnp.sum(pieces, 0, keepdims=True)
    return (phase_plane, output_fields[None], coupling)


def solution(mesh):
    return jax.shard_map(
        local,
        mesh=mesh,
        in_specs=(
            P("modes", "rows", None),
            P("modes", "rows", None),
            P(None, None, ("rows", "modes"), None),
        ),
        out_specs=(P("rows", None), P("modes", "rows", None), P(("modes", "rows"), None)),
        check_vma=False,
    )
```

```python
import numpy as np

import jax
import jax.numpy as jnp
from jax import lax
from jax.experimental import pallas as pl
from jax.experimental.pallas import tpu as pltpu
from jax.sharding import PartitionSpec as P

bf16 = jnp.bfloat16
f32 = jnp.float32


def propagator(grid_size):
    index = np.arange(grid_size)
    centred = (index + grid_size // 2) % grid_size - grid_size // 2
    squared = centred * centred % (4 * grid_size)
    column = np.fft.ifft(np.exp(-2j * np.pi * squared / (4 * grid_size)))
    matrix = column[(index[:, None] - index[None, :]) % grid_size]
    return matrix.real, matrix.imag


def stages(count):
    digits, stride = [], 1
    while count // stride > 4:
        digits.append((stride, 2))
        stride *= 2
    digits.append((stride, count // stride))
    return digits


def exchange(values, offset, count):
    return lax.ppermute(values, "modes", [(i, i ^ offset) for i in range(count)])


def pick(values, index, axis):
    return lax.dynamic_index_in_dim(values, index, axis, keepdims=False)


def reduce_digit(keep, got):
    for g in got:
        keep = keep + g.astype(f32)
    return keep


def gather_digit(block, own, stride, size, axis, count):
    got = [block] + [exchange(block, e * stride, count) for e in range(1, size)]
    stacked = jnp.stack(got, axis)
    if size == 2:
        return jnp.where(own == 0, stacked, jnp.flip(stacked, axis))
    return jnp.stack([pick(stacked, own ^ at, axis) for at in range(size)], axis)


def split_digit(partial, own, size, axis):
    send = [pick(partial, own ^ e, axis).astype(bf16) for e in range(1, size)]
    return send, pick(partial, own, axis)


def product_of(fore, back):
    half = fore.shape[-1] // 2
    fore, back = fore.astype(f32), back.astype(f32)
    fore_re, fore_im = fore[..., :half], fore[..., half:]
    back_re, back_im = back[..., :half], back[..., half:]
    return back_re * fore_re + back_im * fore_im, back_re * fore_im - back_im * fore_re


def products_kernel(rows, fore_ref, back_ref, send_a, keep_a, send_b, keep_b):
    me = lax.axis_index("modes")
    low, high = me % 2 == 1, me // 2 % 2 == 1
    grid_size = fore_ref.shape[1] // 2
    half = grid_size // 2
    pair = 2 * rows
    for group in range(fore_ref.shape[0] // (4 * rows)):
        at = pl.ds(group * 4 * rows, 4 * rows)
        out = pl.ds(group * pair, pair)
        for part in range(2):
            cols = [pl.ds(part * half, half), pl.ds(grid_size + part * half, half)]
            fore_re, fore_im = [fore_ref[at, c].astype(f32) for c in cols]
            back_re, back_im = [back_ref[at, c].astype(f32) for c in cols]
            values = (back_re * fore_re + back_im * fore_im, back_re * fore_im - back_im * fore_re)
            for k, v in enumerate(values):
                into = pl.ds(k * half, half)
                if part == 0:
                    first = jnp.concatenate([v[:rows], v[pair : pair + rows]], 0)
                    second = jnp.concatenate([v[rows:pair], v[pair + rows :]], 0)
                    send_a[out, into] = jnp.where(low, first, second).astype(bf16)
                    keep_a[out, into] = jnp.where(low, second, first)
                else:
                    first, second = v[:pair], v[pair:]
                    send_b[out, into] = jnp.where(high, first, second).astype(bf16)
                    keep_b[out, into] = jnp.where(high, second, first)


def coupling_kernel(mode_rows, starts, fields_ref, *rest):
    targets, out_ref = rest[:-1], rest[-1]
    sources, _, pixel_rows, grid_size = fields_ref.shape
    count = lax.axis_size("modes")
    half = lax.axis_index("modes") // (count // 2)
    left = sources * pixel_rows
    field_re = fields_ref[:, 0].reshape(left, grid_size)
    field_im = fields_ref[:, 1].reshape(left, grid_size)
    contract = (((1,), (1,)), ((), ()))

    def groups(size, each):
        member = lax.broadcasted_iota(jnp.int32, (size // each, size), 1) // each
        group = lax.broadcasted_iota(jnp.int32, (size // each, size), 0)
        return jnp.where(member == group, 1.0, 0.0).astype(f32)

    def times(one, two):
        return lax.dot_general(one, two, contract, preferred_element_type=f32)

    def exactly(one, two, dims):
        return lax.dot_general(one, two, (dims, ((), ())), precision=lax.Precision.HIGHEST, preferred_element_type=f32)

    modes = out_ref.shape[1] // 2
    total_re = total_im = jnp.zeros((sources, modes), f32)
    for which, (start, target) in enumerate(zip(starts, targets)):
        right = target.shape[0]
        each = right // modes
        in_half = half if which == 0 else 1 - half
        target_re, target_im = target[:, :grid_size], target[:, grid_size:]
        row = lax.broadcasted_iota(jnp.int32, (left, right), 0) % pixel_rows
        col = lax.broadcasted_iota(jnp.int32, (left, right), 1) % each
        same = row == col + (in_half * mode_rows + start)
        real = jnp.where(same, times(field_re, target_re) + times(field_im, target_im), 0.0)
        imag = jnp.where(same, times(field_im, target_re) - times(field_re, target_im), 0.0)
        rows_of, cols_of = groups(left, pixel_rows), groups(right, each)
        total_re += exactly(exactly(rows_of, real, ((1,), (0,))), cols_of, ((1,), (1,)))
        total_im += exactly(exactly(rows_of, imag, ((1,), (0,))), cols_of, ((1,), (1,)))
    out_ref[:, :modes] = total_re
    out_ref[:, modes:] = total_im


def kernel_call(kernel, shape, dtype, flops, operands):
    place = pl.BlockSpec(memory_space=pltpu.VMEM)
    several = isinstance(dtype, list)
    if several:
        out_shape = [jax.ShapeDtypeStruct(s, d) for s, d in zip(shape, dtype)]
    else:
        out_shape = jax.ShapeDtypeStruct(shape, dtype)
    return pl.pallas_call(
        kernel,
        out_shape=out_shape,
        in_specs=[place] * len(operands),
        out_specs=[place] * len(shape) if several else place,
        compiler_params=pltpu.CompilerParams(vmem_limit_bytes=32 * 1024 * 1024),
        cost_estimate=pl.CostEstimate(flops=flops, bytes_accessed=4 << 20, transcendentals=0),
    )(*operands)


def local(forward, backward, targets):
    modes_here, local_rows, double_width = forward.shape
    grid_size = double_width // 2
    count = lax.axis_size("modes")
    mode_total = modes_here * count
    block_rows = local_rows // count
    digits = stages(count)
    sizes = [size for _, size in reversed(digits)]
    half = grid_size // 2

    c_re, c_im = propagator(grid_size)
    back_table = jnp.asarray(np.block([[c_re, -c_im], [c_im, c_re]]), bf16)

    def back(part):
        flat = jnp.concatenate([part[0], part[1]], -1).reshape(-1, double_width)
        return jnp.dot(flat, back_table, preferred_element_type=f32).astype(bf16)

    cut = block_rows // 3
    early = exchange(targets[:, :, :cut], count // 2, count)
    seen = back(targets)

    me = lax.axis_index("modes")
    owns = [me // stride % size for stride, size in digits]
    last = len(digits) - 1
    first = list(range(last))
    orders = [first, [1, 0] + first[2:]]
    kernel_first = block_rows % 8 == 0 and local_rows % (4 * block_rows) == 0
    if kernel_first:
        halves = kernel_call(
            lambda *refs: products_kernel(block_rows, *refs),
            [(local_rows // 2, grid_size)] * 4,
            [bf16, f32, bf16, f32],
            8 * local_rows * double_width,
            (forward[0], backward[0]),
        )
    else:
        product = product_of(forward[0], backward[0])
    kept = []
    for part, order in enumerate(orders):
        cols = slice(part * half, (part + 1) * half)
        axes = [last - d for d in range(len(digits))]
        if not kernel_first:
            partial = jnp.concatenate([p[:, cols] for p in product], -1)
            partial = partial.reshape(*sizes, block_rows, grid_size)
        for at, d in enumerate(order):
            stride, size = digits[d]
            left = sizes[: axes[d]] + sizes[axes[d] + 1 :] if at == 0 else None
            if at == 0 and kernel_first:
                send = [halves[2 * part].reshape(*left, block_rows, grid_size)]
                keep = halves[2 * part + 1].reshape(*left, block_rows, grid_size)
            else:
                send, keep = split_digit(partial, owns[d], size, axes[d])
            got = [exchange(v, (e + 1) * stride, count) for e, v in enumerate(send)]
            if at == 0 and part == 0:
                got, seen = lax.optimization_barrier((got, seen))
            partial = reduce_digit(keep, got)
            axes = [a - (a > axes[d]) for a in axes]
        kept.append(partial)
    stride, size = digits[last]
    send, keep = split_digit(jnp.concatenate(kept, -1), owns[last], size, 0)
    got = [exchange(v, (e + 1) * stride, count) for e, v in enumerate(send)]
    summed = reduce_digit(keep, got).reshape(block_rows, 2, 2, half)
    over_re, over_im = summed[:, :, 0], summed[:, :, 1]
    scale = lax.rsqrt(over_re * over_re + over_im * over_im + mode_total)
    block = jnp.stack([over_re * scale, over_im * scale], 2).astype(bf16)
    block = block.reshape(block_rows, double_width)

    block = gather_digit(block, owns[last], stride, size, 0, count)
    block, later = lax.optimization_barrier((block, targets[:, :, cut:]))
    later = exchange(later, count // 2, count)
    planes = []
    for part, order in enumerate(orders):
        piece = block[..., part * grid_size : (part + 1) * grid_size]
        done = [last]
        for d in reversed(order):
            axis = sum(1 for other in done if other > d)
            piece = gather_digit(piece, owns[d], *digits[d], axis, count)
            done.append(d)
        planes.append(piece.reshape(local_rows, grid_size))
    plane_re = jnp.concatenate([p[:, :half] for p in planes], -1)
    plane_im = jnp.concatenate([p[:, half:] for p in planes], -1)
    phase_plane = jnp.concatenate([plane_re, plane_im], -1)

    fore = forward[0].astype(f32)
    fore_re, fore_im = fore[:, :grid_size], fore[:, grid_size:]
    plane_re, plane_im = plane_re.astype(f32), plane_im.astype(f32)
    shaped = jnp.concatenate(
        [fore_re * plane_re - fore_im * plane_im, fore_re * plane_im + fore_im * plane_re], 0
    ).astype(bf16)
    other = lax.ppermute(shaped, "rows", [(0, 1), (1, 0)])

    order = np.arange(local_rows).reshape(2, count // 2, block_rows).transpose(1, 0, 2).reshape(count // 2, -1)

    def table(cols):
        real, imag = c_re[:local_rows, cols], c_im[:local_rows, cols]
        rows = np.stack([np.concatenate([real, -imag], 1)[order], np.concatenate([imag, real], 1)[order]], 1)
        return jnp.asarray(rows.reshape(2 * local_rows, -1), bf16)

    columns = jnp.dot(table(slice(0, local_rows)), shaped, preferred_element_type=f32)
    columns, other = lax.optimization_barrier((columns, other))
    columns = columns + jnp.dot(table(slice(local_rows, None)), other, preferred_element_type=f32)
    columns = columns.astype(bf16).reshape(count // 2, 2, 2 * block_rows, grid_size)

    together = [list(range(count // 2)), list(range(count // 2, count))]
    pixels = lax.all_to_all(columns, "modes", 0, 0, tiled=True, axis_index_groups=together)

    columns = columns.reshape(count // 2, 2, 2, block_rows, grid_size)
    columns = columns.transpose(2, 0, 3, 1, 4).reshape(local_rows, double_width)
    rows_table = jnp.asarray(np.block([[c_re, c_im], [-c_im, c_re]]), bf16)
    output_fields = jnp.dot(columns, rows_table, preferred_element_type=f32).astype(bf16)
    pixels, output_fields = lax.optimization_barrier((pixels, output_fields))

    term = kernel_call(
        lambda *refs: coupling_kernel(block_rows, (0, 0, cut), *refs),
        (mode_total // 2, 2 * mode_total),
        f32,
        8 * local_rows * local_rows * double_width,
        (pixels, seen, back(early), back(later)),
    )
    term = term.reshape(mode_total // 2, 2, 1, mode_total).transpose(1, 2, 0, 3)
    in_half = (jnp.arange(2) == me // (count // 2)).reshape(1, 2, 1, 1)
    term = jnp.where(in_half, term, 0.0).reshape(2 * mode_total, mode_total)
    pieces = lax.all_to_all(term, ("modes", "rows"), 0, 0, tiled=True)
    coupling = jnp.sum(pieces, 0, keepdims=True)
    return (phase_plane, output_fields[None], coupling)


def solution(mesh):
    return jax.shard_map(
        local,
        mesh=mesh,
        in_specs=(
            P("modes", "rows", None),
            P("modes", "rows", None),
            P(None, None, ("rows", "modes"), None),
        ),
        out_specs=(P("rows", None), P("modes", "rows", None), P(("modes", "rows"), None)),
        check_vma=False,
    )
```

```python
import numpy as np

import jax
import jax.numpy as jnp
from jax import lax
from jax.experimental import pallas as pl
from jax.experimental.pallas import tpu as pltpu
from jax.sharding import PartitionSpec as P

bf16 = jnp.bfloat16
f32 = jnp.float32


def propagator(grid_size):
    index = np.arange(grid_size)
    centred = (index + grid_size // 2) % grid_size - grid_size // 2
    squared = centred * centred % (4 * grid_size)
    column = np.fft.ifft(np.exp(-2j * np.pi * squared / (4 * grid_size)))
    matrix = column[(index[:, None] - index[None, :]) % grid_size]
    return matrix.real, matrix.imag


def stages(count):
    digits, stride = [], 1
    while count // stride > 4:
        digits.append((stride, 2))
        stride *= 2
    digits.append((stride, count // stride))
    return digits


def exchange(values, offset, count):
    return lax.ppermute(values, "modes", [(i, i ^ offset) for i in range(count)])


def pick(values, index, axis):
    return lax.dynamic_index_in_dim(values, index, axis, keepdims=False)


def reduce_digit(keep, got):
    for g in got:
        keep = keep + g.astype(f32)
    return keep


def gather_digit(block, own, stride, size, axis, count):
    got = [block] + [exchange(block, e * stride, count) for e in range(1, size)]
    stacked = jnp.stack(got, axis)
    if size == 2:
        return jnp.where(own == 0, stacked, jnp.flip(stacked, axis))
    return jnp.stack([pick(stacked, own ^ at, axis) for at in range(size)], axis)


def split_digit(partial, own, size, axis):
    send = [pick(partial, own ^ e, axis).astype(bf16) for e in range(1, size)]
    return send, pick(partial, own, axis)


def product_of(fore, back):
    half = fore.shape[-1] // 2
    fore, back = fore.astype(f32), back.astype(f32)
    fore_re, fore_im = fore[..., :half], fore[..., half:]
    back_re, back_im = back[..., :half], back[..., half:]
    return back_re * fore_re + back_im * fore_im, back_re * fore_im - back_im * fore_re


def products_kernel(rows, fore_ref, back_ref, send_a, keep_a, send_b, keep_b):
    me = lax.axis_index("modes")
    low, high = me % 2 == 1, me // 2 % 2 == 1
    grid_size = fore_ref.shape[1] // 2
    half = grid_size // 2
    pair = 2 * rows
    for part in range(2):
        cols = [pl.ds(part * half, half), pl.ds(grid_size + part * half, half)]
        fore_re, fore_im = [fore_ref[:, c].astype(f32) for c in cols]
        back_re, back_im = [back_ref[:, c].astype(f32) for c in cols]
        values = (back_re * fore_re + back_im * fore_im, back_re * fore_im - back_im * fore_re)
        for k, v in enumerate(values):
            into = pl.ds(k * half, half)
            if part == 0:
                first = jnp.concatenate([v[:rows], v[pair : pair + rows]], 0)
                second = jnp.concatenate([v[rows:pair], v[pair + rows :]], 0)
                send_a[:, into] = jnp.where(low, first, second).astype(bf16)
                keep_a[:, into] = jnp.where(low, second, first)
            else:
                first, second = v[:pair], v[pair:]
                send_b[:, into] = jnp.where(high, first, second).astype(bf16)
                keep_b[:, into] = jnp.where(high, second, first)


def halve_kernel(rows, stride, keep_ref, got_ref, send_ref, left_ref):
    upper = lax.axis_index("modes") // stride % 2 == 1
    pair = 2 * rows
    for group in range(keep_ref.shape[0] // (2 * pair)):
        at = pl.ds(group * 2 * pair, 2 * pair)
        v = keep_ref[at] + got_ref[at].astype(f32)
        first = jnp.concatenate([v[:rows], v[pair : pair + rows]], 0)
        second = jnp.concatenate([v[rows:pair], v[pair + rows :]], 0)
        into = pl.ds(group * pair, pair)
        send_ref[into] = jnp.where(upper, first, second).astype(bf16)
        left_ref[into] = jnp.where(upper, second, first)


def shape_kernel(plane_a, plane_b, fore_ref, plane_ref, shaped_ref):
    rows, grid_size = plane_a.shape
    half = grid_size // 2
    step = 48
    for at in range(0, rows, step):
        here = pl.ds(at, step)
        for part, ref in enumerate((plane_a, plane_b)):
            real, imag = ref[here, :half], ref[here, half:]
            left, right = pl.ds(part * half, half), pl.ds(grid_size + part * half, half)
            plane_ref[here, left] = real
            plane_ref[here, right] = imag
            real, imag = real.astype(f32), imag.astype(f32)
            fore_re, fore_im = fore_ref[here, left].astype(f32), fore_ref[here, right].astype(f32)
            shaped_ref[here, left] = (fore_re * real - fore_im * imag).astype(bf16)
            shaped_ref[pl.ds(rows + at, step), left] = (fore_re * imag + fore_im * real).astype(bf16)


def times(one, two):
    return jnp.dot(one, two, preferred_element_type=f32)


def own_kernel(table_ref, shaped_ref, out_ref):
    out_ref[...] = times(table_ref[...], shaped_ref[...])


def other_kernel(table_ref, shaped_ref, own_ref, out_ref):
    out_ref[...] = (own_ref[...] + times(table_ref[...], shaped_ref[...])).astype(bf16)


def fields_kernel(mode_rows, columns_ref, re_ref, im_ref, out_ref):
    owners, _, pixel_rows, grid_size = columns_ref.shape
    rows = owners * pixel_rows
    real = columns_ref[:, 0].reshape(rows, grid_size)
    imag = columns_ref[:, 1].reshape(rows, grid_size)
    c_re, c_im = re_ref[...], im_ref[...]
    for k, v in enumerate(
        (times(real, c_re) - times(imag, c_im), times(real, c_im) + times(imag, c_re))
    ):
        into = pl.ds(k * grid_size, grid_size)
        if mode_rows % 8 == 0:
            for half in range(2):
                for owner in range(0, owners, 2):
                    at = [o * pixel_rows + half * mode_rows for o in (owner, owner + 1)]
                    both = jnp.concatenate([v[a : a + mode_rows] for a in at], 0)
                    start = half * owners * mode_rows + owner * mode_rows
                    out_ref[pl.ds(start, 2 * mode_rows), into] = both.astype(bf16)
        else:
            out_ref[:, into] = v.astype(bf16)


def targets_kernel(re_ref, im_ref, *refs):
    grid_size = re_ref.shape[0]
    c_re, c_im = re_ref[...], im_ref[...]
    start = 0
    for ref in refs[:-1]:
        real, imag = ref[0], ref[1]
        rows = pl.ds(start, real.shape[0])
        refs[-1][rows, :grid_size] = (times(real, c_re) + times(imag, c_im)).astype(bf16)
        refs[-1][rows, grid_size:] = (times(imag, c_re) - times(real, c_im)).astype(bf16)
        start += real.shape[0]


def coupling_kernel(mode_rows, fields_ref, *rest):
    targets, out_ref = rest[:-1], rest[-1]
    sources, _, pixel_rows, grid_size = fields_ref.shape
    count = lax.axis_size("modes")
    half = lax.axis_index("modes") // (count // 2)
    left = sources * pixel_rows
    field_re = fields_ref[:, 0].reshape(left, grid_size)
    field_im = fields_ref[:, 1].reshape(left, grid_size)

    def against(one, two):
        return lax.dot_general(one, two, (((1,), (1,)), ((), ())), preferred_element_type=f32)

    modes = out_ref.shape[1] // 2
    totals = [jnp.zeros((sources, modes), f32)] * 2
    first = 0
    for which, target in enumerate(targets):
        right = target.shape[0]
        if which == 1:
            first = 0
        in_half = half if which == 0 else 1 - half
        target_re, target_im = target[:, :grid_size], target[:, grid_size:]
        row = lax.broadcasted_iota(jnp.int32, (left, right), 0) % pixel_rows
        col = lax.broadcasted_iota(jnp.int32, (left, right), 1) % mode_rows
        same = row == col + in_half * mode_rows
        member = lax.broadcasted_iota(jnp.int32, (modes, right), 1) // mode_rows + first
        group = lax.broadcasted_iota(jnp.int32, (modes, right), 0)
        groups = jnp.where(member == group, 1.0, 0.0).astype(f32)
        parts = (
            against(field_re, target_re) + against(field_im, target_im),
            against(field_im, target_re) - against(field_re, target_im),
        )
        for k, v in enumerate(parts):
            v = jnp.where(same, v, 0.0).reshape(sources, pixel_rows, right)
            totals[k] = totals[k] + lax.dot_general(
                jnp.sum(v, 1),
                groups,
                (((1,), (1,)), ((), ())),
                precision=lax.Precision.HIGHEST,
                preferred_element_type=f32,
            )
        first += right // mode_rows
    out_ref[:, :modes] = totals[0]
    out_ref[:, modes:] = totals[1]


def kernel_call(kernel, shape, dtype, flops, operands, grant=8, **more):
    place = pl.BlockSpec(memory_space=pltpu.VMEM)
    several = isinstance(dtype, list)
    if several:
        out_shape = [jax.ShapeDtypeStruct(s, d) for s, d in zip(shape, dtype)]
    else:
        out_shape = jax.ShapeDtypeStruct(shape, dtype)
    specs = dict(in_specs=[place] * len(operands), out_specs=[place] * len(shape) if several else place)
    return pl.pallas_call(
        kernel,
        out_shape=out_shape,
        compiler_params=pltpu.CompilerParams(vmem_limit_bytes=grant << 20),
        cost_estimate=pl.CostEstimate(flops=flops, bytes_accessed=1 << 20, transcendentals=0),
        **(specs | more),
    )(*operands)


def local(forward, backward, targets):
    modes_here, local_rows, double_width = forward.shape
    grid_size = double_width // 2
    count = lax.axis_size("modes")
    mode_total = modes_here * count
    block_rows = local_rows // count
    digits = stages(count)
    sizes = [size for _, size in reversed(digits)]
    half = grid_size // 2
    matmul = 2 * local_rows * double_width * double_width
    me = lax.axis_index("modes")
    owns = [me // stride % size for stride, size in digits]
    last = len(digits) - 1

    c_re, c_im = propagator(grid_size)
    full_re, full_im = jnp.asarray(c_re, bf16), jnp.asarray(c_im, bf16)

    def across(*parts):
        flat = [part.reshape(2, -1, grid_size) for part in parts]
        rows = sum(f.shape[1] for f in flat)
        flops = 4 * rows * grid_size * double_width
        return kernel_call(targets_kernel, (rows, double_width), bf16, flops, (full_re, full_im, *flat))

    unit = mode_total // 8
    cuts = [unit * at for at in range(6)] + [mode_total]
    chunks = [targets[:, a:b] for a, b in zip(cuts, cuts[1:])]
    partner = [exchange(chunk, count // 2, count) for chunk in chunks]
    seen = across(targets)

    first = list(range(last))
    orders = [first, [1, 0] + first[2:]]
    in_kernels = last == 2 and block_rows % 8 == 0
    kept = []
    if in_kernels:
        lanes, wide = 4 * block_rows, pl.BlockSpec((4 * block_rows, double_width), lambda i: (i, 0))
        narrow = pl.BlockSpec((2 * block_rows, grid_size), lambda i: (i, 0))
        halves = kernel_call(
            lambda *refs: products_kernel(block_rows, *refs),
            [(local_rows // 2, grid_size)] * 4,
            [bf16, f32, bf16, f32],
            8 * local_rows * double_width,
            (forward[0], backward[0]),
            grid=(local_rows // lanes,),
            grant=56,
            in_specs=[wide] * 2,
            out_specs=[narrow] * 4,
        )
        got = [exchange(halves[2 * part], digits[part][0], count) for part in range(2)]
        got[0], seen = lax.optimization_barrier((got[0], seen))
        got[1], partner[0] = lax.optimization_barrier((got[1], partner[0]))
        for part in range(2):
            stride = digits[1 - part][0]
            send, keep = kernel_call(
                lambda *refs: halve_kernel(block_rows, stride, *refs),
                [(local_rows // 4, grid_size)] * 2,
                [bf16, f32],
                4 * local_rows * grid_size,
                (halves[2 * part + 1], got[part]),
            )
            came = exchange(send, stride, count)
            if part == 1:
                came, partner[1] = lax.optimization_barrier((came, partner[1]))
            keep = reduce_digit(keep, [came])
            kept.append(keep.reshape(-1, block_rows, grid_size))
    else:
        product = product_of(forward[0], backward[0])
        for part, order in enumerate(orders):
            cols = slice(part * half, (part + 1) * half)
            axes = [last - d for d in range(len(digits))]
            partial = jnp.concatenate([p[:, cols] for p in product], -1)
            partial = partial.reshape(*sizes, block_rows, grid_size)
            for d in order:
                stride, size = digits[d]
                send, keep = split_digit(partial, owns[d], size, axes[d])
                got = [exchange(v, (e + 1) * stride, count) for e, v in enumerate(send)]
                partial = reduce_digit(keep, got)
                axes = [a - (a > axes[d]) for a in axes]
            kept.append(partial)
    stride, size = digits[last]
    send, keep = split_digit(jnp.concatenate(kept, -1), owns[last], size, 0)
    got = [exchange(v, (e + 1) * stride, count) for e, v in enumerate(send)]
    summed = reduce_digit(keep, got)
    parts = []
    for part in range(2):
        over_re = summed[:, part * grid_size : part * grid_size + half]
        over_im = summed[:, part * grid_size + half : (part + 1) * grid_size]
        scale = lax.rsqrt(over_re * over_re + over_im * over_im + mode_total)
        parts += [over_re * scale, over_im * scale]
    block = jnp.concatenate(parts, -1).astype(bf16)

    block = gather_digit(block, owns[last], stride, size, 0, count)
    planes = []
    for part, order in enumerate(orders):
        piece = block[..., part * grid_size : (part + 1) * grid_size]
        done = [last]
        for at, d in enumerate(reversed(order)):
            axis = sum(1 for other in done if other > d)
            piece = gather_digit(piece, owns[d], *digits[d], axis, count)
            if part == 1 and at < 2:
                piece, partner[2 + at] = lax.optimization_barrier((piece, partner[2 + at]))
            done.append(d)
        planes.append(piece.reshape(local_rows, grid_size))

    phase_plane, shaped = kernel_call(
        shape_kernel,
        [(local_rows, double_width), (2 * local_rows, grid_size)],
        [bf16, bf16],
        8 * local_rows * double_width,
        (*planes, forward[0]),
    )
    other = lax.ppermute(shaped, "rows", [(0, 1), (1, 0)])

    order = np.arange(local_rows).reshape(2, count // 2, block_rows).transpose(1, 0, 2).reshape(count // 2, -1)

    def table(cols):
        real, imag = c_re[:local_rows, cols], c_im[:local_rows, cols]
        rows = np.stack([np.concatenate([real, -imag], 1)[order], np.concatenate([imag, real], 1)[order]], 1)
        return jnp.asarray(rows.reshape(2 * local_rows, -1), bf16)

    column_shape = (2 * local_rows, grid_size)
    columns = kernel_call(
        own_kernel, column_shape, f32, matmul // 2, (table(slice(0, local_rows)), shaped)
    )
    columns, other, partner[4] = lax.optimization_barrier((columns, other, partner[4]))
    columns = kernel_call(
        other_kernel, column_shape, bf16, matmul // 2, (table(slice(local_rows, None)), other, columns)
    ).reshape(count // 2, 2, 2 * block_rows, grid_size)

    together = [list(range(count // 2)), list(range(count // 2, count))]
    pixels = lax.all_to_all(columns, "modes", 0, 0, tiled=True, axis_index_groups=together)

    output_fields = kernel_call(
        lambda *refs: fields_kernel(block_rows, *refs),
        (local_rows, double_width),
        bf16,
        matmul,
        (columns, full_re, full_im),
    )
    if block_rows % 8 != 0:
        output_fields = output_fields.reshape(count // 2, 2, block_rows, double_width)
        output_fields = output_fields.transpose(1, 0, 2, 3).reshape(local_rows, double_width)
    pixels, output_fields = lax.optimization_barrier((pixels, output_fields))

    term = kernel_call(
        lambda *refs: coupling_kernel(block_rows, *refs),
        (mode_total // 2, 2 * mode_total),
        f32,
        2 * matmul,
        (pixels, seen, across(*partner[:5]), across(partner[5])),
        grant=16,
    )
    term = term.reshape(mode_total // 2, 2, 1, mode_total).transpose(1, 2, 0, 3)
    in_half = (jnp.arange(2) == me // (count // 2)).reshape(1, 2, 1, 1)
    term = jnp.where(in_half, term, 0.0).reshape(2 * mode_total, mode_total)
    pieces = lax.all_to_all(term, ("modes", "rows"), 0, 0, tiled=True)
    coupling = jnp.sum(pieces, 0, keepdims=True)
    return (phase_plane, output_fields[None], coupling)


def solution(mesh):
    return jax.shard_map(
        local,
        mesh=mesh,
        in_specs=(
            P("modes", "rows", None),
            P("modes", "rows", None),
            P(None, None, ("rows", "modes"), None),
        ),
        out_specs=(P("rows", None), P("modes", "rows", None), P(("modes", "rows"), None)),
        check_vma=False,
    )
```

```python
import numpy as np

import jax
import jax.numpy as jnp
from jax import lax
from jax.experimental import pallas as pl
from jax.experimental.pallas import tpu as pltpu
from jax.sharding import PartitionSpec as P

bf16 = jnp.bfloat16
f32 = jnp.float32


def propagator(grid_size):
    index = np.arange(grid_size)
    centred = (index + grid_size // 2) % grid_size - grid_size // 2
    squared = centred * centred % (4 * grid_size)
    column = np.fft.ifft(np.exp(-2j * np.pi * squared / (4 * grid_size)))
    matrix = column[(index[:, None] - index[None, :]) % grid_size]
    return matrix.real, matrix.imag


def stages(count):
    digits, stride = [], 1
    while count // stride > 4:
        digits.append((stride, 2))
        stride *= 2
    digits.append((stride, count // stride))
    return digits


def exchange(values, offset, count):
    return lax.ppermute(values, "modes", [(i, i ^ offset) for i in range(count)])


def pick(values, index, axis):
    return lax.dynamic_index_in_dim(values, index, axis, keepdims=False)


def reduce_digit(keep, got):
    for g in got:
        keep = keep + g.astype(f32)
    return keep


def gather_digit(block, own, stride, size, axis, count):
    got = [block] + [exchange(block, e * stride, count) for e in range(1, size)]
    stacked = jnp.stack(got, axis)
    if size == 2:
        return jnp.where(own == 0, stacked, jnp.flip(stacked, axis))
    return jnp.stack([pick(stacked, own ^ at, axis) for at in range(size)], axis)


def split_digit(partial, own, size, axis):
    send = [pick(partial, own ^ e, axis).astype(bf16) for e in range(1, size)]
    return send, pick(partial, own, axis)


def product_of(fore, back):
    half = fore.shape[-1] // 2
    fore, back = fore.astype(f32), back.astype(f32)
    fore_re, fore_im = fore[..., :half], fore[..., half:]
    back_re, back_im = back[..., :half], back[..., half:]
    return back_re * fore_re + back_im * fore_im, back_re * fore_im - back_im * fore_re


def products_kernel(rows, fore_hbm, back_hbm, send_a, keep_a, send_b, keep_b, fore_ref, back_ref, sems):
    me = lax.axis_index("modes")
    low, high = me % 2 == 1, me // 2 % 2 == 1
    grid_size = fore_ref.shape[1] // 2
    half = grid_size // 2
    pair = 2 * rows
    groups = fore_ref.shape[0] // (4 * rows)
    copies = []
    for group in range(groups):
        at = pl.ds(group * 4 * rows, 4 * rows)
        for k, (hbm, ref) in enumerate(((fore_hbm, fore_ref), (back_hbm, back_ref))):
            copies.append(pltpu.make_async_copy(hbm.at[at], ref.at[at], sems.at[2 * group + k]))
    for copy in copies:
        copy.start()
    for group in range(groups):
        copies[2 * group].wait()
        copies[2 * group + 1].wait()
        at = pl.ds(group * 4 * rows, 4 * rows)
        out = pl.ds(group * pair, pair)
        for part in range(2):
            cols = [pl.ds(part * half, half), pl.ds(grid_size + part * half, half)]
            fore_re, fore_im = [fore_ref[at, c].astype(f32) for c in cols]
            back_re, back_im = [back_ref[at, c].astype(f32) for c in cols]
            values = (back_re * fore_re + back_im * fore_im, back_re * fore_im - back_im * fore_re)
            for k, v in enumerate(values):
                into = pl.ds(k * half, half)
                if part == 0:
                    first = jnp.concatenate([v[:rows], v[pair : pair + rows]], 0)
                    second = jnp.concatenate([v[rows:pair], v[pair + rows :]], 0)
                    send_a[out, into] = jnp.where(low, first, second).astype(bf16)
                    keep_a[out, into] = jnp.where(low, second, first)
                else:
                    first, second = v[:pair], v[pair:]
                    send_b[out, into] = jnp.where(high, first, second).astype(bf16)
                    keep_b[out, into] = jnp.where(high, second, first)


def times(one, two):
    return jnp.dot(one, two, preferred_element_type=f32)


def own_kernel(table_ref, shaped_ref, out_ref):
    out_ref[...] = times(table_ref[...], shaped_ref[...])


def other_kernel(table_ref, shaped_ref, own_ref, out_ref):
    out_ref[...] = (own_ref[...] + times(table_ref[...], shaped_ref[...])).astype(bf16)


def fields_kernel(block_rows, columns_ref, re_ref, im_ref, out_ref):
    rows, grid_size = out_ref.shape[0], columns_ref.shape[1]
    by_re, by_im = times(columns_ref[...], re_ref[...]), times(columns_ref[...], im_ref[...])
    if block_rows % 8 == 0:
        step, block = 2 * block_rows, block_rows
    else:
        step, block = rows, rows
    for at in range(0, rows, step):
        pieces = [[], []]
        for start in range(2 * at, 2 * (at + step), 2 * block):
            real, imag = slice(start, start + block), slice(start + block, start + 2 * block)
            pieces[0].append(by_re[real] - by_im[imag])
            pieces[1].append(by_im[real] + by_re[imag])
        for k, piece in enumerate(pieces):
            out = jnp.concatenate(piece, 0).astype(bf16)
            out_ref[pl.ds(at, step), pl.ds(k * grid_size, grid_size)] = out


def targets_kernel(targets_ref, re_ref, im_ref, out_ref):
    rows = targets_ref.shape[0] // 2
    real, imag = targets_ref[:rows], targets_ref[rows:]
    c_re, c_im = re_ref[...], im_ref[...]
    out_ref[:rows] = (times(real, c_re) + times(imag, c_im)).astype(bf16)
    out_ref[rows:] = (times(imag, c_re) - times(real, c_im)).astype(bf16)


def exactly(one, two, dims):
    return lax.dot_general(
        one, two, (dims, ((), ())), precision=lax.Precision.HIGHEST, preferred_element_type=f32
    )


def coupling_kernel(block_rows, fields_ref, targets_ref, out_ref):
    modes = out_ref.shape[1]
    product = lax.dot_general(
        fields_ref[...], targets_ref[...], (((1,), (1,)), ((), ())), preferred_element_type=f32
    )
    left, right = product.shape
    row = lax.broadcasted_iota(jnp.int32, (left, right), 0) % block_rows
    col = lax.broadcasted_iota(jnp.int32, (left, right), 1) % block_rows
    product = jnp.where(row == col, product, 0.0)

    def groups(size):
        member = lax.broadcasted_iota(jnp.int32, (size // block_rows, size), 1) // block_rows
        group = lax.broadcasted_iota(jnp.int32, (size // block_rows, size), 0)
        return jnp.where(member == group, 1.0, 0.0).astype(f32)

    if block_rows % 8 == 0:
        product = jnp.sum(product.reshape(left // block_rows, block_rows, right), 1)
    else:
        product = exactly(groups(left), product, ((1,), (0,)))
    product = exactly(product, groups(right), ((1,), (1,)))
    by_re, by_im = product[:, :modes], product[:, modes:]
    mode = lax.broadcasted_iota(jnp.int32, (modes, 2 * modes), 0)
    from_row = lax.broadcasted_iota(jnp.int32, (modes, 2 * modes), 1)
    real = jnp.where(from_row == 2 * mode, 1.0, 0.0).astype(f32)
    imag = jnp.where(from_row == 2 * mode + 1, 1.0, 0.0).astype(f32)
    inner = ((1,), (0,))
    out_ref[:modes] = exactly(real, by_re, inner) + exactly(imag, by_im, inner)
    out_ref[modes:] = exactly(imag, by_re, inner) - exactly(real, by_im, inner)


def kernel_call(kernel, shape, dtype, flops, operands, grant=12, **more):
    place = pl.BlockSpec(memory_space=pltpu.VMEM)
    several = isinstance(dtype, list)
    if several:
        out_shape = [jax.ShapeDtypeStruct(s, d) for s, d in zip(shape, dtype)]
    else:
        out_shape = jax.ShapeDtypeStruct(shape, dtype)
    specs = dict(in_specs=[place] * len(operands), out_specs=[place] * len(shape) if several else place)
    return pl.pallas_call(
        kernel,
        out_shape=out_shape,
        compiler_params=pltpu.CompilerParams(vmem_limit_bytes=grant << 20),
        cost_estimate=pl.CostEstimate(flops=flops, bytes_accessed=4 << 20, transcendentals=0),
        **(specs | more),
    )(*operands)


def local(forward, backward, targets):
    modes_here, local_rows, double_width = forward.shape
    grid_size = double_width // 2
    count = lax.axis_size("modes")
    mode_total = modes_here * count
    block_rows = local_rows // count
    digits = stages(count)
    sizes = [size for _, size in reversed(digits)]
    half = grid_size // 2
    matmul = 2 * local_rows * double_width * double_width

    me = lax.axis_index("modes")
    owns = [me // stride % size for stride, size in digits]
    last = len(digits) - 1
    first = list(range(last))
    orders = [first, [1, 0] + first[2:]]
    kernel_first = block_rows % 8 == 0 and local_rows % (4 * block_rows) == 0
    if kernel_first:
        halves = kernel_call(
            lambda *refs: products_kernel(block_rows, *refs),
            [(local_rows // 2, grid_size)] * 4,
            [bf16, f32, bf16, f32],
            8 * local_rows * double_width,
            (forward[0], backward[0]),
            in_specs=[pl.BlockSpec(memory_space=pltpu.HBM)] * 2,
            scratch_shapes=[pltpu.VMEM((local_rows, double_width), bf16)] * 2
            + [pltpu.SemaphoreType.DMA((2 * local_rows // (4 * block_rows),))],
        )
    else:
        product = product_of(forward[0], backward[0])
    kept = []
    for part, order in enumerate(orders):
        cols = slice(part * half, (part + 1) * half)
        axes = [last - d for d in range(len(digits))]
        if not kernel_first:
            partial = jnp.concatenate([p[:, cols] for p in product], -1)
            partial = partial.reshape(*sizes, block_rows, grid_size)
        for at, d in enumerate(order):
            stride, size = digits[d]
            left = sizes[: axes[d]] + sizes[axes[d] + 1 :] if at == 0 else None
            if at == 0 and kernel_first:
                send = [halves[2 * part].reshape(*left, block_rows, grid_size)]
                keep = halves[2 * part + 1].reshape(*left, block_rows, grid_size)
            else:
                send, keep = split_digit(partial, owns[d], size, axes[d])
            got = [exchange(v, (e + 1) * stride, count) for e, v in enumerate(send)]
            partial = reduce_digit(keep, got)
            axes = [a - (a > axes[d]) for a in axes]
        kept.append(partial)
    stride, size = digits[last]
    send, keep = split_digit(jnp.concatenate(kept, -1), owns[last], size, 0)
    got = [exchange(v, (e + 1) * stride, count) for e, v in enumerate(send)]
    summed = reduce_digit(keep, got)
    parts = []
    for part in range(2):
        over_re = summed[:, part * grid_size : part * grid_size + half]
        over_im = summed[:, part * grid_size + half : (part + 1) * grid_size]
        scale = lax.rsqrt(over_re * over_re + over_im * over_im + mode_total)
        parts += [over_re * scale, over_im * scale]
    block = jnp.concatenate(parts, -1).astype(bf16)

    block = gather_digit(block, owns[last], stride, size, 0, count)
    planes = []
    for part, order in enumerate(orders):
        piece = block[..., part * grid_size : (part + 1) * grid_size]
        done = [last]
        for d in reversed(order):
            axis = sum(1 for other in done if other > d)
            piece = gather_digit(piece, owns[d], *digits[d], axis, count)
            done.append(d)
        planes.append(piece.reshape(local_rows, grid_size))
    plane_re = jnp.concatenate([p[:, :half] for p in planes], -1)
    plane_im = jnp.concatenate([p[:, half:] for p in planes], -1)
    phase_plane = jnp.concatenate([plane_re, plane_im], -1)

    fore = forward[0].astype(f32)
    fore_re, fore_im = fore[:, :grid_size], fore[:, grid_size:]
    plane_re, plane_im = plane_re.astype(f32), plane_im.astype(f32)
    shaped = jnp.concatenate(
        [fore_re * plane_re - fore_im * plane_im, fore_re * plane_im + fore_im * plane_re], 0
    ).astype(bf16)
    other = lax.ppermute(shaped, "rows", [(0, 1), (1, 0)])

    c_re, c_im = propagator(grid_size)
    full_re, full_im = jnp.asarray(c_re, bf16), jnp.asarray(c_im, bf16)
    owners = count if block_rows % 8 == 0 else 1
    order = np.arange(local_rows).reshape(owners, -1)

    def table(cols):
        real, imag = c_re[:local_rows, cols], c_im[:local_rows, cols]
        rows = np.stack([np.concatenate([real, -imag], 1)[order], np.concatenate([imag, real], 1)[order]], 1)
        return jnp.asarray(rows.reshape(2 * local_rows, -1), bf16)

    column_shape = (2 * local_rows, grid_size)
    columns = kernel_call(
        own_kernel, column_shape, f32, matmul // 2, (table(slice(0, local_rows)), shaped)
    )
    columns, other = lax.optimization_barrier((columns, other))
    columns = kernel_call(
        other_kernel, column_shape, bf16, matmul // 2, (table(slice(local_rows, None)), other, columns)
    )
    blocks = columns.reshape(owners, 2, -1, block_rows, grid_size).transpose(0, 2, 1, 3, 4)
    blocks = blocks.reshape(count, 2 * block_rows, grid_size)
    pixels = lax.all_to_all(blocks, "modes", 0, 0, tiled=True).reshape(column_shape)

    seen = kernel_call(
        targets_kernel, column_shape, bf16, matmul, (targets.reshape(column_shape), full_re, full_im)
    )
    output_fields = kernel_call(
        lambda *refs: fields_kernel(block_rows, *refs),
        (local_rows, double_width),
        bf16,
        matmul,
        (columns, full_re, full_im),
    )
    pixels, output_fields, seen = lax.optimization_barrier((pixels, output_fields, seen))

    term = kernel_call(
        lambda *refs: coupling_kernel(block_rows, *refs),
        (2 * mode_total, mode_total),
        f32,
        matmul,
        (pixels, seen),
    )
    pieces = lax.all_to_all(term, ("modes", "rows"), 0, 0, tiled=True)
    coupling = jnp.sum(pieces, 0, keepdims=True)
    return (phase_plane, output_fields[None], coupling)


def solution(mesh):
    return jax.shard_map(
        local,
        mesh=mesh,
        in_specs=(
            P("modes", "rows", None),
            P("modes", "rows", None),
            P(None, None, ("rows", "modes"), None),
        ),
        out_specs=(P("rows", None), P("modes", "rows", None), P(("modes", "rows"), None)),
        check_vma=False,
    )
```

```python
import numpy as np

import jax
import jax.numpy as jnp
from jax import lax
from jax.experimental import pallas as pl
from jax.experimental.pallas import tpu as pltpu
from jax.sharding import PartitionSpec as P

bf16 = jnp.bfloat16
f32 = jnp.float32


def propagator(grid_size):
    index = np.arange(grid_size)
    centred = (index + grid_size // 2) % grid_size - grid_size // 2
    squared = centred * centred % (4 * grid_size)
    column = np.fft.ifft(np.exp(-2j * np.pi * squared / (4 * grid_size)))
    matrix = column[(index[:, None] - index[None, :]) % grid_size]
    return matrix.real, matrix.imag


def stages(count):
    digits, stride = [], 1
    while count // stride > 4:
        digits.append((stride, 2))
        stride *= 2
    digits.append((stride, count // stride))
    return digits


def exchange(values, offset, count):
    return lax.ppermute(values, "modes", [(i, i ^ offset) for i in range(count)])


def pick(values, index, axis):
    return lax.dynamic_index_in_dim(values, index, axis, keepdims=False)


def reduce_digit(keep, got):
    for g in got:
        keep = keep + g.astype(f32)
    return keep


def gather_digit(block, own, stride, size, axis, count):
    got = [block] + [exchange(block, e * stride, count) for e in range(1, size)]
    stacked = jnp.stack(got, axis)
    if size == 2:
        return jnp.where(own == 0, stacked, jnp.flip(stacked, axis))
    return jnp.stack([pick(stacked, own ^ at, axis) for at in range(size)], axis)


def split_digit(partial, own, size, axis):
    send = [pick(partial, own ^ e, axis).astype(bf16) for e in range(1, size)]
    return send, pick(partial, own, axis)


def product_of(fore, back):
    half = fore.shape[-1] // 2
    fore, back = fore.astype(f32), back.astype(f32)
    fore_re, fore_im = fore[..., :half], fore[..., half:]
    back_re, back_im = back[..., :half], back[..., half:]
    return back_re * fore_re + back_im * fore_im, back_re * fore_im - back_im * fore_re


def products_kernel(rows, fore_hbm, back_hbm, send_a, keep_a, send_b, keep_b, fore_ref, back_ref, sems):
    me = lax.axis_index("modes")
    low, high = me % 2 == 1, me // 2 % 2 == 1
    grid_size = fore_ref.shape[1] // 2
    half = grid_size // 2
    pair = 2 * rows
    groups = fore_ref.shape[0] // (4 * rows)
    copies = []
    for group in range(groups):
        at = pl.ds(group * 4 * rows, 4 * rows)
        for k, (hbm, ref) in enumerate(((fore_hbm, fore_ref), (back_hbm, back_ref))):
            copies.append(pltpu.make_async_copy(hbm.at[at], ref.at[at], sems.at[2 * group + k]))
    for copy in copies:
        copy.start()
    for group in range(groups):
        copies[2 * group].wait()
        copies[2 * group + 1].wait()
        at = pl.ds(group * 4 * rows, 4 * rows)
        out = pl.ds(group * pair, pair)
        for part in range(2):
            cols = [pl.ds(part * half, half), pl.ds(grid_size + part * half, half)]
            fore_re, fore_im = [fore_ref[at, c].astype(f32) for c in cols]
            back_re, back_im = [back_ref[at, c].astype(f32) for c in cols]
            values = (back_re * fore_re + back_im * fore_im, back_re * fore_im - back_im * fore_re)
            for k, v in enumerate(values):
                into = pl.ds(k * half, half)
                if part == 0:
                    first = jnp.concatenate([v[:rows], v[pair : pair + rows]], 0)
                    second = jnp.concatenate([v[rows:pair], v[pair + rows :]], 0)
                    send_a[out, into] = jnp.where(low, first, second).astype(bf16)
                    keep_a[out, into] = jnp.where(low, second, first)
                else:
                    first, second = v[:pair], v[pair:]
                    send_b[out, into] = jnp.where(high, first, second).astype(bf16)
                    keep_b[out, into] = jnp.where(high, second, first)


def times(one, two):
    return jnp.dot(one, two, preferred_element_type=f32)


def own_kernel(table_ref, shaped_ref, out_ref):
    out_ref[...] = times(table_ref[...], shaped_ref[...])


def other_kernel(table_ref, shaped_ref, own_ref, out_ref):
    out_ref[...] = (own_ref[...] + times(table_ref[...], shaped_ref[...])).astype(bf16)


def fields_kernel(block_rows, columns_ref, re_ref, im_ref, out_ref):
    rows, grid_size = out_ref.shape[0], columns_ref.shape[1]
    by_re, by_im = times(columns_ref[...], re_ref[...]), times(columns_ref[...], im_ref[...])
    if block_rows % 8 == 0:
        step, block = 2 * block_rows, block_rows
    else:
        step, block = rows, rows
    for at in range(0, rows, step):
        pieces = [[], []]
        for start in range(2 * at, 2 * (at + step), 2 * block):
            real, imag = slice(start, start + block), slice(start + block, start + 2 * block)
            pieces[0].append(by_re[real] - by_im[imag])
            pieces[1].append(by_im[real] + by_re[imag])
        for k, piece in enumerate(pieces):
            out = jnp.concatenate(piece, 0).astype(bf16)
            out_ref[pl.ds(at, step), pl.ds(k * grid_size, grid_size)] = out


def targets_kernel(targets_ref, re_ref, im_ref, out_ref):
    rows = targets_ref.shape[0] // 2
    real, imag = targets_ref[:rows], targets_ref[rows:]
    c_re, c_im = re_ref[...], im_ref[...]
    out_ref[:rows] = (times(real, c_re) + times(imag, c_im)).astype(bf16)
    out_ref[rows:] = (times(imag, c_re) - times(real, c_im)).astype(bf16)


def exactly(one, two, dims):
    return lax.dot_general(
        one, two, (dims, ((), ())), precision=lax.Precision.HIGHEST, preferred_element_type=f32
    )


def coupling_kernel(block_rows, by_xor, fields_ref, targets_ref, out_ref):
    modes = out_ref.shape[1]
    product = lax.dot_general(
        fields_ref[...], targets_ref[...], (((1,), (1,)), ((), ())), preferred_element_type=f32
    )
    left, right = product.shape
    row = lax.broadcasted_iota(jnp.int32, (left, right), 0) % block_rows
    col = lax.broadcasted_iota(jnp.int32, (left, right), 1) % block_rows
    product = jnp.where(row == col, product, 0.0)

    def groups(size):
        member = lax.broadcasted_iota(jnp.int32, (size // block_rows, size), 1) // block_rows
        group = lax.broadcasted_iota(jnp.int32, (size // block_rows, size), 0)
        return jnp.where(member == group, 1.0, 0.0).astype(f32)

    if block_rows % 8 == 0:
        product = jnp.sum(product.reshape(left // block_rows, block_rows, right), 1)
    else:
        product = exactly(groups(left), product, ((1,), (0,)))
    product = exactly(product, groups(right), ((1,), (1,)))
    by_re, by_im = product[:, :modes], product[:, modes:]
    mode = lax.broadcasted_iota(jnp.int32, (modes, 2 * modes), 0)
    if by_xor:
        mode = mode ^ lax.axis_index("modes")
        mode = mode % (modes // 2) * 2 + mode // (modes // 2)
    from_row = lax.broadcasted_iota(jnp.int32, (modes, 2 * modes), 1)
    real = jnp.where(from_row == 2 * mode, 1.0, 0.0).astype(f32)
    imag = jnp.where(from_row == 2 * mode + 1, 1.0, 0.0).astype(f32)
    inner = ((1,), (0,))
    out_ref[:modes] = exactly(real, by_re, inner) + exactly(imag, by_im, inner)
    out_ref[modes:] = exactly(imag, by_re, inner) - exactly(real, by_im, inner)


def kernel_call(kernel, shape, dtype, flops, operands, grant=12, **more):
    place = pl.BlockSpec(memory_space=pltpu.VMEM)
    several = isinstance(dtype, list)
    if several:
        out_shape = [jax.ShapeDtypeStruct(s, d) for s, d in zip(shape, dtype)]
    else:
        out_shape = jax.ShapeDtypeStruct(shape, dtype)
    specs = dict(in_specs=[place] * len(operands), out_specs=[place] * len(shape) if several else place)
    return pl.pallas_call(
        kernel,
        out_shape=out_shape,
        compiler_params=pltpu.CompilerParams(vmem_limit_bytes=grant << 20),
        cost_estimate=pl.CostEstimate(flops=flops, bytes_accessed=4 << 20, transcendentals=0),
        **(specs | more),
    )(*operands)


def local(forward, backward, targets):
    modes_here, local_rows, double_width = forward.shape
    grid_size = double_width // 2
    count = lax.axis_size("modes")
    mode_total = modes_here * count
    block_rows = local_rows // count
    digits = stages(count)
    sizes = [size for _, size in reversed(digits)]
    half = grid_size // 2
    matmul = 2 * local_rows * double_width * double_width

    me = lax.axis_index("modes")
    owns = [me // stride % size for stride, size in digits]
    last = len(digits) - 1
    first = list(range(last))
    orders = [first, [1, 0] + first[2:]]
    kernel_first = block_rows % 8 == 0 and local_rows % (4 * block_rows) == 0
    if kernel_first:
        halves = kernel_call(
            lambda *refs: products_kernel(block_rows, *refs),
            [(local_rows // 2, grid_size)] * 4,
            [bf16, f32, bf16, f32],
            8 * local_rows * double_width,
            (forward[0], backward[0]),
            in_specs=[pl.BlockSpec(memory_space=pltpu.HBM)] * 2,
            scratch_shapes=[pltpu.VMEM((local_rows, double_width), bf16)] * 2
            + [pltpu.SemaphoreType.DMA((2 * local_rows // (4 * block_rows),))],
        )
    else:
        product = product_of(forward[0], backward[0])
    kept = []
    for part, order in enumerate(orders):
        cols = slice(part * half, (part + 1) * half)
        axes = [last - d for d in range(len(digits))]
        if not kernel_first:
            partial = jnp.concatenate([p[:, cols] for p in product], -1)
            partial = partial.reshape(*sizes, block_rows, grid_size)
        for at, d in enumerate(order):
            stride, size = digits[d]
            left = sizes[: axes[d]] + sizes[axes[d] + 1 :] if at == 0 else None
            if at == 0 and kernel_first:
                send = [halves[2 * part].reshape(*left, block_rows, grid_size)]
                keep = halves[2 * part + 1].reshape(*left, block_rows, grid_size)
            else:
                send, keep = split_digit(partial, owns[d], size, axes[d])
            got = [exchange(v, (e + 1) * stride, count) for e, v in enumerate(send)]
            partial = reduce_digit(keep, got)
            axes = [a - (a > axes[d]) for a in axes]
        kept.append(partial)
    stride, size = digits[last]
    send, keep = split_digit(jnp.concatenate(kept, -1), owns[last], size, 0)
    got = [exchange(v, (e + 1) * stride, count) for e, v in enumerate(send)]
    summed = reduce_digit(keep, got)
    parts = []
    for part in range(2):
        over_re = summed[:, part * grid_size : part * grid_size + half]
        over_im = summed[:, part * grid_size + half : (part + 1) * grid_size]
        scale = lax.rsqrt(over_re * over_re + over_im * over_im + mode_total)
        parts += [over_re * scale, over_im * scale]
    block = jnp.concatenate(parts, -1).astype(bf16)

    block = gather_digit(block, owns[last], stride, size, 0, count)
    planes = []
    for part, order in enumerate(orders):
        piece = block[..., part * grid_size : (part + 1) * grid_size]
        done = [last]
        for d in reversed(order):
            axis = sum(1 for other in done if other > d)
            piece = gather_digit(piece, owns[d], *digits[d], axis, count)
            done.append(d)
        planes.append(piece.reshape(local_rows, grid_size))
    plane_re = jnp.concatenate([p[:, :half] for p in planes], -1)
    plane_im = jnp.concatenate([p[:, half:] for p in planes], -1)
    phase_plane = jnp.concatenate([plane_re, plane_im], -1)

    fore = forward[0].astype(f32)
    fore_re, fore_im = fore[:, :grid_size], fore[:, grid_size:]
    plane_re, plane_im = plane_re.astype(f32), plane_im.astype(f32)
    shaped = jnp.concatenate(
        [fore_re * plane_re - fore_im * plane_im, fore_re * plane_im + fore_im * plane_re], 0
    ).astype(bf16)
    other = lax.ppermute(shaped, "rows", [(0, 1), (1, 0)])

    c_re, c_im = propagator(grid_size)
    full_re, full_im = jnp.asarray(c_re, bf16), jnp.asarray(c_im, bf16)
    owners = count if block_rows % 8 == 0 else 1
    order = np.arange(local_rows).reshape(owners, -1)

    def table(cols):
        real, imag = c_re[:local_rows, cols], c_im[:local_rows, cols]
        rows = np.stack([np.concatenate([real, -imag], 1)[order], np.concatenate([imag, real], 1)[order]], 1)
        return jnp.asarray(rows.reshape(2 * local_rows, -1), bf16)

    column_shape = (2 * local_rows, grid_size)
    columns = kernel_call(
        own_kernel, column_shape, f32, matmul // 2, (table(slice(0, local_rows)), shaped)
    )
    columns, other = lax.optimization_barrier((columns, other))
    columns = kernel_call(
        other_kernel, column_shape, bf16, matmul // 2, (table(slice(local_rows, None)), other, columns)
    )
    blocks = columns.reshape(owners, 2, -1, block_rows, grid_size).transpose(0, 2, 1, 3, 4)
    blocks = blocks.reshape(count, 2 * block_rows, grid_size)
    if count <= 16:
        turns = [at // 2 + count // 2 * (at % 2) for at in range(count)]
        pixels = tuple(exchange(pick(blocks, me ^ e, 0), e, count) if e else pick(blocks, me, 0) for e in turns)
    else:
        pixels = (lax.all_to_all(blocks, "modes", 0, 0, tiled=True),)

    output_fields = kernel_call(
        lambda *refs: fields_kernel(block_rows, *refs),
        (local_rows, double_width),
        bf16,
        matmul,
        (columns, full_re, full_im),
    )
    targets, output_fields = lax.optimization_barrier((targets, output_fields))
    seen = kernel_call(
        targets_kernel, column_shape, bf16, matmul, (targets.reshape(column_shape), full_re, full_im)
    )
    pixels, output_fields, seen = lax.optimization_barrier((pixels, output_fields, seen))

    term = kernel_call(
        lambda *refs: coupling_kernel(block_rows, len(pixels) > 1, *refs),
        (2 * mode_total, mode_total),
        f32,
        matmul,
        (jnp.concatenate(pixels, 0).reshape(column_shape), seen),
    )
    pieces = lax.all_to_all(term, ("modes", "rows"), 0, 0, tiled=True)
    coupling = jnp.sum(pieces, 0, keepdims=True)
    return (phase_plane, output_fields[None], coupling)


def solution(mesh):
    return jax.shard_map(
        local,
        mesh=mesh,
        in_specs=(
            P("modes", "rows", None),
            P("modes", "rows", None),
            P(None, None, ("rows", "modes"), None),
        ),
        out_specs=(P("rows", None), P("modes", "rows", None), P(("modes", "rows"), None)),
        check_vma=False,
    )
```

```python
import numpy as np

import jax
import jax.numpy as jnp
from jax import lax
from jax.experimental import pallas as pl
from jax.experimental.pallas import tpu as pltpu
from jax.sharding import PartitionSpec as P

bf16 = jnp.bfloat16
f32 = jnp.float32


def propagator(grid_size):
    index = np.arange(grid_size)
    centred = (index + grid_size // 2) % grid_size - grid_size // 2
    squared = centred * centred % (4 * grid_size)
    column = np.fft.ifft(np.exp(-2j * np.pi * squared / (4 * grid_size)))
    matrix = column[(index[:, None] - index[None, :]) % grid_size]
    return matrix.real, matrix.imag


def stages(count):
    digits, stride = [], 1
    while count // stride > 4:
        digits.append((stride, 2))
        stride *= 2
    digits.append((stride, count // stride))
    return digits


def exchange(values, offset, count):
    return lax.ppermute(values, "modes", [(i, i ^ offset) for i in range(count)])


def pick(values, index, axis):
    return lax.dynamic_index_in_dim(values, index, axis, keepdims=False)


def reduce_digit(keep, got):
    for g in got:
        keep = keep + g.astype(f32)
    return keep


def gather_digit(block, own, stride, size, axis, count):
    got = [block] + [exchange(block, e * stride, count) for e in range(1, size)]
    stacked = jnp.stack(got, axis)
    if size == 2:
        return jnp.where(own == 0, stacked, jnp.flip(stacked, axis))
    return jnp.stack([pick(stacked, own ^ at, axis) for at in range(size)], axis)


def split_digit(partial, own, size, axis):
    send = [pick(partial, own ^ e, axis).astype(bf16) for e in range(1, size)]
    return send, pick(partial, own, axis)


def product_of(fore, back):
    half = fore.shape[-1] // 2
    fore, back = fore.astype(f32), back.astype(f32)
    fore_re, fore_im = fore[..., :half], fore[..., half:]
    back_re, back_im = back[..., :half], back[..., half:]
    return back_re * fore_re + back_im * fore_im, back_re * fore_im - back_im * fore_re


def products_kernel(rows, fore_hbm, back_hbm, send_a, keep_a, send_b, keep_b, fore_ref, back_ref, sems):
    me = lax.axis_index("modes")
    low, high = me % 2 == 1, me // 2 % 2 == 1
    grid_size = fore_ref.shape[1] // 2
    half = grid_size // 2
    pair = 2 * rows
    groups = fore_ref.shape[0] // (4 * rows)
    copies = []
    for group in range(groups):
        at = pl.ds(group * 4 * rows, 4 * rows)
        for k, (hbm, ref) in enumerate(((fore_hbm, fore_ref), (back_hbm, back_ref))):
            copies.append(pltpu.make_async_copy(hbm.at[at], ref.at[at], sems.at[2 * group + k]))
    for copy in copies:
        copy.start()
    for group in range(groups):
        copies[2 * group].wait()
        copies[2 * group + 1].wait()
        at = pl.ds(group * 4 * rows, 4 * rows)
        out = pl.ds(group * pair, pair)
        for part in range(2):
            cols = [pl.ds(part * half, half), pl.ds(grid_size + part * half, half)]
            fore_re, fore_im = [fore_ref[at, c].astype(f32) for c in cols]
            back_re, back_im = [back_ref[at, c].astype(f32) for c in cols]
            values = (back_re * fore_re + back_im * fore_im, back_re * fore_im - back_im * fore_re)
            for k, v in enumerate(values):
                into = pl.ds(k * half, half)
                if part == 0:
                    first = jnp.concatenate([v[:rows], v[pair : pair + rows]], 0)
                    second = jnp.concatenate([v[rows:pair], v[pair + rows :]], 0)
                    send_a[out, into] = jnp.where(low, first, second).astype(bf16)
                    keep_a[out, into] = jnp.where(low, second, first)
                else:
                    first, second = v[:pair], v[pair:]
                    send_b[out, into] = jnp.where(high, first, second).astype(bf16)
                    keep_b[out, into] = jnp.where(high, second, first)


def times(one, two):
    return jnp.dot(one, two, preferred_element_type=f32)


def own_kernel(table_ref, shaped_ref, out_ref):
    out_ref[...] = times(table_ref[...], shaped_ref[...])


def other_kernel(table_ref, shaped_ref, own_ref, out_ref):
    out_ref[...] = (own_ref[...] + times(table_ref[...], shaped_ref[...])).astype(bf16)


def fields_kernel(block_rows, columns_ref, re_ref, im_ref, out_ref):
    rows, grid_size = out_ref.shape[0], columns_ref.shape[1]
    by_re, by_im = times(columns_ref[...], re_ref[...]), times(columns_ref[...], im_ref[...])
    if block_rows % 8 == 0:
        step, block = 2 * block_rows, block_rows
    else:
        step, block = rows, rows
    for at in range(0, rows, step):
        pieces = [[], []]
        for start in range(2 * at, 2 * (at + step), 2 * block):
            real, imag = slice(start, start + block), slice(start + block, start + 2 * block)
            pieces[0].append(by_re[real] - by_im[imag])
            pieces[1].append(by_im[real] + by_re[imag])
        for k, piece in enumerate(pieces):
            out = jnp.concatenate(piece, 0).astype(bf16)
            out_ref[pl.ds(at, step), pl.ds(k * grid_size, grid_size)] = out


def targets_kernel(targets_ref, re_ref, im_ref, out_ref):
    rows = targets_ref.shape[0] // 2
    real, imag = targets_ref[:rows], targets_ref[rows:]
    c_re, c_im = re_ref[...], im_ref[...]
    out_ref[:rows] = (times(real, c_re) + times(imag, c_im)).astype(bf16)
    out_ref[rows:] = (times(imag, c_re) - times(real, c_im)).astype(bf16)


def exactly(one, two, dims):
    return lax.dot_general(
        one, two, (dims, ((), ())), precision=lax.Precision.HIGHEST, preferred_element_type=f32
    )


def coupling_kernel(block_rows, by_xor, fields_ref, targets_ref, out_ref):
    modes = out_ref.shape[1]
    product = lax.dot_general(
        fields_ref[...], targets_ref[...], (((1,), (1,)), ((), ())), preferred_element_type=f32
    )
    left, right = product.shape
    row = lax.broadcasted_iota(jnp.int32, (left, right), 0) % block_rows
    col = lax.broadcasted_iota(jnp.int32, (left, right), 1) % block_rows
    product = jnp.where(row == col, product, 0.0)

    def groups(size):
        member = lax.broadcasted_iota(jnp.int32, (size // block_rows, size), 1) // block_rows
        group = lax.broadcasted_iota(jnp.int32, (size // block_rows, size), 0)
        return jnp.where(member == group, 1.0, 0.0).astype(f32)

    if block_rows % 8 == 0:
        product = jnp.sum(product.reshape(left // block_rows, block_rows, right), 1)
    else:
        product = exactly(groups(left), product, ((1,), (0,)))
    product = exactly(product, groups(right), ((1,), (1,)))
    by_re, by_im = product[:, :modes], product[:, modes:]
    mode = lax.broadcasted_iota(jnp.int32, (modes, 2 * modes), 0)
    if by_xor:
        mode = mode ^ lax.axis_index("modes")
        mode = mode % (modes // 2) * 2 + mode // (modes // 2)
    from_row = lax.broadcasted_iota(jnp.int32, (modes, 2 * modes), 1)
    real = jnp.where(from_row == 2 * mode, 1.0, 0.0).astype(f32)
    imag = jnp.where(from_row == 2 * mode + 1, 1.0, 0.0).astype(f32)
    inner = ((1,), (0,))
    out_ref[:modes] = exactly(real, by_re, inner) + exactly(imag, by_im, inner)
    out_ref[modes:] = exactly(imag, by_re, inner) - exactly(real, by_im, inner)


def kernel_call(kernel, shape, dtype, flops, operands, grant=12, **more):
    place = pl.BlockSpec(memory_space=pltpu.VMEM)
    several = isinstance(dtype, list)
    if several:
        out_shape = [jax.ShapeDtypeStruct(s, d) for s, d in zip(shape, dtype)]
    else:
        out_shape = jax.ShapeDtypeStruct(shape, dtype)
    specs = dict(in_specs=[place] * len(operands), out_specs=[place] * len(shape) if several else place)
    return pl.pallas_call(
        kernel,
        out_shape=out_shape,
        compiler_params=pltpu.CompilerParams(vmem_limit_bytes=grant << 20),
        cost_estimate=pl.CostEstimate(flops=flops, bytes_accessed=4 << 20, transcendentals=0),
        **(specs | more),
    )(*operands)


def local(forward, backward, targets):
    modes_here, local_rows, double_width = forward.shape
    grid_size = double_width // 2
    count = lax.axis_size("modes")
    mode_total = modes_here * count
    block_rows = local_rows // count
    digits = stages(count)
    sizes = [size for _, size in reversed(digits)]
    half = grid_size // 2
    matmul = 2 * local_rows * double_width * double_width

    c_re, c_im = propagator(grid_size)
    full_re, full_im = jnp.asarray(c_re, bf16), jnp.asarray(c_im, bf16)
    column_shape = (2 * local_rows, grid_size)
    seen = kernel_call(
        targets_kernel, column_shape, bf16, matmul, (targets.reshape(column_shape), full_re, full_im)
    )

    me = lax.axis_index("modes")
    owns = [me // stride % size for stride, size in digits]
    last = len(digits) - 1
    first = list(range(last))
    orders = [first, [1, 0] + first[2:]]
    kernel_first = block_rows % 8 == 0 and local_rows % (4 * block_rows) == 0
    if kernel_first:
        halves = kernel_call(
            lambda *refs: products_kernel(block_rows, *refs),
            [(local_rows // 2, grid_size)] * 4,
            [bf16, f32, bf16, f32],
            8 * local_rows * double_width,
            (forward[0], backward[0]),
            grant=52,
            in_specs=[pl.BlockSpec(memory_space=pltpu.HBM)] * 2,
            scratch_shapes=[pltpu.VMEM((local_rows, double_width), bf16)] * 2
            + [pltpu.SemaphoreType.DMA((2 * local_rows // (4 * block_rows),))],
        )
    else:
        product = product_of(forward[0], backward[0])
    kept = []
    for part, order in enumerate(orders):
        cols = slice(part * half, (part + 1) * half)
        axes = [last - d for d in range(len(digits))]
        if not kernel_first:
            partial = jnp.concatenate([p[:, cols] for p in product], -1)
            partial = partial.reshape(*sizes, block_rows, grid_size)
        for at, d in enumerate(order):
            stride, size = digits[d]
            left = sizes[: axes[d]] + sizes[axes[d] + 1 :] if at == 0 else None
            if at == 0 and kernel_first:
                send = [halves[2 * part].reshape(*left, block_rows, grid_size)]
                keep = halves[2 * part + 1].reshape(*left, block_rows, grid_size)
            else:
                send, keep = split_digit(partial, owns[d], size, axes[d])
            got = [exchange(v, (e + 1) * stride, count) for e, v in enumerate(send)]
            if at == 0 and part == 0:
                got, seen = lax.optimization_barrier((got, seen))
            partial = reduce_digit(keep, got)
            axes = [a - (a > axes[d]) for a in axes]
        kept.append(partial)
    stride, size = digits[last]
    send, keep = split_digit(jnp.concatenate(kept, -1), owns[last], size, 0)
    got = [exchange(v, (e + 1) * stride, count) for e, v in enumerate(send)]
    summed = reduce_digit(keep, got)
    parts = []
    for part in range(2):
        over_re = summed[:, part * grid_size : part * grid_size + half]
        over_im = summed[:, part * grid_size + half : (part + 1) * grid_size]
        scale = lax.rsqrt(over_re * over_re + over_im * over_im + mode_total)
        parts += [over_re * scale, over_im * scale]
    block = jnp.concatenate(parts, -1).astype(bf16)

    block = gather_digit(block, owns[last], stride, size, 0, count)
    planes = []
    for part, order in enumerate(orders):
        piece = block[..., part * grid_size : (part + 1) * grid_size]
        done = [last]
        for d in reversed(order):
            axis = sum(1 for other in done if other > d)
            piece = gather_digit(piece, owns[d], *digits[d], axis, count)
            done.append(d)
        planes.append(piece.reshape(local_rows, grid_size))
    plane_re = jnp.concatenate([p[:, :half] for p in planes], -1)
    plane_im = jnp.concatenate([p[:, half:] for p in planes], -1)
    phase_plane = jnp.concatenate([plane_re, plane_im], -1)

    fore = forward[0].astype(f32)
    fore_re, fore_im = fore[:, :grid_size], fore[:, grid_size:]
    plane_re, plane_im = plane_re.astype(f32), plane_im.astype(f32)
    shaped = jnp.concatenate(
        [fore_re * plane_re - fore_im * plane_im, fore_re * plane_im + fore_im * plane_re], 0
    ).astype(bf16)
    other = lax.ppermute(shaped, "rows", [(0, 1), (1, 0)])

    owners = count if block_rows % 8 == 0 else 1
    order = np.arange(local_rows).reshape(owners, -1)

    def table(cols):
        real, imag = c_re[:local_rows, cols], c_im[:local_rows, cols]
        rows = np.stack([np.concatenate([real, -imag], 1)[order], np.concatenate([imag, real], 1)[order]], 1)
        return jnp.asarray(rows.reshape(2 * local_rows, -1), bf16)

    columns = kernel_call(
        own_kernel, column_shape, f32, matmul // 2, (table(slice(0, local_rows)), shaped)
    )
    columns, other, phase_plane = lax.optimization_barrier((columns, other, phase_plane))
    columns = kernel_call(
        other_kernel, column_shape, bf16, matmul // 2, (table(slice(local_rows, None)), other, columns)
    )
    blocks = columns.reshape(owners, 2, -1, block_rows, grid_size).transpose(0, 2, 1, 3, 4)
    blocks = blocks.reshape(count, 2 * block_rows, grid_size)
    if count <= 16:
        turns = [at // 2 + count // 2 * (at % 2) for at in range(count)]
        pixels = tuple(exchange(pick(blocks, me ^ e, 0), e, count) if e else pick(blocks, me, 0) for e in turns)
    else:
        pixels = (lax.all_to_all(blocks, "modes", 0, 0, tiled=True),)

    term = kernel_call(
        lambda *refs: coupling_kernel(block_rows, len(pixels) > 1, *refs),
        (2 * mode_total, mode_total),
        f32,
        matmul,
        (jnp.concatenate(pixels, 0).reshape(column_shape), seen),
    )
    columns, term = lax.optimization_barrier((columns, term))
    output_fields = kernel_call(
        lambda *refs: fields_kernel(block_rows, *refs),
        (local_rows, double_width),
        bf16,
        matmul,
        (columns, full_re, full_im),
    )
    pieces = lax.all_to_all(term, ("modes", "rows"), 0, 0, tiled=True)
    coupling = jnp.sum(pieces, 0, keepdims=True)
    return (phase_plane, output_fields[None], coupling)


def solution(mesh):
    return jax.shard_map(
        local,
        mesh=mesh,
        in_specs=(
            P("modes", "rows", None),
            P("modes", "rows", None),
            P(None, None, ("rows", "modes"), None),
        ),
        out_specs=(P("rows", None), P("modes", "rows", None), P(("modes", "rows"), None)),
        check_vma=False,
    )
```

```python
import numpy as np

import jax
import jax.numpy as jnp
from jax import lax
from jax.experimental import pallas as pl
from jax.experimental.pallas import tpu as pltpu
from jax.sharding import PartitionSpec as P

bf16 = jnp.bfloat16
f32 = jnp.float32
LANES = 5


def propagator(grid_size):
    index = np.arange(grid_size)
    centred = (index + grid_size // 2) % grid_size - grid_size // 2
    squared = centred * centred % (4 * grid_size)
    column = np.fft.ifft(np.exp(-2j * np.pi * squared / (4 * grid_size)))
    matrix = column[(index[:, None] - index[None, :]) % grid_size]
    return matrix.real, matrix.imag


def stages(count):
    digits, stride = [], 1
    while count // stride > 4:
        digits.append((stride, 2))
        stride *= 2
    digits.append((stride, count // stride))
    return digits


def exchange(values, offset, count):
    return lax.ppermute(values, "modes", [(i, i ^ offset) for i in range(count)])


def pick(values, index, axis):
    return lax.dynamic_index_in_dim(values, index, axis, keepdims=False)


def reduce_digit(keep, got):
    for g in got:
        keep = keep + g.astype(f32)
    return keep


def gather_digit(block, own, stride, size, axis, count):
    got = [block] + [exchange(block, e * stride, count) for e in range(1, size)]
    stacked = jnp.stack(got, axis)
    if size == 2:
        return jnp.where(own == 0, stacked, jnp.flip(stacked, axis))
    return jnp.stack([pick(stacked, own ^ at, axis) for at in range(size)], axis)


def split_digit(partial, own, size, axis):
    send = [pick(partial, own ^ e, axis).astype(bf16) for e in range(1, size)]
    return send, pick(partial, own, axis)


def product_of(fore, back):
    half = fore.shape[-1] // 2
    fore, back = fore.astype(f32), back.astype(f32)
    fore_re, fore_im = fore[..., :half], fore[..., half:]
    back_re, back_im = back[..., :half], back[..., half:]
    return back_re * fore_re + back_im * fore_im, back_re * fore_im - back_im * fore_re


def products_kernel(rows, fore_hbm, back_hbm, send_a, keep_a, send_b, keep_b, fore_ref, back_ref, sems):
    me = lax.axis_index("modes")
    low, high = me % 2 == 1, me // 2 % 2 == 1
    grid_size = fore_ref.shape[1] // 2
    half = grid_size // 2
    pair = 2 * rows
    groups = fore_ref.shape[0] // (4 * rows)
    copies = []
    for group in range(groups):
        at = pl.ds(group * 4 * rows, 4 * rows)
        for k, (hbm, ref) in enumerate(((fore_hbm, fore_ref), (back_hbm, back_ref))):
            copies.append(pltpu.make_async_copy(hbm.at[at], ref.at[at], sems.at[2 * group + k]))
    for copy in copies:
        copy.start()
    for group in range(groups):
        copies[2 * group].wait()
        copies[2 * group + 1].wait()
        at = pl.ds(group * 4 * rows, 4 * rows)
        out = pl.ds(group * pair, pair)
        for part in range(2):
            cols = [pl.ds(part * half, half), pl.ds(grid_size + part * half, half)]
            fore_re, fore_im = [fore_ref[at, c].astype(f32) for c in cols]
            back_re, back_im = [back_ref[at, c].astype(f32) for c in cols]
            values = (back_re * fore_re + back_im * fore_im, back_re * fore_im - back_im * fore_re)
            for k, v in enumerate(values):
                into = pl.ds(k * half, half)
                if part == 0:
                    first = jnp.concatenate([v[:rows], v[pair : pair + rows]], 0)
                    second = jnp.concatenate([v[rows:pair], v[pair + rows :]], 0)
                    send_a[out, into] = jnp.where(low, first, second).astype(bf16)
                    keep_a[out, into] = jnp.where(low, second, first)
                else:
                    first, second = v[:pair], v[pair:]
                    send_b[out, into] = jnp.where(high, first, second).astype(bf16)
                    keep_b[out, into] = jnp.where(high, second, first)


def times(one, two):
    return jnp.dot(one, two, preferred_element_type=f32)


def own_kernel(table_ref, shaped_ref, out_ref):
    out_ref[...] = times(table_ref[...], shaped_ref[...])


def other_kernel(table_ref, shaped_ref, own_ref, out_ref):
    out_ref[...] = (own_ref[...] + times(table_ref[...], shaped_ref[...])).astype(bf16)


def fields_kernel(block_rows, columns_ref, re_ref, im_ref, out_ref):
    rows, grid_size = out_ref.shape[0], columns_ref.shape[1]
    by_re, by_im = times(columns_ref[...], re_ref[...]), times(columns_ref[...], im_ref[...])
    if block_rows % 8 == 0:
        step, block = 2 * block_rows, block_rows
    else:
        step, block = rows, rows
    for at in range(0, rows, step):
        pieces = [[], []]
        for start in range(2 * at, 2 * (at + step), 2 * block):
            real, imag = slice(start, start + block), slice(start + block, start + 2 * block)
            pieces[0].append(by_re[real] - by_im[imag])
            pieces[1].append(by_im[real] + by_re[imag])
        for k, piece in enumerate(pieces):
            out = jnp.concatenate(piece, 0).astype(bf16)
            out_ref[pl.ds(at, step), pl.ds(k * grid_size, grid_size)] = out


def targets_kernel(targets_ref, re_ref, im_ref, out_ref):
    rows = targets_ref.shape[0] // 2
    real, imag = targets_ref[:rows], targets_ref[rows:]
    c_re, c_im = re_ref[...], im_ref[...]
    out_ref[:rows] = (times(real, c_re) + times(imag, c_im)).astype(bf16)
    out_ref[rows:] = (times(imag, c_re) - times(real, c_im)).astype(bf16)


def exactly(one, two, dims):
    return lax.dot_general(
        one, two, (dims, ((), ())), precision=lax.Precision.HIGHEST, preferred_element_type=f32
    )


def coupling_kernel(block_rows, by_xor, fields_ref, targets_ref, out_ref):
    modes = out_ref.shape[1]
    product = lax.dot_general(
        fields_ref[...], targets_ref[...], (((1,), (1,)), ((), ())), preferred_element_type=f32
    )
    left, right = product.shape
    row = lax.broadcasted_iota(jnp.int32, (left, right), 0) % block_rows
    col = lax.broadcasted_iota(jnp.int32, (left, right), 1) % block_rows
    product = jnp.where(row == col, product, 0.0)

    def groups(size):
        member = lax.broadcasted_iota(jnp.int32, (size // block_rows, size), 1) // block_rows
        group = lax.broadcasted_iota(jnp.int32, (size // block_rows, size), 0)
        return jnp.where(member == group, 1.0, 0.0).astype(f32)

    if block_rows % 8 == 0:
        product = jnp.sum(product.reshape(left // block_rows, block_rows, right), 1)
    else:
        product = exactly(groups(left), product, ((1,), (0,)))
    product = exactly(product, groups(right), ((1,), (1,)))
    by_re, by_im = product[:, :modes], product[:, modes:]
    mode = lax.broadcasted_iota(jnp.int32, (modes, 2 * modes), 0)
    if by_xor:
        mode = mode ^ lax.axis_index("modes")
        mode = mode % (modes // 2) * 2 + mode // (modes // 2)
    from_row = lax.broadcasted_iota(jnp.int32, (modes, 2 * modes), 1)
    real = jnp.where(from_row == 2 * mode, 1.0, 0.0).astype(f32)
    imag = jnp.where(from_row == 2 * mode + 1, 1.0, 0.0).astype(f32)
    inner = ((1,), (0,))
    out_ref[:modes] = exactly(real, by_re, inner) + exactly(imag, by_im, inner)
    out_ref[modes:] = exactly(imag, by_re, inner) - exactly(real, by_im, inner)


def kernel_call(kernel, shape, dtype, flops, operands, grant=12, **more):
    place = pl.BlockSpec(memory_space=pltpu.VMEM)
    several = isinstance(dtype, list)
    if several:
        out_shape = [jax.ShapeDtypeStruct(s, d) for s, d in zip(shape, dtype)]
    else:
        out_shape = jax.ShapeDtypeStruct(shape, dtype)
    specs = dict(in_specs=[place] * len(operands), out_specs=[place] * len(shape) if several else place)
    return pl.pallas_call(
        kernel,
        out_shape=out_shape,
        compiler_params=pltpu.CompilerParams(vmem_limit_bytes=grant << 20),
        cost_estimate=pl.CostEstimate(flops=flops, bytes_accessed=4 << 20, transcendentals=0),
        **(specs | more),
    )(*operands)


def local(forward, backward, targets):
    modes_here, local_rows, double_width = forward.shape
    grid_size = double_width // 2
    count = lax.axis_size("modes")
    mode_total = modes_here * count
    block_rows = local_rows // count
    digits = stages(count)
    sizes = [size for _, size in reversed(digits)]
    half = grid_size // 2
    matmul = 2 * local_rows * double_width * double_width

    c_re, c_im = propagator(grid_size)
    full_re, full_im = jnp.asarray(c_re, bf16), jnp.asarray(c_im, bf16)
    column_shape = (2 * local_rows, grid_size)
    seen = kernel_call(
        targets_kernel, column_shape, bf16, matmul, (targets.reshape(column_shape), full_re, full_im)
    )

    me = lax.axis_index("modes")
    owns = [me // stride % size for stride, size in digits]
    last = len(digits) - 1
    first = list(range(last))
    orders = [first, [1, 0] + first[2:]]
    kernel_first = block_rows % 8 == 0 and local_rows % (4 * block_rows) == 0
    if kernel_first:
        halves = kernel_call(
            lambda *refs: products_kernel(block_rows, *refs),
            [(local_rows // 2, grid_size)] * 4,
            [bf16, f32, bf16, f32],
            8 * local_rows * double_width,
            (forward[0], backward[0]),
            grant=12,
            in_specs=[pl.BlockSpec(memory_space=pltpu.HBM)] * 2,
            scratch_shapes=[pltpu.VMEM((local_rows, double_width), bf16)] * 2
            + [pltpu.SemaphoreType.DMA((2 * local_rows // (4 * block_rows),))],
        )
    else:
        product = product_of(forward[0], backward[0])
    kept = []
    for part, order in enumerate(orders):
        cols = slice(part * half, (part + 1) * half)
        axes = [last - d for d in range(len(digits))]
        if not kernel_first:
            partial = jnp.concatenate([p[:, cols] for p in product], -1)
            partial = partial.reshape(*sizes, block_rows, grid_size)
        for at, d in enumerate(order):
            stride, size = digits[d]
            left = sizes[: axes[d]] + sizes[axes[d] + 1 :] if at == 0 else None
            if at == 0 and kernel_first:
                send = [halves[2 * part].reshape(*left, block_rows, grid_size)]
                keep = halves[2 * part + 1].reshape(*left, block_rows, grid_size)
            else:
                send, keep = split_digit(partial, owns[d], size, axes[d])
            got = [exchange(v, (e + 1) * stride, count) for e, v in enumerate(send)]
            if at == 0 and part == 0:
                got, seen = lax.optimization_barrier((got, seen))
            partial = reduce_digit(keep, got)
            axes = [a - (a > axes[d]) for a in axes]
        kept.append(partial)
    stride, size = digits[last]
    send, keep = split_digit(jnp.concatenate(kept, -1), owns[last], size, 0)
    got = [exchange(v, (e + 1) * stride, count) for e, v in enumerate(send)]
    summed = reduce_digit(keep, got)
    parts = []
    for part in range(2):
        over_re = summed[:, part * grid_size : part * grid_size + half]
        over_im = summed[:, part * grid_size + half : (part + 1) * grid_size]
        scale = lax.rsqrt(over_re * over_re + over_im * over_im + mode_total)
        parts += [over_re * scale, over_im * scale]
    block = jnp.concatenate(parts, -1).astype(bf16)

    block = gather_digit(block, owns[last], stride, size, 0, count)
    planes = []
    for part, order in enumerate(orders):
        piece = block[..., part * grid_size : (part + 1) * grid_size]
        done = [last]
        for d in reversed(order):
            axis = sum(1 for other in done if other > d)
            piece = gather_digit(piece, owns[d], *digits[d], axis, count)
            done.append(d)
        planes.append(piece.reshape(local_rows, grid_size))
    plane_re = jnp.concatenate([p[:, :half] for p in planes], -1)
    plane_im = jnp.concatenate([p[:, half:] for p in planes], -1)
    phase_plane = jnp.concatenate([plane_re, plane_im], -1)

    fore = forward[0].astype(f32)
    fore_re, fore_im = fore[:, :grid_size], fore[:, grid_size:]
    plane_re, plane_im = plane_re.astype(f32), plane_im.astype(f32)
    shaped = jnp.concatenate(
        [fore_re * plane_re - fore_im * plane_im, fore_re * plane_im + fore_im * plane_re], 0
    ).astype(bf16)
    other = lax.ppermute(shaped, "rows", [(0, 1), (1, 0)])

    owners = count if block_rows % 8 == 0 else 1
    order = np.arange(local_rows).reshape(owners, -1)

    def table(cols):
        real, imag = c_re[:local_rows, cols], c_im[:local_rows, cols]
        rows = np.stack([np.concatenate([real, -imag], 1)[order], np.concatenate([imag, real], 1)[order]], 1)
        return jnp.asarray(rows.reshape(2 * local_rows, -1), bf16)

    columns = kernel_call(
        own_kernel, column_shape, f32, matmul // 2, (table(slice(0, local_rows)), shaped)
    )
    columns, other, phase_plane = lax.optimization_barrier((columns, other, phase_plane))
    columns = kernel_call(
        other_kernel, column_shape, bf16, matmul // 2, (table(slice(local_rows, None)), other, columns)
    )
    blocks = columns.reshape(owners, 2, -1, block_rows, grid_size).transpose(0, 2, 1, 3, 4)
    blocks = blocks.reshape(count, 2 * block_rows, grid_size)
    if count <= 16:
        turns = [at // 2 + count // 2 * (at % 2) for at in range(count)]
        pixels = [pick(blocks, me, 0)]
        for at, e in enumerate(turns[1:], 1):
            block = pick(blocks, me ^ e, 0)
            if at > LANES:
                block, pixels[at - LANES] = lax.optimization_barrier((block, pixels[at - LANES]))
            pixels.append(exchange(block, e, count))
    else:
        pixels = (lax.all_to_all(blocks, "modes", 0, 0, tiled=True),)

    term = kernel_call(
        lambda *refs: coupling_kernel(block_rows, len(pixels) > 1, *refs),
        (2 * mode_total, mode_total),
        f32,
        matmul,
        (jnp.concatenate(pixels, 0).reshape(column_shape), seen),
    )
    columns, term = lax.optimization_barrier((columns, term))
    output_fields = kernel_call(
        lambda *refs: fields_kernel(block_rows, *refs),
        (local_rows, double_width),
        bf16,
        matmul,
        (columns, full_re, full_im),
    )
    pieces = lax.all_to_all(term, ("modes", "rows"), 0, 0, tiled=True)
    coupling = jnp.sum(pieces, 0, keepdims=True)
    return (phase_plane, output_fields[None], coupling)


def solution(mesh):
    return jax.shard_map(
        local,
        mesh=mesh,
        in_specs=(
            P("modes", "rows", None),
            P("modes", "rows", None),
            P(None, None, ("rows", "modes"), None),
        ),
        out_specs=(P("rows", None), P("modes", "rows", None), P(("modes", "rows"), None)),
        check_vma=False,
    )
```

```python
import numpy as np

import jax
import jax.numpy as jnp
from jax import lax
from jax.experimental import pallas as pl
from jax.experimental.pallas import tpu as pltpu
from jax.sharding import PartitionSpec as P

bf16 = jnp.bfloat16
f32 = jnp.float32
LANES = 5
LATE = 4


def propagator(grid_size):
    index = np.arange(grid_size)
    centred = (index + grid_size // 2) % grid_size - grid_size // 2
    squared = centred * centred % (4 * grid_size)
    column = np.fft.ifft(np.exp(-2j * np.pi * squared / (4 * grid_size)))
    matrix = column[(index[:, None] - index[None, :]) % grid_size]
    return matrix.real, matrix.imag


def stages(count):
    digits, stride = [], 1
    while count // stride > 4:
        digits.append((stride, 2))
        stride *= 2
    digits.append((stride, count // stride))
    return digits


def exchange(values, offset, count):
    return lax.ppermute(values, "modes", [(i, i ^ offset) for i in range(count)])


def pick(values, index, axis):
    return lax.dynamic_index_in_dim(values, index, axis, keepdims=False)


def reduce_digit(keep, got):
    for g in got:
        keep = keep + g.astype(f32)
    return keep


def gather_digit(block, own, stride, size, axis, count):
    got = [block] + [exchange(block, e * stride, count) for e in range(1, size)]
    stacked = jnp.stack(got, axis)
    if size == 2:
        return jnp.where(own == 0, stacked, jnp.flip(stacked, axis))
    return jnp.stack([pick(stacked, own ^ at, axis) for at in range(size)], axis)


def split_digit(partial, own, size, axis):
    send = [pick(partial, own ^ e, axis).astype(bf16) for e in range(1, size)]
    return send, pick(partial, own, axis)


def product_of(fore, back):
    half = fore.shape[-1] // 2
    fore, back = fore.astype(f32), back.astype(f32)
    fore_re, fore_im = fore[..., :half], fore[..., half:]
    back_re, back_im = back[..., :half], back[..., half:]
    return back_re * fore_re + back_im * fore_im, back_re * fore_im - back_im * fore_re


def products_kernel(rows, fore_hbm, back_hbm, send_a, keep_a, send_b, keep_b, fore_ref, back_ref, sems):
    me = lax.axis_index("modes")
    low, high = me % 2 == 1, me // 2 % 2 == 1
    grid_size = fore_ref.shape[1] // 2
    half = grid_size // 2
    pair = 2 * rows
    groups = fore_ref.shape[0] // (4 * rows)
    copies = []
    for group in range(groups):
        at = pl.ds(group * 4 * rows, 4 * rows)
        for k, (hbm, ref) in enumerate(((fore_hbm, fore_ref), (back_hbm, back_ref))):
            copies.append(pltpu.make_async_copy(hbm.at[at], ref.at[at], sems.at[2 * group + k]))
    for copy in copies:
        copy.start()
    for group in range(groups):
        copies[2 * group].wait()
        copies[2 * group + 1].wait()
        at = pl.ds(group * 4 * rows, 4 * rows)
        out = pl.ds(group * pair, pair)
        for part in range(2):
            cols = [pl.ds(part * half, half), pl.ds(grid_size + part * half, half)]
            fore_re, fore_im = [fore_ref[at, c].astype(f32) for c in cols]
            back_re, back_im = [back_ref[at, c].astype(f32) for c in cols]
            values = (back_re * fore_re + back_im * fore_im, back_re * fore_im - back_im * fore_re)
            for k, v in enumerate(values):
                into = pl.ds(k * half, half)
                if part == 0:
                    first = jnp.concatenate([v[:rows], v[pair : pair + rows]], 0)
                    second = jnp.concatenate([v[rows:pair], v[pair + rows :]], 0)
                    send_a[out, into] = jnp.where(low, first, second).astype(bf16)
                    keep_a[out, into] = jnp.where(low, second, first)
                else:
                    first, second = v[:pair], v[pair:]
                    send_b[out, into] = jnp.where(high, first, second).astype(bf16)
                    keep_b[out, into] = jnp.where(high, second, first)


def times(one, two):
    return jnp.dot(one, two, preferred_element_type=f32)


def own_kernel(table_ref, shaped_ref, out_ref):
    out_ref[...] = times(table_ref[...], shaped_ref[...])


def other_kernel(table_ref, shaped_ref, own_ref, out_ref):
    out_ref[...] = (own_ref[...] + times(table_ref[...], shaped_ref[...])).astype(bf16)


def fields_kernel(block_rows, columns_ref, re_ref, im_ref, out_ref):
    rows, grid_size = out_ref.shape[0], columns_ref.shape[1]
    by_re, by_im = times(columns_ref[...], re_ref[...]), times(columns_ref[...], im_ref[...])
    if block_rows % 8 == 0:
        step, block = 2 * block_rows, block_rows
    else:
        step, block = rows, rows
    for at in range(0, rows, step):
        pieces = [[], []]
        for start in range(2 * at, 2 * (at + step), 2 * block):
            real, imag = slice(start, start + block), slice(start + block, start + 2 * block)
            pieces[0].append(by_re[real] - by_im[imag])
            pieces[1].append(by_im[real] + by_re[imag])
        for k, piece in enumerate(pieces):
            out = jnp.concatenate(piece, 0).astype(bf16)
            out_ref[pl.ds(at, step), pl.ds(k * grid_size, grid_size)] = out


def targets_kernel(targets_ref, re_ref, im_ref, out_ref):
    rows = targets_ref.shape[0] // 2
    real, imag = targets_ref[:rows], targets_ref[rows:]
    c_re, c_im = re_ref[...], im_ref[...]
    out_ref[:rows] = (times(real, c_re) + times(imag, c_im)).astype(bf16)
    out_ref[rows:] = (times(imag, c_re) - times(real, c_im)).astype(bf16)


def exactly(one, two, dims):
    return lax.dot_general(
        one, two, (dims, ((), ())), precision=lax.Precision.HIGHEST, preferred_element_type=f32
    )


def coupling_kernel(block_rows, by_xor, first, fields_ref, targets_ref, *rest):
    out_ref = rest[-1]
    modes = out_ref.shape[1]
    product = lax.dot_general(
        fields_ref[...], targets_ref[...], (((1,), (1,)), ((), ())), preferred_element_type=f32
    )
    left, right = product.shape
    row = lax.broadcasted_iota(jnp.int32, (left, right), 0) % block_rows
    col = lax.broadcasted_iota(jnp.int32, (left, right), 1) % block_rows
    product = jnp.where(row == col, product, 0.0)

    def groups(size):
        member = lax.broadcasted_iota(jnp.int32, (size // block_rows, size), 1) // block_rows
        group = lax.broadcasted_iota(jnp.int32, (size // block_rows, size), 0)
        return jnp.where(member == group, 1.0, 0.0).astype(f32)

    if block_rows % 8 == 0:
        product = jnp.sum(product.reshape(left // block_rows, block_rows, right), 1)
    else:
        product = exactly(groups(left), product, ((1,), (0,)))
    product = exactly(product, groups(right), ((1,), (1,)))
    by_re, by_im = product[:, :modes], product[:, modes:]
    sources = left // block_rows
    mode = lax.broadcasted_iota(jnp.int32, (modes, sources), 0)
    if by_xor:
        mode = mode ^ lax.axis_index("modes")
        mode = mode % (modes // 2) * 2 + mode // (modes // 2)
    from_row = lax.broadcasted_iota(jnp.int32, (modes, sources), 1) + 2 * first
    real = jnp.where(from_row == 2 * mode, 1.0, 0.0).astype(f32)
    imag = jnp.where(from_row == 2 * mode + 1, 1.0, 0.0).astype(f32)
    inner = ((1,), (0,))
    total_re = exactly(real, by_re, inner) + exactly(imag, by_im, inner)
    total_im = exactly(imag, by_re, inner) - exactly(real, by_im, inner)
    if len(rest) > 1:
        total_re, total_im = total_re + rest[0][:modes], total_im + rest[0][modes:]
    out_ref[:modes] = total_re
    out_ref[modes:] = total_im


def kernel_call(kernel, shape, dtype, flops, operands, grant=12, **more):
    place = pl.BlockSpec(memory_space=pltpu.VMEM)
    several = isinstance(dtype, list)
    if several:
        out_shape = [jax.ShapeDtypeStruct(s, d) for s, d in zip(shape, dtype)]
    else:
        out_shape = jax.ShapeDtypeStruct(shape, dtype)
    specs = dict(in_specs=[place] * len(operands), out_specs=[place] * len(shape) if several else place)
    return pl.pallas_call(
        kernel,
        out_shape=out_shape,
        compiler_params=pltpu.CompilerParams(vmem_limit_bytes=grant << 20),
        cost_estimate=pl.CostEstimate(flops=flops, bytes_accessed=4 << 20, transcendentals=0),
        **(specs | more),
    )(*operands)


def local(forward, backward, targets):
    modes_here, local_rows, double_width = forward.shape
    grid_size = double_width // 2
    count = lax.axis_size("modes")
    mode_total = modes_here * count
    block_rows = local_rows // count
    digits = stages(count)
    sizes = [size for _, size in reversed(digits)]
    half = grid_size // 2
    matmul = 2 * local_rows * double_width * double_width

    me = lax.axis_index("modes")
    owns = [me // stride % size for stride, size in digits]
    last = len(digits) - 1
    first = list(range(last))
    orders = [first, [1, 0] + first[2:]]
    kernel_first = block_rows % 8 == 0 and local_rows % (4 * block_rows) == 0
    if kernel_first:
        halves = kernel_call(
            lambda *refs: products_kernel(block_rows, *refs),
            [(local_rows // 2, grid_size)] * 4,
            [bf16, f32, bf16, f32],
            8 * local_rows * double_width,
            (forward[0], backward[0]),
            grant=52,
            in_specs=[pl.BlockSpec(memory_space=pltpu.HBM)] * 2,
            scratch_shapes=[pltpu.VMEM((local_rows, double_width), bf16)] * 2
            + [pltpu.SemaphoreType.DMA((2 * local_rows // (4 * block_rows),))],
        )
    else:
        product = product_of(forward[0], backward[0])
    kept = []
    for part, order in enumerate(orders):
        cols = slice(part * half, (part + 1) * half)
        axes = [last - d for d in range(len(digits))]
        if not kernel_first:
            partial = jnp.concatenate([p[:, cols] for p in product], -1)
            partial = partial.reshape(*sizes, block_rows, grid_size)
        for at, d in enumerate(order):
            stride, size = digits[d]
            left = sizes[: axes[d]] + sizes[axes[d] + 1 :] if at == 0 else None
            if at == 0 and kernel_first:
                send = [halves[2 * part].reshape(*left, block_rows, grid_size)]
                keep = halves[2 * part + 1].reshape(*left, block_rows, grid_size)
            else:
                send, keep = split_digit(partial, owns[d], size, axes[d])
            got = [exchange(v, (e + 1) * stride, count) for e, v in enumerate(send)]
            partial = reduce_digit(keep, got)
            axes = [a - (a > axes[d]) for a in axes]
        kept.append(partial)
    stride, size = digits[last]
    send, keep = split_digit(jnp.concatenate(kept, -1), owns[last], size, 0)
    got = [exchange(v, (e + 1) * stride, count) for e, v in enumerate(send)]
    summed = reduce_digit(keep, got)
    parts = []
    for part in range(2):
        over_re = summed[:, part * grid_size : part * grid_size + half]
        over_im = summed[:, part * grid_size + half : (part + 1) * grid_size]
        scale = lax.rsqrt(over_re * over_re + over_im * over_im + mode_total)
        parts += [over_re * scale, over_im * scale]
    block = jnp.concatenate(parts, -1).astype(bf16)

    block = gather_digit(block, owns[last], stride, size, 0, count)
    planes = []
    for part, order in enumerate(orders):
        piece = block[..., part * grid_size : (part + 1) * grid_size]
        done = [last]
        for d in reversed(order):
            axis = sum(1 for other in done if other > d)
            piece = gather_digit(piece, owns[d], *digits[d], axis, count)
            done.append(d)
        planes.append(piece.reshape(local_rows, grid_size))
    plane_re = jnp.concatenate([p[:, :half] for p in planes], -1)
    plane_im = jnp.concatenate([p[:, half:] for p in planes], -1)
    phase_plane = jnp.concatenate([plane_re, plane_im], -1)

    fore = forward[0].astype(f32)
    fore_re, fore_im = fore[:, :grid_size], fore[:, grid_size:]
    plane_re, plane_im = plane_re.astype(f32), plane_im.astype(f32)
    shaped = jnp.concatenate(
        [fore_re * plane_re - fore_im * plane_im, fore_re * plane_im + fore_im * plane_re], 0
    ).astype(bf16)
    other = lax.ppermute(shaped, "rows", [(0, 1), (1, 0)])

    c_re, c_im = propagator(grid_size)
    full_re, full_im = jnp.asarray(c_re, bf16), jnp.asarray(c_im, bf16)
    owners = count if block_rows % 8 == 0 else 1
    order = np.arange(local_rows).reshape(owners, -1)

    def table(cols):
        real, imag = c_re[:local_rows, cols], c_im[:local_rows, cols]
        rows = np.stack([np.concatenate([real, -imag], 1)[order], np.concatenate([imag, real], 1)[order]], 1)
        return jnp.asarray(rows.reshape(2 * local_rows, -1), bf16)

    column_shape = (2 * local_rows, grid_size)
    columns = kernel_call(
        own_kernel, column_shape, f32, matmul // 2, (table(slice(0, local_rows)), shaped)
    )
    columns, other = lax.optimization_barrier((columns, other))
    columns = kernel_call(
        other_kernel, column_shape, bf16, matmul // 2, (table(slice(local_rows, None)), other, columns)
    )
    blocks = columns.reshape(owners, 2, -1, block_rows, grid_size).transpose(0, 2, 1, 3, 4)
    blocks = blocks.reshape(count, 2 * block_rows, grid_size)
    if count <= 16:
        turns = [at // 2 + count // 2 * (at % 2) for at in range(count)]
        pixels = [pick(blocks, me, 0)]
        for at, e in enumerate(turns[1:], 1):
            block = pick(blocks, me ^ e, 0)
            if at > LANES:
                block, pixels[at - LANES] = lax.optimization_barrier((block, pixels[at - LANES]))
            pixels.append(exchange(block, e, count))
    else:
        pixels = [lax.all_to_all(blocks, "modes", 0, 0, tiled=True)]

    output_fields = kernel_call(
        lambda *refs: fields_kernel(block_rows, *refs),
        (local_rows, double_width),
        bf16,
        matmul,
        (columns, full_re, full_im),
    )
    targets, output_fields = lax.optimization_barrier((targets, output_fields))
    seen = kernel_call(
        targets_kernel, column_shape, bf16, matmul, (targets.reshape(column_shape), full_re, full_im)
    )
    cut = len(pixels) - LATE if len(pixels) > LATE else len(pixels)
    seen, output_fields = lax.optimization_barrier((seen, output_fields))
    term, at = None, 0
    for group in (pixels[:cut], pixels[cut:]):
        if group:
            rows = jnp.concatenate(group, 0).reshape(-1, grid_size)
            term = kernel_call(
                lambda *refs: coupling_kernel(block_rows, len(pixels) > 1, at, *refs),
                (2 * mode_total, mode_total),
                f32,
                2 * rows.shape[0] * 2 * local_rows * grid_size,
                (rows, seen) if term is None else (rows, seen, term),
            )
            at += len(group)
    pieces = lax.all_to_all(term, ("modes", "rows"), 0, 0, tiled=True)
    coupling = jnp.sum(pieces, 0, keepdims=True)
    return (phase_plane, output_fields[None], coupling)


def solution(mesh):
    return jax.shard_map(
        local,
        mesh=mesh,
        in_specs=(
            P("modes", "rows", None),
            P("modes", "rows", None),
            P(None, None, ("rows", "modes"), None),
        ),
        out_specs=(P("rows", None), P("modes", "rows", None), P(("modes", "rows"), None)),
        check_vma=False,
    )
```

```python
import numpy as np

import jax
import jax.numpy as jnp
from jax import lax
from jax.experimental import pallas as pl
from jax.experimental.pallas import tpu as pltpu
from jax.sharding import PartitionSpec as P

bf16 = jnp.bfloat16
f32 = jnp.float32
LANES = 5


def propagator(grid_size):
    index = np.arange(grid_size)
    centred = (index + grid_size // 2) % grid_size - grid_size // 2
    squared = centred * centred % (4 * grid_size)
    column = np.fft.ifft(np.exp(-2j * np.pi * squared / (4 * grid_size)))
    matrix = column[(index[:, None] - index[None, :]) % grid_size]
    return matrix.real, matrix.imag


def stages(count):
    digits, stride = [], 1
    while count // stride > 4:
        digits.append((stride, 2))
        stride *= 2
    digits.append((stride, count // stride))
    return digits


def exchange(values, offset, count):
    return lax.ppermute(values, "modes", [(i, i ^ offset) for i in range(count)])


def pick(values, index, axis):
    return lax.dynamic_index_in_dim(values, index, axis, keepdims=False)


def reduce_digit(keep, got):
    for g in got:
        keep = keep + g.astype(f32)
    return keep


def gather_digit(block, own, stride, size, axis, count):
    got = [block] + [exchange(block, e * stride, count) for e in range(1, size)]
    stacked = jnp.stack(got, axis)
    if size == 2:
        return jnp.where(own == 0, stacked, jnp.flip(stacked, axis))
    return jnp.stack([pick(stacked, own ^ at, axis) for at in range(size)], axis)


def split_digit(partial, own, size, axis):
    send = [pick(partial, own ^ e, axis).astype(bf16) for e in range(1, size)]
    return send, pick(partial, own, axis)


def product_of(fore, back):
    half = fore.shape[-1] // 2
    fore, back = fore.astype(f32), back.astype(f32)
    fore_re, fore_im = fore[..., :half], fore[..., half:]
    back_re, back_im = back[..., :half], back[..., half:]
    return back_re * fore_re + back_im * fore_im, back_re * fore_im - back_im * fore_re


def products_kernel(rows, fore_hbm, back_hbm, send_a, keep_a, send_b, keep_b, fore_ref, back_ref, sems):
    me = lax.axis_index("modes")
    low, high = me % 2 == 1, me // 2 % 2 == 1
    grid_size = fore_ref.shape[1] // 2
    half = grid_size // 2
    pair = 2 * rows
    groups = fore_ref.shape[0] // (4 * rows)
    copies = []
    for group in range(groups):
        at = pl.ds(group * 4 * rows, 4 * rows)
        for k, (hbm, ref) in enumerate(((fore_hbm, fore_ref), (back_hbm, back_ref))):
            copies.append(pltpu.make_async_copy(hbm.at[at], ref.at[at], sems.at[2 * group + k]))
    for copy in copies:
        copy.start()
    for group in range(groups):
        copies[2 * group].wait()
        copies[2 * group + 1].wait()
        at = pl.ds(group * 4 * rows, 4 * rows)
        out = pl.ds(group * pair, pair)
        for part in range(2):
            cols = [pl.ds(part * half, half), pl.ds(grid_size + part * half, half)]
            fore_re, fore_im = [fore_ref[at, c].astype(f32) for c in cols]
            back_re, back_im = [back_ref[at, c].astype(f32) for c in cols]
            values = (back_re * fore_re + back_im * fore_im, back_re * fore_im - back_im * fore_re)
            for k, v in enumerate(values):
                into = pl.ds(k * half, half)
                if part == 0:
                    first = jnp.concatenate([v[:rows], v[pair : pair + rows]], 0)
                    second = jnp.concatenate([v[rows:pair], v[pair + rows :]], 0)
                    send_a[out, into] = jnp.where(low, first, second).astype(bf16)
                    keep_a[out, into] = jnp.where(low, second, first)
                else:
                    first, second = v[:pair], v[pair:]
                    send_b[out, into] = jnp.where(high, first, second).astype(bf16)
                    keep_b[out, into] = jnp.where(high, second, first)


def times(one, two):
    return jnp.dot(one, two, preferred_element_type=f32)


def own_kernel(table_ref, shaped_ref, out_ref):
    out_ref[...] = times(table_ref[...], shaped_ref[...])


def other_kernel(table_ref, shaped_ref, own_ref, out_ref):
    out_ref[...] = (own_ref[...] + times(table_ref[...], shaped_ref[...])).astype(bf16)


def fields_kernel(block_rows, columns_ref, re_ref, im_ref, out_ref):
    rows, grid_size = out_ref.shape[0], columns_ref.shape[1]
    by_re, by_im = times(columns_ref[...], re_ref[...]), times(columns_ref[...], im_ref[...])
    if block_rows % 8 == 0:
        step, block = 2 * block_rows, block_rows
    else:
        step, block = rows, rows
    for at in range(0, rows, step):
        pieces = [[], []]
        for start in range(2 * at, 2 * (at + step), 2 * block):
            real, imag = slice(start, start + block), slice(start + block, start + 2 * block)
            pieces[0].append(by_re[real] - by_im[imag])
            pieces[1].append(by_im[real] + by_re[imag])
        for k, piece in enumerate(pieces):
            out = jnp.concatenate(piece, 0).astype(bf16)
            out_ref[pl.ds(at, step), pl.ds(k * grid_size, grid_size)] = out


def targets_kernel(targets_ref, re_ref, im_ref, out_ref):
    rows = targets_ref.shape[0] // 2
    real, imag = targets_ref[:rows], targets_ref[rows:]
    c_re, c_im = re_ref[...], im_ref[...]
    out_ref[:rows] = (times(real, c_re) + times(imag, c_im)).astype(bf16)
    out_ref[rows:] = (times(imag, c_re) - times(real, c_im)).astype(bf16)


def exactly(one, two, dims):
    return lax.dot_general(
        one, two, (dims, ((), ())), precision=lax.Precision.HIGHEST, preferred_element_type=f32
    )


def coupling_kernel(block_rows, by_xor, fields_ref, targets_ref, out_ref, held):
    modes = out_ref.shape[1]
    product = lax.dot_general(
        fields_ref[...], targets_ref[...], (((1,), (1,)), ((), ())), preferred_element_type=f32
    )
    left, right = product.shape
    row = lax.broadcasted_iota(jnp.int32, (left, right), 0) % block_rows
    col = lax.broadcasted_iota(jnp.int32, (left, right), 1) % block_rows
    product = jnp.where(row == col, product, 0.0)

    def groups(size):
        member = lax.broadcasted_iota(jnp.int32, (size // block_rows, size), 1) // block_rows
        group = lax.broadcasted_iota(jnp.int32, (size // block_rows, size), 0)
        return jnp.where(member == group, 1.0, 0.0).astype(f32)

    if block_rows % 8 == 0:
        product = jnp.sum(product.reshape(left // block_rows, block_rows, right), 1)
    else:
        product = exactly(groups(left), product, ((1,), (0,)))
    product = product.reshape(modes, 2, right)
    real, imag = product[:, 0], product[:, 1]
    right = right // 2
    both = jnp.concatenate(
        [real[:, :right] + imag[:, right:], imag[:, :right] - real[:, right:]], 0
    )
    held[...] = exactly(both, groups(right), ((1,), (1,)))
    if by_xor:
        me, there = lax.axis_index("modes"), modes // 2
        for mode in range(modes):
            e = mode ^ me
            at = e % there * 2 + e // there
            out_ref[pl.ds(mode, 1)] = held[pl.ds(at, 1)]
            out_ref[pl.ds(modes + mode, 1)] = held[pl.ds(modes + at, 1)]
    else:
        out_ref[...] = held[...]


def kernel_call(kernel, shape, dtype, flops, operands, grant=12, **more):
    place = pl.BlockSpec(memory_space=pltpu.VMEM)
    several = isinstance(dtype, list)
    if several:
        out_shape = [jax.ShapeDtypeStruct(s, d) for s, d in zip(shape, dtype)]
    else:
        out_shape = jax.ShapeDtypeStruct(shape, dtype)
    specs = dict(in_specs=[place] * len(operands), out_specs=[place] * len(shape) if several else place)
    return pl.pallas_call(
        kernel,
        out_shape=out_shape,
        compiler_params=pltpu.CompilerParams(vmem_limit_bytes=grant << 20),
        cost_estimate=pl.CostEstimate(flops=flops, bytes_accessed=4 << 20, transcendentals=0),
        **(specs | more),
    )(*operands)


def local(forward, backward, targets):
    modes_here, local_rows, double_width = forward.shape
    grid_size = double_width // 2
    count = lax.axis_size("modes")
    mode_total = modes_here * count
    block_rows = local_rows // count
    digits = stages(count)
    sizes = [size for _, size in reversed(digits)]
    half = grid_size // 2
    matmul = 2 * local_rows * double_width * double_width

    me = lax.axis_index("modes")
    owns = [me // stride % size for stride, size in digits]
    last = len(digits) - 1
    first = list(range(last))
    orders = [first, [1, 0] + first[2:]]
    kernel_first = block_rows % 8 == 0 and local_rows % (4 * block_rows) == 0
    if kernel_first:
        halves = kernel_call(
            lambda *refs: products_kernel(block_rows, *refs),
            [(local_rows // 2, grid_size)] * 4,
            [bf16, f32, bf16, f32],
            8 * local_rows * double_width,
            (forward[0], backward[0]),
            grant=52,
            in_specs=[pl.BlockSpec(memory_space=pltpu.HBM)] * 2,
            scratch_shapes=[pltpu.VMEM((local_rows, double_width), bf16)] * 2
            + [pltpu.SemaphoreType.DMA((2 * local_rows // (4 * block_rows),))],
        )
    else:
        product = product_of(forward[0], backward[0])
    kept = []
    for part, order in enumerate(orders):
        cols = slice(part * half, (part + 1) * half)
        axes = [last - d for d in range(len(digits))]
        if not kernel_first:
            partial = jnp.concatenate([p[:, cols] for p in product], -1)
            partial = partial.reshape(*sizes, block_rows, grid_size)
        for at, d in enumerate(order):
            stride, size = digits[d]
            left = sizes[: axes[d]] + sizes[axes[d] + 1 :] if at == 0 else None
            if at == 0 and kernel_first:
                send = [halves[2 * part].reshape(*left, block_rows, grid_size)]
                keep = halves[2 * part + 1].reshape(*left, block_rows, grid_size)
            else:
                send, keep = split_digit(partial, owns[d], size, axes[d])
            got = [exchange(v, (e + 1) * stride, count) for e, v in enumerate(send)]
            partial = reduce_digit(keep, got)
            axes = [a - (a > axes[d]) for a in axes]
        kept.append(partial)
    stride, size = digits[last]
    send, keep = split_digit(jnp.concatenate(kept, -1), owns[last], size, 0)
    got = [exchange(v, (e + 1) * stride, count) for e, v in enumerate(send)]
    summed = reduce_digit(keep, got)
    parts = []
    for part in range(2):
        over_re = summed[:, part * grid_size : part * grid_size + half]
        over_im = summed[:, part * grid_size + half : (part + 1) * grid_size]
        scale = lax.rsqrt(over_re * over_re + over_im * over_im + mode_total)
        parts += [over_re * scale, over_im * scale]
    block = jnp.concatenate(parts, -1).astype(bf16)

    block = gather_digit(block, owns[last], stride, size, 0, count)
    planes = []
    for part, order in enumerate(orders):
        piece = block[..., part * grid_size : (part + 1) * grid_size]
        done = [last]
        for d in reversed(order):
            axis = sum(1 for other in done if other > d)
            piece = gather_digit(piece, owns[d], *digits[d], axis, count)
            done.append(d)
        planes.append(piece.reshape(local_rows, grid_size))
    plane_re = jnp.concatenate([p[:, :half] for p in planes], -1)
    plane_im = jnp.concatenate([p[:, half:] for p in planes], -1)
    phase_plane = jnp.concatenate([plane_re, plane_im], -1)

    fore = forward[0].astype(f32)
    fore_re, fore_im = fore[:, :grid_size], fore[:, grid_size:]
    plane_re, plane_im = plane_re.astype(f32), plane_im.astype(f32)
    shaped = jnp.concatenate(
        [fore_re * plane_re - fore_im * plane_im, fore_re * plane_im + fore_im * plane_re], 0
    ).astype(bf16)
    other = lax.ppermute(shaped, "rows", [(0, 1), (1, 0)])

    c_re, c_im = propagator(grid_size)
    full_re, full_im = jnp.asarray(c_re, bf16), jnp.asarray(c_im, bf16)
    owners = count if block_rows % 8 == 0 else 1
    order = np.arange(local_rows).reshape(owners, -1)

    def table(cols):
        real, imag = c_re[:local_rows, cols], c_im[:local_rows, cols]
        rows = np.stack([np.concatenate([real, -imag], 1)[order], np.concatenate([imag, real], 1)[order]], 1)
        return jnp.asarray(rows.reshape(2 * local_rows, -1), bf16)

    column_shape = (2 * local_rows, grid_size)
    columns = kernel_call(
        own_kernel, column_shape, f32, matmul // 2, (table(slice(0, local_rows)), shaped)
    )
    columns, other = lax.optimization_barrier((columns, other))
    columns = kernel_call(
        other_kernel, column_shape, bf16, matmul // 2, (table(slice(local_rows, None)), other, columns)
    )
    blocks = columns.reshape(owners, 2, -1, block_rows, grid_size).transpose(0, 2, 1, 3, 4)
    blocks = blocks.reshape(count, 2 * block_rows, grid_size)
    if count <= 16:
        turns = [at // 2 + count // 2 * (at % 2) for at in range(count)]
        pixels = [pick(blocks, me, 0)]
        for at, e in enumerate(turns[1:], 1):
            block = pick(blocks, me ^ e, 0)
            if at > LANES:
                block, pixels[at - LANES] = lax.optimization_barrier((block, pixels[at - LANES]))
            pixels.append(exchange(block, e, count))
    else:
        pixels = [lax.all_to_all(blocks, "modes", 0, 0, tiled=True)]

    if len(pixels) > 1:
        targets, pixels[1] = lax.optimization_barrier((targets, pixels[1]))
    seen = kernel_call(
        targets_kernel, column_shape, bf16, matmul, (targets.reshape(column_shape), full_re, full_im)
    )
    rows = jnp.concatenate(pixels, 0).reshape(column_shape)
    term = kernel_call(
        lambda *refs: coupling_kernel(block_rows, len(pixels) > 1, *refs),
        (2 * mode_total, mode_total),
        f32,
        matmul,
        (rows, seen),
        scratch_shapes=[pltpu.VMEM((2 * mode_total, mode_total), f32)],
    )
    columns, term = lax.optimization_barrier((columns, term))
    output_fields = kernel_call(
        lambda *refs: fields_kernel(block_rows, *refs),
        (local_rows, double_width),
        bf16,
        matmul,
        (columns, full_re, full_im),
    )
    pieces = lax.all_to_all(term, ("modes", "rows"), 0, 0, tiled=True)
    coupling = jnp.sum(pieces, 0, keepdims=True)
    return (phase_plane, output_fields[None], coupling)


def solution(mesh):
    return jax.shard_map(
        local,
        mesh=mesh,
        in_specs=(
            P("modes", "rows", None),
            P("modes", "rows", None),
            P(None, None, ("rows", "modes"), None),
        ),
        out_specs=(P("rows", None), P("modes", "rows", None), P(("modes", "rows"), None)),
        check_vma=False,
    )
```

```python
import numpy as np

import jax
import jax.numpy as jnp
from jax import lax
from jax.experimental import pallas as pl
from jax.experimental.pallas import tpu as pltpu
from jax.sharding import PartitionSpec as P

bf16 = jnp.bfloat16
f32 = jnp.float32
LANES = 5


def propagator(grid_size):
    index = np.arange(grid_size)
    centred = (index + grid_size // 2) % grid_size - grid_size // 2
    squared = centred * centred % (4 * grid_size)
    column = np.fft.ifft(np.exp(-2j * np.pi * squared / (4 * grid_size)))
    matrix = column[(index[:, None] - index[None, :]) % grid_size]
    return matrix.real, matrix.imag


def stages(count):
    digits, stride = [], 1
    while count // stride > 4:
        digits.append((stride, 2))
        stride *= 2
    digits.append((stride, count // stride))
    return digits


def turns(count):
    far, near = list(range(count // 2, count)), list(range(1, count // 2))
    taken = [0]
    while far or near:
        some = far[:3] + near[: LANES - len(far[:3])]
        far, near = far[3:], near[LANES - len(far[:3]) :]
        taken += some[::-1]
    return taken


def exchange(values, offset, count):
    return lax.ppermute(values, "modes", [(i, i ^ offset) for i in range(count)])


def pick(values, index, axis):
    return lax.dynamic_index_in_dim(values, index, axis, keepdims=False)


def reduce_digit(keep, got):
    for g in got:
        keep = keep + g.astype(f32)
    return keep


def gather_digit(block, own, stride, size, axis, count):
    got = [block] + [exchange(block, e * stride, count) for e in range(1, size)]
    stacked = jnp.stack(got, axis)
    if size == 2:
        return jnp.where(own == 0, stacked, jnp.flip(stacked, axis))
    return jnp.stack([pick(stacked, own ^ at, axis) for at in range(size)], axis)


def split_digit(partial, own, size, axis):
    send = [pick(partial, own ^ e, axis).astype(bf16) for e in range(1, size)]
    return send, pick(partial, own, axis)


def product_of(fore, back):
    half = fore.shape[-1] // 2
    fore, back = fore.astype(f32), back.astype(f32)
    fore_re, fore_im = fore[..., :half], fore[..., half:]
    back_re, back_im = back[..., :half], back[..., half:]
    return back_re * fore_re + back_im * fore_im, back_re * fore_im - back_im * fore_re


def products_kernel(rows, fore_hbm, back_hbm, send_a, keep_a, send_b, keep_b, fore_ref, back_ref, sems):
    me = lax.axis_index("modes")
    low, high = me % 2 == 1, me // 2 % 2 == 1
    grid_size = fore_ref.shape[1] // 2
    half = grid_size // 2
    pair = 2 * rows
    groups = fore_ref.shape[0] // (4 * rows)
    copies = []
    for group in range(groups):
        at = pl.ds(group * 4 * rows, 4 * rows)
        for k, (hbm, ref) in enumerate(((fore_hbm, fore_ref), (back_hbm, back_ref))):
            copies.append(pltpu.make_async_copy(hbm.at[at], ref.at[at], sems.at[2 * group + k]))
    for copy in copies:
        copy.start()
    for group in range(groups):
        copies[2 * group].wait()
        copies[2 * group + 1].wait()
        at = pl.ds(group * 4 * rows, 4 * rows)
        out = pl.ds(group * pair, pair)
        for part in range(2):
            cols = [pl.ds(part * half, half), pl.ds(grid_size + part * half, half)]
            fore_re, fore_im = [fore_ref[at, c].astype(f32) for c in cols]
            back_re, back_im = [back_ref[at, c].astype(f32) for c in cols]
            values = (back_re * fore_re + back_im * fore_im, back_re * fore_im - back_im * fore_re)
            for k, v in enumerate(values):
                into = pl.ds(k * half, half)
                if part == 0:
                    first = jnp.concatenate([v[:rows], v[pair : pair + rows]], 0)
                    second = jnp.concatenate([v[rows:pair], v[pair + rows :]], 0)
                    send_a[out, into] = jnp.where(low, first, second).astype(bf16)
                    keep_a[out, into] = jnp.where(low, second, first)
                else:
                    first, second = v[:pair], v[pair:]
                    send_b[out, into] = jnp.where(high, first, second).astype(bf16)
                    keep_b[out, into] = jnp.where(high, second, first)


def times(one, two):
    return jnp.dot(one, two, preferred_element_type=f32)


def own_kernel(table_ref, shaped_ref, out_ref):
    out_ref[...] = times(table_ref[...], shaped_ref[...])


def other_kernel(table_ref, shaped_ref, own_ref, out_ref):
    out_ref[...] = (own_ref[...] + times(table_ref[...], shaped_ref[...])).astype(bf16)


def fields_kernel(block_rows, columns_ref, re_ref, im_ref, out_ref):
    rows, grid_size = out_ref.shape[0], columns_ref.shape[1]
    by_re, by_im = times(columns_ref[...], re_ref[...]), times(columns_ref[...], im_ref[...])
    if block_rows % 8 == 0:
        step, block = 2 * block_rows, block_rows
    else:
        step, block = rows, rows
    for at in range(0, rows, step):
        pieces = [[], []]
        for start in range(2 * at, 2 * (at + step), 2 * block):
            real, imag = slice(start, start + block), slice(start + block, start + 2 * block)
            pieces[0].append(by_re[real] - by_im[imag])
            pieces[1].append(by_im[real] + by_re[imag])
        for k, piece in enumerate(pieces):
            out = jnp.concatenate(piece, 0).astype(bf16)
            out_ref[pl.ds(at, step), pl.ds(k * grid_size, grid_size)] = out


def targets_kernel(targets_ref, re_ref, im_ref, out_ref):
    rows = targets_ref.shape[0] // 2
    real, imag = targets_ref[:rows], targets_ref[rows:]
    c_re, c_im = re_ref[...], im_ref[...]
    out_ref[:rows] = (times(real, c_re) + times(imag, c_im)).astype(bf16)
    out_ref[rows:] = (times(imag, c_re) - times(real, c_im)).astype(bf16)


def exactly(one, two, dims):
    return lax.dot_general(
        one, two, (dims, ((), ())), precision=lax.Precision.HIGHEST, preferred_element_type=f32
    )


def coupling_kernel(block_rows, by_xor, fields_ref, targets_ref, out_ref, held):
    modes = out_ref.shape[1]
    product = lax.dot_general(
        fields_ref[...], targets_ref[...], (((1,), (1,)), ((), ())), preferred_element_type=f32
    )
    left, right = product.shape
    row = lax.broadcasted_iota(jnp.int32, (left, right), 0) % block_rows
    col = lax.broadcasted_iota(jnp.int32, (left, right), 1) % block_rows
    product = jnp.where(row == col, product, 0.0)

    def groups(size):
        member = lax.broadcasted_iota(jnp.int32, (size // block_rows, size), 1) // block_rows
        group = lax.broadcasted_iota(jnp.int32, (size // block_rows, size), 0)
        return jnp.where(member == group, 1.0, 0.0).astype(f32)

    if block_rows % 8 == 0:
        product = jnp.sum(product.reshape(left // block_rows, block_rows, right), 1)
    else:
        product = exactly(groups(left), product, ((1,), (0,)))
    product = product.reshape(modes, 2, right)
    real, imag = product[:, 0], product[:, 1]
    right = right // 2
    both = jnp.concatenate(
        [real[:, :right] + imag[:, right:], imag[:, :right] - real[:, right:]], 0
    )
    held[...] = exactly(both, groups(right), ((1,), (1,)))
    if by_xor:
        me = lax.axis_index("modes")
        for at, e in enumerate(turns(modes)):
            out_ref[pl.ds(me ^ e, 1)] = held[pl.ds(at, 1)]
            out_ref[pl.ds(modes + (me ^ e), 1)] = held[pl.ds(modes + at, 1)]
    else:
        out_ref[...] = held[...]


def kernel_call(kernel, shape, dtype, flops, operands, grant=12, **more):
    place = pl.BlockSpec(memory_space=pltpu.VMEM)
    several = isinstance(dtype, list)
    if several:
        out_shape = [jax.ShapeDtypeStruct(s, d) for s, d in zip(shape, dtype)]
    else:
        out_shape = jax.ShapeDtypeStruct(shape, dtype)
    specs = dict(in_specs=[place] * len(operands), out_specs=[place] * len(shape) if several else place)
    return pl.pallas_call(
        kernel,
        out_shape=out_shape,
        compiler_params=pltpu.CompilerParams(vmem_limit_bytes=grant << 20),
        cost_estimate=pl.CostEstimate(flops=flops, bytes_accessed=4 << 20, transcendentals=0),
        **(specs | more),
    )(*operands)


def local(forward, backward, targets):
    modes_here, local_rows, double_width = forward.shape
    grid_size = double_width // 2
    count = lax.axis_size("modes")
    mode_total = modes_here * count
    block_rows = local_rows // count
    digits = stages(count)
    sizes = [size for _, size in reversed(digits)]
    half = grid_size // 2
    matmul = 2 * local_rows * double_width * double_width

    me = lax.axis_index("modes")
    owns = [me // stride % size for stride, size in digits]
    last = len(digits) - 1
    first = list(range(last))
    orders = [first, [1, 0] + first[2:]]
    kernel_first = block_rows % 8 == 0 and local_rows % (4 * block_rows) == 0
    if kernel_first:
        halves = kernel_call(
            lambda *refs: products_kernel(block_rows, *refs),
            [(local_rows // 2, grid_size)] * 4,
            [bf16, f32, bf16, f32],
            8 * local_rows * double_width,
            (forward[0], backward[0]),
            grant=52,
            in_specs=[pl.BlockSpec(memory_space=pltpu.HBM)] * 2,
            scratch_shapes=[pltpu.VMEM((local_rows, double_width), bf16)] * 2
            + [pltpu.SemaphoreType.DMA((2 * local_rows // (4 * block_rows),))],
        )
    else:
        product = product_of(forward[0], backward[0])
    kept = []
    for part, order in enumerate(orders):
        cols = slice(part * half, (part + 1) * half)
        axes = [last - d for d in range(len(digits))]
        if not kernel_first:
            partial = jnp.concatenate([p[:, cols] for p in product], -1)
            partial = partial.reshape(*sizes, block_rows, grid_size)
        for at, d in enumerate(order):
            stride, size = digits[d]
            left = sizes[: axes[d]] + sizes[axes[d] + 1 :] if at == 0 else None
            if at == 0 and kernel_first:
                send = [halves[2 * part].reshape(*left, block_rows, grid_size)]
                keep = halves[2 * part + 1].reshape(*left, block_rows, grid_size)
            else:
                send, keep = split_digit(partial, owns[d], size, axes[d])
            got = [exchange(v, (e + 1) * stride, count) for e, v in enumerate(send)]
            partial = reduce_digit(keep, got)
            axes = [a - (a > axes[d]) for a in axes]
        kept.append(partial)
    stride, size = digits[last]
    send, keep = split_digit(jnp.concatenate(kept, -1), owns[last], size, 0)
    got = [exchange(v, (e + 1) * stride, count) for e, v in enumerate(send)]
    summed = reduce_digit(keep, got)
    parts = []
    for part in range(2):
        over_re = summed[:, part * grid_size : part * grid_size + half]
        over_im = summed[:, part * grid_size + half : (part + 1) * grid_size]
        scale = lax.rsqrt(over_re * over_re + over_im * over_im + mode_total)
        parts += [over_re * scale, over_im * scale]
    block = jnp.concatenate(parts, -1).astype(bf16)

    block = gather_digit(block, owns[last], stride, size, 0, count)
    planes = []
    for part, order in enumerate(orders):
        piece = block[..., part * grid_size : (part + 1) * grid_size]
        done = [last]
        for d in reversed(order):
            axis = sum(1 for other in done if other > d)
            piece = gather_digit(piece, owns[d], *digits[d], axis, count)
            done.append(d)
        planes.append(piece.reshape(local_rows, grid_size))
    plane_re = jnp.concatenate([p[:, :half] for p in planes], -1)
    plane_im = jnp.concatenate([p[:, half:] for p in planes], -1)
    phase_plane = jnp.concatenate([plane_re, plane_im], -1)

    fore = forward[0].astype(f32)
    fore_re, fore_im = fore[:, :grid_size], fore[:, grid_size:]
    plane_re, plane_im = plane_re.astype(f32), plane_im.astype(f32)
    shaped = jnp.concatenate(
        [fore_re * plane_re - fore_im * plane_im, fore_re * plane_im + fore_im * plane_re], 0
    ).astype(bf16)
    other = lax.ppermute(shaped, "rows", [(0, 1), (1, 0)])

    c_re, c_im = propagator(grid_size)
    full_re, full_im = jnp.asarray(c_re, bf16), jnp.asarray(c_im, bf16)
    owners = count if block_rows % 8 == 0 else 1
    order = np.arange(local_rows).reshape(owners, -1)

    def table(cols):
        real, imag = c_re[:local_rows, cols], c_im[:local_rows, cols]
        rows = np.stack([np.concatenate([real, -imag], 1)[order], np.concatenate([imag, real], 1)[order]], 1)
        return jnp.asarray(rows.reshape(2 * local_rows, -1), bf16)

    column_shape = (2 * local_rows, grid_size)
    columns = kernel_call(
        own_kernel, column_shape, f32, matmul // 2, (table(slice(0, local_rows)), shaped)
    )
    columns, other = lax.optimization_barrier((columns, other))
    columns = kernel_call(
        other_kernel, column_shape, bf16, matmul // 2, (table(slice(local_rows, None)), other, columns)
    )
    blocks = columns.reshape(owners, 2, -1, block_rows, grid_size).transpose(0, 2, 1, 3, 4)
    blocks = blocks.reshape(count, 2 * block_rows, grid_size)
    if count <= 16:
        pixels = [pick(blocks, me, 0)]
        for at, e in enumerate(turns(count)[1:], 1):
            block = pick(blocks, me ^ e, 0)
            if at > LANES:
                block, pixels[at - LANES] = lax.optimization_barrier((block, pixels[at - LANES]))
            pixels.append(exchange(block, e, count))
    else:
        pixels = [lax.all_to_all(blocks, "modes", 0, 0, tiled=True)]

    output_fields = kernel_call(
        lambda *refs: fields_kernel(block_rows, *refs),
        (local_rows, double_width),
        bf16,
        matmul,
        (columns, full_re, full_im),
    )
    targets, output_fields = lax.optimization_barrier((targets, output_fields))
    seen = kernel_call(
        targets_kernel, column_shape, bf16, matmul, (targets.reshape(column_shape), full_re, full_im)
    )
    seen, output_fields = lax.optimization_barrier((seen, output_fields))
    rows = jnp.concatenate(pixels, 0).reshape(column_shape)
    term = kernel_call(
        lambda *refs: coupling_kernel(block_rows, len(pixels) > 1, *refs),
        (2 * mode_total, mode_total),
        f32,
        matmul,
        (rows, seen),
        scratch_shapes=[pltpu.VMEM((2 * mode_total, mode_total), f32)],
    )
    pieces = lax.all_to_all(term, ("modes", "rows"), 0, 0, tiled=True)
    coupling = jnp.sum(pieces, 0, keepdims=True)
    return (phase_plane, output_fields[None], coupling)


def solution(mesh):
    return jax.shard_map(
        local,
        mesh=mesh,
        in_specs=(
            P("modes", "rows", None),
            P("modes", "rows", None),
            P(None, None, ("rows", "modes"), None),
        ),
        out_specs=(P("rows", None), P("modes", "rows", None), P(("modes", "rows"), None)),
        check_vma=False,
    )
```

```python
import numpy as np

import jax
import jax.numpy as jnp
from jax import lax
from jax.experimental import pallas as pl
from jax.experimental.pallas import tpu as pltpu
from jax.sharding import PartitionSpec as P

bf16 = jnp.bfloat16
f32 = jnp.float32
LANES = 5
LATE = 4


def propagator(grid_size):
    index = np.arange(grid_size)
    centred = (index + grid_size // 2) % grid_size - grid_size // 2
    squared = centred * centred % (4 * grid_size)
    column = np.fft.ifft(np.exp(-2j * np.pi * squared / (4 * grid_size)))
    matrix = column[(index[:, None] - index[None, :]) % grid_size]
    return matrix.real, matrix.imag


def stages(count):
    digits, stride = [], 1
    while count // stride > 4:
        digits.append((stride, 2))
        stride *= 2
    digits.append((stride, count // stride))
    return digits


def exchange(values, offset, count):
    return lax.ppermute(values, "modes", [(i, i ^ offset) for i in range(count)])


def pick(values, index, axis):
    return lax.dynamic_index_in_dim(values, index, axis, keepdims=False)


def reduce_digit(keep, got):
    for g in got:
        keep = keep + g.astype(f32)
    return keep


def gather_digit(block, own, stride, size, axis, count):
    got = [block] + [exchange(block, e * stride, count) for e in range(1, size)]
    stacked = jnp.stack(got, axis)
    if size == 2:
        return jnp.where(own == 0, stacked, jnp.flip(stacked, axis))
    return jnp.stack([pick(stacked, own ^ at, axis) for at in range(size)], axis)


def split_digit(partial, own, size, axis):
    send = [pick(partial, own ^ e, axis).astype(bf16) for e in range(1, size)]
    return send, pick(partial, own, axis)


def product_of(fore, back):
    half = fore.shape[-1] // 2
    fore, back = fore.astype(f32), back.astype(f32)
    fore_re, fore_im = fore[..., :half], fore[..., half:]
    back_re, back_im = back[..., :half], back[..., half:]
    return back_re * fore_re + back_im * fore_im, back_re * fore_im - back_im * fore_re


def products_kernel(rows, part, fore_hbm, back_hbm, send, keep, fore_ref, back_ref, sems):
    upper = lax.axis_index("modes") // (part + 1) % 2 == 1
    grid_size = fore_ref.shape[1]
    half = grid_size // 2
    pair = 2 * rows
    groups = fore_ref.shape[0] // (4 * rows)
    copies = []
    for group in range(groups):
        at = pl.ds(group * 4 * rows, 4 * rows)
        for k in range(2):
            come, into = pl.ds(k * grid_size + part * half, half), pl.ds(k * half, half)
            for hbm, ref in ((fore_hbm, fore_ref), (back_hbm, back_ref)):
                sem = sems.at[len(copies)]
                copies.append(pltpu.make_async_copy(hbm.at[at, come], ref.at[at, into], sem))
    for copy in copies:
        copy.start()
    for group in range(groups):
        for copy in copies[4 * group : 4 * group + 4]:
            copy.wait()
        at = pl.ds(group * 4 * rows, 4 * rows)
        out = pl.ds(group * pair, pair)
        fore_re, fore_im = fore_ref[at, :half].astype(f32), fore_ref[at, half:].astype(f32)
        back_re, back_im = back_ref[at, :half].astype(f32), back_ref[at, half:].astype(f32)
        values = (back_re * fore_re + back_im * fore_im, back_re * fore_im - back_im * fore_re)
        for k, v in enumerate(values):
            into = pl.ds(k * half, half)
            if part == 0:
                first = jnp.concatenate([v[:rows], v[pair : pair + rows]], 0)
                second = jnp.concatenate([v[rows:pair], v[pair + rows :]], 0)
            else:
                first, second = v[:pair], v[pair:]
            send[out, into] = jnp.where(upper, first, second).astype(bf16)
            keep[out, into] = jnp.where(upper, second, first)


def times(one, two):
    return jnp.dot(one, two, preferred_element_type=f32)


def own_kernel(table_ref, shaped_ref, out_ref):
    out_ref[...] = times(table_ref[...], shaped_ref[...])


def other_kernel(table_ref, shaped_ref, own_ref, out_ref):
    out_ref[...] = (own_ref[...] + times(table_ref[...], shaped_ref[...])).astype(bf16)


def fields_kernel(block_rows, columns_ref, re_ref, im_ref, out_ref):
    rows, grid_size = out_ref.shape[0], columns_ref.shape[1]
    by_re, by_im = times(columns_ref[...], re_ref[...]), times(columns_ref[...], im_ref[...])
    if block_rows % 8 == 0:
        step, block = 2 * block_rows, block_rows
    else:
        step, block = rows, rows
    for at in range(0, rows, step):
        pieces = [[], []]
        for start in range(2 * at, 2 * (at + step), 2 * block):
            real, imag = slice(start, start + block), slice(start + block, start + 2 * block)
            pieces[0].append(by_re[real] - by_im[imag])
            pieces[1].append(by_im[real] + by_re[imag])
        for k, piece in enumerate(pieces):
            out = jnp.concatenate(piece, 0).astype(bf16)
            out_ref[pl.ds(at, step), pl.ds(k * grid_size, grid_size)] = out


def targets_kernel(targets_ref, re_ref, im_ref, out_ref):
    rows = targets_ref.shape[0] // 2
    real, imag = targets_ref[:rows], targets_ref[rows:]
    c_re, c_im = re_ref[...], im_ref[...]
    out_ref[:rows] = (times(real, c_re) + times(imag, c_im)).astype(bf16)
    out_ref[rows:] = (times(imag, c_re) - times(real, c_im)).astype(bf16)


def exactly(one, two, dims):
    return lax.dot_general(
        one, two, (dims, ((), ())), precision=lax.Precision.HIGHEST, preferred_element_type=f32
    )


def coupling_kernel(block_rows, by_xor, first, fields_ref, targets_ref, *rest):
    out_ref, held = rest[-2:]
    modes = out_ref.shape[1]
    product = lax.dot_general(
        fields_ref[...], targets_ref[...], (((1,), (1,)), ((), ())), preferred_element_type=f32
    )
    left, right = product.shape
    row = lax.broadcasted_iota(jnp.int32, (left, right), 0) % block_rows
    col = lax.broadcasted_iota(jnp.int32, (left, right), 1) % block_rows
    product = jnp.where(row == col, product, 0.0)

    def groups(size):
        member = lax.broadcasted_iota(jnp.int32, (size // block_rows, size), 1) // block_rows
        group = lax.broadcasted_iota(jnp.int32, (size // block_rows, size), 0)
        return jnp.where(member == group, 1.0, 0.0).astype(f32)

    if block_rows % 8 == 0:
        product = jnp.sum(product.reshape(left // block_rows, block_rows, right), 1)
    else:
        product = exactly(groups(left), product, ((1,), (0,)))
    sources = left // block_rows // 2
    product = product.reshape(sources, 2, right)
    real, imag = product[:, 0], product[:, 1]
    right = right // 2
    both = jnp.concatenate(
        [real[:, :right] + imag[:, right:], imag[:, :right] - real[:, right:]], 0
    )
    held[...] = exactly(both, groups(right), ((1,), (1,)))
    out_ref[...] = rest[0][...] if len(rest) > 2 else jnp.zeros_like(out_ref)
    me, there = lax.axis_index("modes"), modes // 2
    if by_xor:
        for at in range(sources):
            mode = me ^ ((first + at) // 2 + (first + at) % 2 * there)
            out_ref[pl.ds(mode, 1)] = held[pl.ds(at, 1)]
            out_ref[pl.ds(modes + mode, 1)] = held[pl.ds(sources + at, 1)]
    else:
        out_ref[...] = held[...]


def kernel_call(kernel, shape, dtype, flops, operands, grant=12, **more):
    place = pl.BlockSpec(memory_space=pltpu.VMEM)
    several = isinstance(dtype, list)
    if several:
        out_shape = [jax.ShapeDtypeStruct(s, d) for s, d in zip(shape, dtype)]
    else:
        out_shape = jax.ShapeDtypeStruct(shape, dtype)
    specs = dict(in_specs=[place] * len(operands), out_specs=[place] * len(shape) if several else place)
    return pl.pallas_call(
        kernel,
        out_shape=out_shape,
        compiler_params=pltpu.CompilerParams(vmem_limit_bytes=grant << 20),
        cost_estimate=pl.CostEstimate(flops=flops, bytes_accessed=4 << 20, transcendentals=0),
        **(specs | more),
    )(*operands)


def local(forward, backward, targets):
    modes_here, local_rows, double_width = forward.shape
    grid_size = double_width // 2
    count = lax.axis_size("modes")
    mode_total = modes_here * count
    block_rows = local_rows // count
    digits = stages(count)
    sizes = [size for _, size in reversed(digits)]
    half = grid_size // 2
    matmul = 2 * local_rows * double_width * double_width

    me = lax.axis_index("modes")
    owns = [me // stride % size for stride, size in digits]
    last = len(digits) - 1
    first = list(range(last))
    orders = [first, [1, 0] + first[2:]]
    kernel_first = block_rows % 8 == 0 and local_rows % (4 * block_rows) == 0
    if kernel_first:
        halves = []
        for part in range(2):
            halves += kernel_call(
                lambda *refs: products_kernel(block_rows, part, *refs),
                [(local_rows // 2, grid_size)] * 2,
                [bf16, f32],
                4 * local_rows * double_width,
                (forward[0], backward[0]),
                grant=52,
                in_specs=[pl.BlockSpec(memory_space=pltpu.HBM)] * 2,
                scratch_shapes=[pltpu.VMEM((local_rows, grid_size), bf16)] * 2
                + [pltpu.SemaphoreType.DMA((local_rows // block_rows,))],
            )
    else:
        product = product_of(forward[0], backward[0])
    kept = []
    for part, order in enumerate(orders):
        cols = slice(part * half, (part + 1) * half)
        axes = [last - d for d in range(len(digits))]
        if not kernel_first:
            partial = jnp.concatenate([p[:, cols] for p in product], -1)
            partial = partial.reshape(*sizes, block_rows, grid_size)
        for at, d in enumerate(order):
            stride, size = digits[d]
            left = sizes[: axes[d]] + sizes[axes[d] + 1 :] if at == 0 else None
            if at == 0 and kernel_first:
                send = [halves[2 * part].reshape(*left, block_rows, grid_size)]
                keep = halves[2 * part + 1].reshape(*left, block_rows, grid_size)
            else:
                send, keep = split_digit(partial, owns[d], size, axes[d])
            got = [exchange(v, (e + 1) * stride, count) for e, v in enumerate(send)]
            partial = reduce_digit(keep, got)
            axes = [a - (a > axes[d]) for a in axes]
        kept.append(partial)
    stride, size = digits[last]
    send, keep = split_digit(jnp.concatenate(kept, -1), owns[last], size, 0)
    got = [exchange(v, (e + 1) * stride, count) for e, v in enumerate(send)]
    summed = reduce_digit(keep, got)
    parts = []
    for part in range(2):
        over_re = summed[:, part * grid_size : part * grid_size + half]
        over_im = summed[:, part * grid_size + half : (part + 1) * grid_size]
        scale = lax.rsqrt(over_re * over_re + over_im * over_im + mode_total)
        parts += [over_re * scale, over_im * scale]
    block = jnp.concatenate(parts, -1).astype(bf16)

    block = gather_digit(block, owns[last], stride, size, 0, count)
    planes = []
    for part, order in enumerate(orders):
        piece = block[..., part * grid_size : (part + 1) * grid_size]
        done = [last]
        for d in reversed(order):
            axis = sum(1 for other in done if other > d)
            piece = gather_digit(piece, owns[d], *digits[d], axis, count)
            done.append(d)
        planes.append(piece.reshape(local_rows, grid_size))
    plane_re = jnp.concatenate([p[:, :half] for p in planes], -1)
    plane_im = jnp.concatenate([p[:, half:] for p in planes], -1)
    phase_plane = jnp.concatenate([plane_re, plane_im], -1)

    fore = forward[0].astype(f32)
    fore_re, fore_im = fore[:, :grid_size], fore[:, grid_size:]
    plane_re, plane_im = plane_re.astype(f32), plane_im.astype(f32)
    shaped = jnp.concatenate(
        [fore_re * plane_re - fore_im * plane_im, fore_re * plane_im + fore_im * plane_re], 0
    ).astype(bf16)
    other = lax.ppermute(shaped, "rows", [(0, 1), (1, 0)])

    c_re, c_im = propagator(grid_size)
    full_re, full_im = jnp.asarray(c_re, bf16), jnp.asarray(c_im, bf16)
    owners = count if block_rows % 8 == 0 else 1
    order = np.arange(local_rows).reshape(owners, -1)

    def table(cols):
        real, imag = c_re[:local_rows, cols], c_im[:local_rows, cols]
        rows = np.stack([np.concatenate([real, -imag], 1)[order], np.concatenate([imag, real], 1)[order]], 1)
        return jnp.asarray(rows.reshape(2 * local_rows, -1), bf16)

    column_shape = (2 * local_rows, grid_size)
    columns = kernel_call(
        own_kernel, column_shape, f32, matmul // 2, (table(slice(0, local_rows)), shaped)
    )
    columns, other = lax.optimization_barrier((columns, other))
    columns = kernel_call(
        other_kernel, column_shape, bf16, matmul // 2, (table(slice(local_rows, None)), other, columns)
    )
    blocks = columns.reshape(owners, 2, -1, block_rows, grid_size).transpose(0, 2, 1, 3, 4)
    blocks = blocks.reshape(count, 2 * block_rows, grid_size)
    if count <= 16:
        turns = [at // 2 + count // 2 * (at % 2) for at in range(count)]
        pixels = [pick(blocks, me, 0)]
        for at, e in enumerate(turns[1:], 1):
            block = pick(blocks, me ^ e, 0)
            if at > LANES:
                block, pixels[at - LANES] = lax.optimization_barrier((block, pixels[at - LANES]))
            pixels.append(exchange(block, e, count))
    else:
        pixels = [lax.all_to_all(blocks, "modes", 0, 0, tiled=True)]

    output_fields = kernel_call(
        lambda *refs: fields_kernel(block_rows, *refs),
        (local_rows, double_width),
        bf16,
        matmul,
        (columns, full_re, full_im),
    )
    targets, output_fields = lax.optimization_barrier((targets, output_fields))
    seen = kernel_call(
        targets_kernel, column_shape, bf16, matmul, (targets.reshape(column_shape), full_re, full_im)
    )
    cut = len(pixels) - LATE if len(pixels) > LATE else len(pixels)
    seen, output_fields = lax.optimization_barrier((seen, output_fields))
    term, at = None, 0
    for group in (pixels[:cut], pixels[cut:]):
        if group:
            rows = jnp.concatenate(group, 0).reshape(-1, grid_size)
            term = kernel_call(
                lambda *refs: coupling_kernel(block_rows, len(pixels) > 1, at, *refs),
                (2 * mode_total, mode_total),
                f32,
                2 * rows.shape[0] * 2 * local_rows * grid_size,
                (rows, seen) if term is None else (rows, seen, term),
                scratch_shapes=[pltpu.VMEM((rows.shape[0] // block_rows, mode_total), f32)],
            )
            at += len(group)
    pieces = lax.all_to_all(term, ("modes", "rows"), 0, 0, tiled=True)
    coupling = jnp.sum(pieces, 0, keepdims=True)
    return (phase_plane, output_fields[None], coupling)


def solution(mesh):
    return jax.shard_map(
        local,
        mesh=mesh,
        in_specs=(
            P("modes", "rows", None),
            P("modes", "rows", None),
            P(None, None, ("rows", "modes"), None),
        ),
        out_specs=(P("rows", None), P("modes", "rows", None), P(("modes", "rows"), None)),
        check_vma=False,
    )
```

```python
import numpy as np

import jax
import jax.numpy as jnp
from jax import lax
from jax.experimental import pallas as pl
from jax.experimental.pallas import tpu as pltpu
from jax.sharding import PartitionSpec as P

bf16 = jnp.bfloat16
f32 = jnp.float32
LANES = 5
LATE = 4


def propagator(grid_size):
    index = np.arange(grid_size)
    centred = (index + grid_size // 2) % grid_size - grid_size // 2
    squared = centred * centred % (4 * grid_size)
    column = np.fft.ifft(np.exp(-2j * np.pi * squared / (4 * grid_size)))
    matrix = column[(index[:, None] - index[None, :]) % grid_size]
    return matrix.real, matrix.imag


def stages(count):
    digits, stride = [], 1
    while count // stride > 4:
        digits.append((stride, 2))
        stride *= 2
    digits.append((stride, count // stride))
    return digits


def exchange(values, offset, count):
    return lax.ppermute(values, "modes", [(i, i ^ offset) for i in range(count)])


def pick(values, index, axis):
    return lax.dynamic_index_in_dim(values, index, axis, keepdims=False)


def reduce_digit(keep, got):
    for g in got:
        keep = keep + g.astype(f32)
    return keep


def gather_digit(block, own, stride, size, axis, count):
    got = [block] + [exchange(block, e * stride, count) for e in range(1, size)]
    stacked = jnp.stack(got, axis)
    if size == 2:
        return jnp.where(own == 0, stacked, jnp.flip(stacked, axis))
    return jnp.stack([pick(stacked, own ^ at, axis) for at in range(size)], axis)


def split_digit(partial, own, size, axis):
    send = [pick(partial, own ^ e, axis).astype(bf16) for e in range(1, size)]
    return send, pick(partial, own, axis)


def product_of(fore, back):
    half = fore.shape[-1] // 2
    fore, back = fore.astype(f32), back.astype(f32)
    fore_re, fore_im = fore[..., :half], fore[..., half:]
    back_re, back_im = back[..., :half], back[..., half:]
    return back_re * fore_re + back_im * fore_im, back_re * fore_im - back_im * fore_re


def products_kernel(rows, fore_hbm, back_hbm, send_a, keep_a, send_b, keep_b, fore_ref, back_ref, sems):
    me = lax.axis_index("modes")
    low, high = me % 2 == 1, me // 2 % 2 == 1
    grid_size = fore_ref.shape[1] // 2
    half = grid_size // 2
    pair = 2 * rows
    groups = fore_ref.shape[0] // (4 * rows)
    copies = []
    for group in range(groups):
        at = pl.ds(group * 4 * rows, 4 * rows)
        for k, (hbm, ref) in enumerate(((fore_hbm, fore_ref), (back_hbm, back_ref))):
            copies.append(pltpu.make_async_copy(hbm.at[at], ref.at[at], sems.at[2 * group + k]))
    for copy in copies:
        copy.start()
    for group in range(groups):
        copies[2 * group].wait()
        copies[2 * group + 1].wait()
        at = pl.ds(group * 4 * rows, 4 * rows)
        out = pl.ds(group * pair, pair)
        for part in range(2):
            cols = [pl.ds(part * half, half), pl.ds(grid_size + part * half, half)]
            fore_re, fore_im = [fore_ref[at, c].astype(f32) for c in cols]
            back_re, back_im = [back_ref[at, c].astype(f32) for c in cols]
            values = (back_re * fore_re + back_im * fore_im, back_re * fore_im - back_im * fore_re)
            for k, v in enumerate(values):
                into = pl.ds(k * half, half)
                if part == 0:
                    first = jnp.concatenate([v[:rows], v[pair : pair + rows]], 0)
                    second = jnp.concatenate([v[rows:pair], v[pair + rows :]], 0)
                    send_a[out, into] = jnp.where(low, first, second).astype(bf16)
                    keep_a[out, into] = jnp.where(low, second, first)
                else:
                    first, second = v[:pair], v[pair:]
                    send_b[out, into] = jnp.where(high, first, second).astype(bf16)
                    keep_b[out, into] = jnp.where(high, second, first)


def times(one, two):
    return jnp.dot(one, two, preferred_element_type=f32)


def own_kernel(table_ref, shaped_ref, out_ref):
    out_ref[...] = times(table_ref[...], shaped_ref[...])


def other_kernel(table_ref, shaped_ref, own_ref, out_ref):
    out_ref[...] = (own_ref[...] + times(table_ref[...], shaped_ref[...])).astype(bf16)


def fields_kernel(block_rows, columns_ref, re_ref, im_ref, out_ref):
    rows, grid_size = out_ref.shape[0], columns_ref.shape[1]
    by_re, by_im = times(columns_ref[...], re_ref[...]), times(columns_ref[...], im_ref[...])
    if block_rows % 8 == 0:
        step, block = 2 * block_rows, block_rows
    else:
        step, block = rows, rows
    for at in range(0, rows, step):
        pieces = [[], []]
        for start in range(2 * at, 2 * (at + step), 2 * block):
            real, imag = slice(start, start + block), slice(start + block, start + 2 * block)
            pieces[0].append(by_re[real] - by_im[imag])
            pieces[1].append(by_im[real] + by_re[imag])
        for k, piece in enumerate(pieces):
            out = jnp.concatenate(piece, 0).astype(bf16)
            out_ref[pl.ds(at, step), pl.ds(k * grid_size, grid_size)] = out


def targets_kernel(targets_ref, re_ref, im_ref, out_ref):
    rows = targets_ref.shape[0] // 2
    real, imag = targets_ref[:rows], targets_ref[rows:]
    c_re, c_im = re_ref[...], im_ref[...]
    out_ref[:rows] = (times(real, c_re) + times(imag, c_im)).astype(bf16)
    out_ref[rows:] = (times(imag, c_re) - times(real, c_im)).astype(bf16)


def exactly(one, two, dims):
    return lax.dot_general(
        one, two, (dims, ((), ())), precision=lax.Precision.HIGHEST, preferred_element_type=f32
    )


def coupling_kernel(block_rows, by_xor, first, fields_ref, targets_ref, *rest):
    out_ref, held = rest[-2:]
    modes = out_ref.shape[1]
    product = lax.dot_general(
        fields_ref[...], targets_ref[...], (((1,), (1,)), ((), ())), preferred_element_type=f32
    )
    left, right = product.shape
    row = lax.broadcasted_iota(jnp.int32, (left, right), 0) % block_rows
    col = lax.broadcasted_iota(jnp.int32, (left, right), 1) % block_rows
    product = jnp.where(row == col, product, 0.0)

    def groups(size):
        member = lax.broadcasted_iota(jnp.int32, (size // block_rows, size), 1) // block_rows
        group = lax.broadcasted_iota(jnp.int32, (size // block_rows, size), 0)
        return jnp.where(member == group, 1.0, 0.0).astype(f32)

    if block_rows % 8 == 0:
        product = jnp.sum(product.reshape(left // block_rows, block_rows, right), 1)
    else:
        product = exactly(groups(left), product, ((1,), (0,)))
    sources = left // block_rows // 2
    product = product.reshape(sources, 2, right)
    real, imag = product[:, 0], product[:, 1]
    right = right // 2
    both = jnp.concatenate(
        [real[:, :right] + imag[:, right:], imag[:, :right] - real[:, right:]], 0
    )
    held[...] = exactly(both, groups(right), ((1,), (1,)))
    out_ref[...] = rest[0][...] if len(rest) > 2 else jnp.zeros_like(out_ref)
    me, there = lax.axis_index("modes"), modes // 2
    if by_xor:
        for at in range(sources):
            mode = me ^ ((first + at) // 2 + (first + at) % 2 * there)
            out_ref[pl.ds(mode, 1)] = held[pl.ds(at, 1)]
            out_ref[pl.ds(modes + mode, 1)] = held[pl.ds(sources + at, 1)]
    else:
        out_ref[...] = held[...]


def kernel_call(kernel, shape, dtype, flops, operands, grant=12, **more):
    place = pl.BlockSpec(memory_space=pltpu.VMEM)
    several = isinstance(dtype, list)
    if several:
        out_shape = [jax.ShapeDtypeStruct(s, d) for s, d in zip(shape, dtype)]
    else:
        out_shape = jax.ShapeDtypeStruct(shape, dtype)
    specs = dict(in_specs=[place] * len(operands), out_specs=[place] * len(shape) if several else place)
    return pl.pallas_call(
        kernel,
        out_shape=out_shape,
        compiler_params=pltpu.CompilerParams(vmem_limit_bytes=grant << 20),
        cost_estimate=pl.CostEstimate(flops=flops, bytes_accessed=4 << 20, transcendentals=0),
        **(specs | more),
    )(*operands)


def local(forward, backward, targets):
    modes_here, local_rows, double_width = forward.shape
    grid_size = double_width // 2
    count = lax.axis_size("modes")
    mode_total = modes_here * count
    block_rows = local_rows // count
    digits = stages(count)
    sizes = [size for _, size in reversed(digits)]
    half = grid_size // 2
    matmul = 2 * local_rows * double_width * double_width

    me = lax.axis_index("modes")
    owns = [me // stride % size for stride, size in digits]
    last = len(digits) - 1
    first = list(range(last))
    orders = [first, [1, 0] + first[2:]]
    kernel_first = block_rows % 8 == 0 and local_rows % (4 * block_rows) == 0
    if kernel_first:
        halves = kernel_call(
            lambda *refs: products_kernel(block_rows, *refs),
            [(local_rows // 2, grid_size)] * 4,
            [bf16, f32, bf16, f32],
            8 * local_rows * double_width,
            (forward[0], backward[0]),
            grant=52,
            in_specs=[pl.BlockSpec(memory_space=pltpu.HBM)] * 2,
            scratch_shapes=[pltpu.VMEM((local_rows, double_width), bf16)] * 2
            + [pltpu.SemaphoreType.DMA((2 * local_rows // (4 * block_rows),))],
        )
    else:
        product = product_of(forward[0], backward[0])
    kept = []
    for part, order in enumerate(orders):
        cols = slice(part * half, (part + 1) * half)
        axes = [last - d for d in range(len(digits))]
        if not kernel_first:
            partial = jnp.concatenate([p[:, cols] for p in product], -1)
            partial = partial.reshape(*sizes, block_rows, grid_size)
        for at, d in enumerate(order):
            stride, size = digits[d]
            left = sizes[: axes[d]] + sizes[axes[d] + 1 :] if at == 0 else None
            if at == 0 and kernel_first:
                send = [halves[2 * part].reshape(*left, block_rows, grid_size)]
                keep = halves[2 * part + 1].reshape(*left, block_rows, grid_size)
            else:
                send, keep = split_digit(partial, owns[d], size, axes[d])
            got = [exchange(v, (e + 1) * stride, count) for e, v in enumerate(send)]
            partial = reduce_digit(keep, got)
            axes = [a - (a > axes[d]) for a in axes]
        kept.append(partial)
    stride, size = digits[last]
    send, keep = split_digit(jnp.concatenate(kept, -1), owns[last], size, 0)
    got = [exchange(v, (e + 1) * stride, count) for e, v in enumerate(send)]
    summed = reduce_digit(keep, got)
    parts = []
    for part in range(2):
        over_re = summed[:, part * grid_size : part * grid_size + half]
        over_im = summed[:, part * grid_size + half : (part + 1) * grid_size]
        scale = lax.rsqrt(over_re * over_re + over_im * over_im + mode_total)
        parts += [over_re * scale, over_im * scale]
    block = jnp.concatenate(parts, -1).astype(bf16)

    block = gather_digit(block, owns[last], stride, size, 0, count)
    planes = []
    for part, order in enumerate(orders):
        piece = block[..., part * grid_size : (part + 1) * grid_size]
        done = [last]
        for at, d in enumerate(reversed(order)):
            axis = sum(1 for other in done if other > d)
            piece = gather_digit(piece, owns[d], *digits[d], axis, count)
            if part == 0 and at == 0:
                piece, forward = lax.optimization_barrier((piece, forward))
            done.append(d)
        planes.append(piece.reshape(local_rows, grid_size))
    fore = forward[0].astype(f32)
    plane_re = jnp.concatenate([p[:, :half] for p in planes], -1)
    plane_im = jnp.concatenate([p[:, half:] for p in planes], -1)
    phase_plane = jnp.concatenate([plane_re, plane_im], -1)

    fore_re, fore_im = fore[:, :grid_size], fore[:, grid_size:]
    plane_re, plane_im = plane_re.astype(f32), plane_im.astype(f32)
    shaped = jnp.concatenate(
        [fore_re * plane_re - fore_im * plane_im, fore_re * plane_im + fore_im * plane_re], 0
    ).astype(bf16)
    other = lax.ppermute(shaped, "rows", [(0, 1), (1, 0)])

    c_re, c_im = propagator(grid_size)
    full_re, full_im = jnp.asarray(c_re, bf16), jnp.asarray(c_im, bf16)
    owners = count if block_rows % 8 == 0 else 1
    order = np.arange(local_rows).reshape(owners, -1)

    def table(cols):
        real, imag = c_re[:local_rows, cols], c_im[:local_rows, cols]
        rows = np.stack([np.concatenate([real, -imag], 1)[order], np.concatenate([imag, real], 1)[order]], 1)
        return jnp.asarray(rows.reshape(2 * local_rows, -1), bf16)

    column_shape = (2 * local_rows, grid_size)
    columns = kernel_call(
        own_kernel, column_shape, f32, matmul // 2, (table(slice(0, local_rows)), shaped)
    )
    columns, other = lax.optimization_barrier((columns, other))
    columns = kernel_call(
        other_kernel, column_shape, bf16, matmul // 2, (table(slice(local_rows, None)), other, columns)
    )
    blocks = columns.reshape(owners, 2, -1, block_rows, grid_size).transpose(0, 2, 1, 3, 4)
    blocks = blocks.reshape(count, 2 * block_rows, grid_size)
    if count <= 16:
        turns = [at // 2 + count // 2 * (at % 2) for at in range(count)]
        pixels = [pick(blocks, me, 0)]
        for at, e in enumerate(turns[1:], 1):
            block = pick(blocks, me ^ e, 0)
            if at > LANES:
                block, pixels[at - LANES] = lax.optimization_barrier((block, pixels[at - LANES]))
            pixels.append(exchange(block, e, count))
    else:
        pixels = [lax.all_to_all(blocks, "modes", 0, 0, tiled=True)]

    output_fields = kernel_call(
        lambda *refs: fields_kernel(block_rows, *refs),
        (local_rows, double_width),
        bf16,
        matmul,
        (columns, full_re, full_im),
    )
    targets, output_fields = lax.optimization_barrier((targets, output_fields))
    seen = kernel_call(
        targets_kernel, column_shape, bf16, matmul, (targets.reshape(column_shape), full_re, full_im)
    )
    cut = len(pixels) - LATE if len(pixels) > LATE else len(pixels)
    seen, output_fields = lax.optimization_barrier((seen, output_fields))
    term, at = None, 0
    for group in (pixels[:cut], pixels[cut:]):
        if group:
            rows = jnp.concatenate(group, 0).reshape(-1, grid_size)
            term = kernel_call(
                lambda *refs: coupling_kernel(block_rows, len(pixels) > 1, at, *refs),
                (2 * mode_total, mode_total),
                f32,
                2 * rows.shape[0] * 2 * local_rows * grid_size,
                (rows, seen) if term is None else (rows, seen, term),
                scratch_shapes=[pltpu.VMEM((rows.shape[0] // block_rows, mode_total), f32)],
            )
            at += len(group)
    pieces = lax.all_to_all(term, ("modes", "rows"), 0, 0, tiled=True)
    coupling = jnp.sum(pieces, 0, keepdims=True)
    return (phase_plane, output_fields[None], coupling)


def solution(mesh):
    return jax.shard_map(
        local,
        mesh=mesh,
        in_specs=(
            P("modes", "rows", None),
            P("modes", "rows", None),
            P(None, None, ("rows", "modes"), None),
        ),
        out_specs=(P("rows", None), P("modes", "rows", None), P(("modes", "rows"), None)),
        check_vma=False,
    )
```

```python
import numpy as np

import jax
import jax.numpy as jnp
from jax import lax
from jax.experimental import pallas as pl
from jax.experimental.pallas import tpu as pltpu
from jax.sharding import PartitionSpec as P

bf16 = jnp.bfloat16
f32 = jnp.float32


def propagator(grid_size):
    index = np.arange(grid_size)
    centred = (index + grid_size // 2) % grid_size - grid_size // 2
    squared = centred * centred % (4 * grid_size)
    column = np.fft.ifft(np.exp(-2j * np.pi * squared / (4 * grid_size)))
    matrix = column[(index[:, None] - index[None, :]) % grid_size]
    return matrix.real, matrix.imag


def stages(count):
    digits, stride = [], 1
    while count // stride > 4:
        digits.append((stride, 2))
        stride *= 2
    digits.append((stride, count // stride))
    return digits


def exchange(values, offset, count):
    return lax.ppermute(values, "modes", [(i, i ^ offset) for i in range(count)])


def pick(values, index, axis):
    return lax.dynamic_index_in_dim(values, index, axis, keepdims=False)


def reduce_digit(keep, got):
    for g in got:
        keep = keep + g.astype(f32)
    return keep


def gather_digit(block, own, stride, size, axis, count):
    got = [block] + [exchange(block, e * stride, count) for e in range(1, size)]
    stacked = jnp.stack(got, axis)
    if size == 2:
        return jnp.where(own == 0, stacked, jnp.flip(stacked, axis))
    return jnp.stack([pick(stacked, own ^ at, axis) for at in range(size)], axis)


def split_digit(partial, own, size, axis):
    send = [pick(partial, own ^ e, axis).astype(bf16) for e in range(1, size)]
    return send, pick(partial, own, axis)


def product_of(fore, back):
    half = fore.shape[-1] // 2
    fore, back = fore.astype(f32), back.astype(f32)
    fore_re, fore_im = fore[..., :half], fore[..., half:]
    back_re, back_im = back[..., :half], back[..., half:]
    return back_re * fore_re + back_im * fore_im, back_re * fore_im - back_im * fore_re


def products_kernel(rows, fore_hbm, back_hbm, send_a, keep_a, send_b, keep_b, fore_ref, back_ref, sems):
    me = lax.axis_index("modes")
    low, high = me % 2 == 1, me // 2 % 2 == 1
    grid_size = fore_ref.shape[1] // 2
    half = grid_size // 2
    pair = 2 * rows
    groups = fore_ref.shape[0] // (4 * rows)
    copies = []
    for group in range(groups):
        at = pl.ds(group * 4 * rows, 4 * rows)
        for k, (hbm, ref) in enumerate(((fore_hbm, fore_ref), (back_hbm, back_ref))):
            copies.append(pltpu.make_async_copy(hbm.at[at], ref.at[at], sems.at[2 * group + k]))
    for copy in copies:
        copy.start()
    for group in range(groups):
        copies[2 * group].wait()
        copies[2 * group + 1].wait()
        at = pl.ds(group * 4 * rows, 4 * rows)
        out = pl.ds(group * pair, pair)
        for part in range(2):
            cols = [pl.ds(part * half, half), pl.ds(grid_size + part * half, half)]
            fore_re, fore_im = [fore_ref[at, c].astype(f32) for c in cols]
            back_re, back_im = [back_ref[at, c].astype(f32) for c in cols]
            values = (back_re * fore_re + back_im * fore_im, back_re * fore_im - back_im * fore_re)
            for k, v in enumerate(values):
                into = pl.ds(k * half, half)
                if part == 0:
                    first = jnp.concatenate([v[:rows], v[pair : pair + rows]], 0)
                    second = jnp.concatenate([v[rows:pair], v[pair + rows :]], 0)
                    send_a[out, into] = jnp.where(low, first, second).astype(bf16)
                    keep_a[out, into] = jnp.where(low, second, first)
                else:
                    first, second = v[:pair], v[pair:]
                    send_b[out, into] = jnp.where(high, first, second).astype(bf16)
                    keep_b[out, into] = jnp.where(high, second, first)


def times(one, two):
    return jnp.dot(one, two, preferred_element_type=f32)


def own_kernel(table_ref, shaped_ref, out_ref):
    out_ref[...] = times(table_ref[...], shaped_ref[...])


def other_kernel(table_ref, shaped_ref, own_ref, out_ref):
    out_ref[...] = (own_ref[...] + times(table_ref[...], shaped_ref[...])).astype(bf16)


def fields_kernel(block_rows, columns_ref, re_ref, im_ref, out_ref):
    rows, grid_size = out_ref.shape[0], columns_ref.shape[1]
    by_re, by_im = times(columns_ref[...], re_ref[...]), times(columns_ref[...], im_ref[...])
    if block_rows % 8 == 0:
        step, block = 2 * block_rows, block_rows
    else:
        step, block = rows, rows
    for at in range(0, rows, step):
        pieces = [[], []]
        for start in range(2 * at, 2 * (at + step), 2 * block):
            real, imag = slice(start, start + block), slice(start + block, start + 2 * block)
            pieces[0].append(by_re[real] - by_im[imag])
            pieces[1].append(by_im[real] + by_re[imag])
        for k, piece in enumerate(pieces):
            out = jnp.concatenate(piece, 0).astype(bf16)
            out_ref[pl.ds(at, step), pl.ds(k * grid_size, grid_size)] = out


def targets_kernel(targets_ref, re_ref, im_ref, out_ref):
    rows = targets_ref.shape[0] // 2
    real, imag = targets_ref[:rows], targets_ref[rows:]
    c_re, c_im = re_ref[...], im_ref[...]
    out_ref[:rows] = (times(real, c_re) + times(imag, c_im)).astype(bf16)
    out_ref[rows:] = (times(imag, c_re) - times(real, c_im)).astype(bf16)


def exactly(one, two, dims):
    return lax.dot_general(
        one, two, (dims, ((), ())), precision=lax.Precision.HIGHEST, preferred_element_type=f32
    )


def coupling_kernel(block_rows, fields_ref, targets_ref, out_ref):
    modes = out_ref.shape[1]
    product = lax.dot_general(
        fields_ref[...], targets_ref[...], (((1,), (1,)), ((), ())), preferred_element_type=f32
    )
    left, right = product.shape
    row = lax.broadcasted_iota(jnp.int32, (left, right), 0) % block_rows
    col = lax.broadcasted_iota(jnp.int32, (left, right), 1) % block_rows
    product = jnp.where(row == col, product, 0.0)

    def groups(size):
        member = lax.broadcasted_iota(jnp.int32, (size // block_rows, size), 1) // block_rows
        group = lax.broadcasted_iota(jnp.int32, (size // block_rows, size), 0)
        return jnp.where(member == group, 1.0, 0.0).astype(f32)

    if block_rows % 8 == 0:
        product = jnp.sum(product.reshape(left // block_rows, block_rows, right), 1)
    else:
        product = exactly(groups(left), product, ((1,), (0,)))
    product = product.reshape(modes, 2, right)
    real, imag = product[:, 0], product[:, 1]
    right = right // 2
    both = jnp.concatenate(
        [real[:, :right] + imag[:, right:], imag[:, :right] - real[:, right:]], 0
    )
    out_ref[...] = exactly(both, groups(right), ((1,), (1,)))


def kernel_call(kernel, shape, dtype, flops, operands, grant=12, **more):
    place = pl.BlockSpec(memory_space=pltpu.VMEM)
    several = isinstance(dtype, list)
    if several:
        out_shape = [jax.ShapeDtypeStruct(s, d) for s, d in zip(shape, dtype)]
    else:
        out_shape = jax.ShapeDtypeStruct(shape, dtype)
    specs = dict(in_specs=[place] * len(operands), out_specs=[place] * len(shape) if several else place)
    return pl.pallas_call(
        kernel,
        out_shape=out_shape,
        compiler_params=pltpu.CompilerParams(vmem_limit_bytes=grant << 20),
        cost_estimate=pl.CostEstimate(flops=flops, bytes_accessed=4 << 20, transcendentals=0),
        **(specs | more),
    )(*operands)


def local(forward, backward, targets):
    modes_here, local_rows, double_width = forward.shape
    grid_size = double_width // 2
    count = lax.axis_size("modes")
    mode_total = modes_here * count
    block_rows = local_rows // count
    digits = stages(count)
    sizes = [size for _, size in reversed(digits)]
    half = grid_size // 2
    matmul = 2 * local_rows * double_width * double_width

    me = lax.axis_index("modes")
    owns = [me // stride % size for stride, size in digits]
    last = len(digits) - 1
    first = list(range(last))
    orders = [first, [1, 0] + first[2:]]
    kernel_first = block_rows % 8 == 0 and local_rows % (4 * block_rows) == 0
    if kernel_first:
        halves = kernel_call(
            lambda *refs: products_kernel(block_rows, *refs),
            [(local_rows // 2, grid_size)] * 4,
            [bf16, f32, bf16, f32],
            8 * local_rows * double_width,
            (forward[0], backward[0]),
            grant=52,
            in_specs=[pl.BlockSpec(memory_space=pltpu.HBM)] * 2,
            scratch_shapes=[pltpu.VMEM((local_rows, double_width), bf16)] * 2
            + [pltpu.SemaphoreType.DMA((2 * local_rows // (4 * block_rows),))],
        )
    else:
        product = product_of(forward[0], backward[0])
    kept = []
    for part, order in enumerate(orders):
        cols = slice(part * half, (part + 1) * half)
        axes = [last - d for d in range(len(digits))]
        if not kernel_first:
            partial = jnp.concatenate([p[:, cols] for p in product], -1)
            partial = partial.reshape(*sizes, block_rows, grid_size)
        for at, d in enumerate(order):
            stride, size = digits[d]
            left = sizes[: axes[d]] + sizes[axes[d] + 1 :] if at == 0 else None
            if at == 0 and kernel_first:
                send = [halves[2 * part].reshape(*left, block_rows, grid_size)]
                keep = halves[2 * part + 1].reshape(*left, block_rows, grid_size)
            else:
                send, keep = split_digit(partial, owns[d], size, axes[d])
            got = [exchange(v, (e + 1) * stride, count) for e, v in enumerate(send)]
            partial = reduce_digit(keep, got)
            axes = [a - (a > axes[d]) for a in axes]
        kept.append(partial)
    stride, size = digits[last]
    send, keep = split_digit(jnp.concatenate(kept, -1), owns[last], size, 0)
    got = [exchange(v, (e + 1) * stride, count) for e, v in enumerate(send)]
    summed = reduce_digit(keep, got)
    parts = []
    for part in range(2):
        over_re = summed[:, part * grid_size : part * grid_size + half]
        over_im = summed[:, part * grid_size + half : (part + 1) * grid_size]
        scale = lax.rsqrt(over_re * over_re + over_im * over_im + mode_total)
        parts += [over_re * scale, over_im * scale]
    block = jnp.concatenate(parts, -1).astype(bf16)

    block = gather_digit(block, owns[last], stride, size, 0, count)
    planes = []
    for part, order in enumerate(orders):
        piece = block[..., part * grid_size : (part + 1) * grid_size]
        done = [last]
        for d in reversed(order):
            axis = sum(1 for other in done if other > d)
            piece = gather_digit(piece, owns[d], *digits[d], axis, count)
            done.append(d)
        planes.append(piece.reshape(local_rows, grid_size))
    plane_re = jnp.concatenate([p[:, :half] for p in planes], -1)
    plane_im = jnp.concatenate([p[:, half:] for p in planes], -1)
    phase_plane = jnp.concatenate([plane_re, plane_im], -1)

    fore = forward[0].astype(f32)
    fore_re, fore_im = fore[:, :grid_size], fore[:, grid_size:]
    plane_re, plane_im = plane_re.astype(f32), plane_im.astype(f32)
    shaped = jnp.concatenate(
        [fore_re * plane_re - fore_im * plane_im, fore_re * plane_im + fore_im * plane_re], 0
    ).astype(bf16)
    other = lax.ppermute(shaped, "rows", [(0, 1), (1, 0)])

    c_re, c_im = propagator(grid_size)
    full_re, full_im = jnp.asarray(c_re, bf16), jnp.asarray(c_im, bf16)
    owners = count if block_rows % 8 == 0 else 1
    order = np.arange(local_rows).reshape(owners, -1)

    def table(cols):
        real, imag = c_re[:local_rows, cols], c_im[:local_rows, cols]
        rows = np.stack([np.concatenate([real, -imag], 1)[order], np.concatenate([imag, real], 1)[order]], 1)
        return jnp.asarray(rows.reshape(2 * local_rows, -1), bf16)

    column_shape = (2 * local_rows, grid_size)
    columns = kernel_call(
        own_kernel, column_shape, f32, matmul // 2, (table(slice(0, local_rows)), shaped)
    )
    columns, other = lax.optimization_barrier((columns, other))
    columns = kernel_call(
        other_kernel, column_shape, bf16, matmul // 2, (table(slice(local_rows, None)), other, columns)
    )
    blocks = columns.reshape(owners, 2, -1, block_rows, grid_size).transpose(0, 2, 1, 3, 4)
    blocks = blocks.reshape(count, 2 * block_rows, grid_size)
    pixels = lax.all_to_all(blocks, "modes", 0, 0, tiled=True)

    output_fields = kernel_call(
        lambda *refs: fields_kernel(block_rows, *refs),
        (local_rows, double_width),
        bf16,
        matmul,
        (columns, full_re, full_im),
    )
    target_re, target_im = targets.reshape(2, local_rows, grid_size)
    seen = jnp.concatenate(
        [
            times(target_re, full_re) + times(target_im, full_im),
            times(target_im, full_re) - times(target_re, full_im),
        ],
        0,
    ).astype(bf16)
    pixels, output_fields = lax.optimization_barrier((pixels, output_fields))
    term = kernel_call(
        lambda *refs: coupling_kernel(block_rows, *refs),
        (2 * mode_total, mode_total),
        f32,
        matmul,
        (pixels.reshape(column_shape), seen),
    )
    pieces = lax.all_to_all(term, ("modes", "rows"), 0, 0, tiled=True)
    coupling = jnp.sum(pieces, 0, keepdims=True)
    return (phase_plane, output_fields[None], coupling)


def solution(mesh):
    return jax.shard_map(
        local,
        mesh=mesh,
        in_specs=(
            P("modes", "rows", None),
            P("modes", "rows", None),
            P(None, None, ("rows", "modes"), None),
        ),
        out_specs=(P("rows", None), P("modes", "rows", None), P(("modes", "rows"), None)),
        check_vma=False,
    )
```

```python
import numpy as np

import jax
import jax.numpy as jnp
from jax import lax
from jax.experimental import pallas as pl
from jax.experimental.pallas import tpu as pltpu
from jax.sharding import PartitionSpec as P

bf16 = jnp.bfloat16
f32 = jnp.float32


def propagator(grid_size):
    index = np.arange(grid_size)
    centred = (index + grid_size // 2) % grid_size - grid_size // 2
    squared = centred * centred % (4 * grid_size)
    column = np.fft.ifft(np.exp(-2j * np.pi * squared / (4 * grid_size)))
    matrix = column[(index[:, None] - index[None, :]) % grid_size]
    return matrix.real, matrix.imag


def stages(count):
    digits, stride = [], 1
    while count // stride > 4:
        digits.append((stride, 2))
        stride *= 2
    digits.append((stride, count // stride))
    return digits


def exchange(values, offset, count):
    return lax.ppermute(values, "modes", [(i, i ^ offset) for i in range(count)])


def pick(values, index, axis):
    return lax.dynamic_index_in_dim(values, index, axis, keepdims=False)


def reduce_digit(keep, got):
    for g in got:
        keep = keep + g.astype(f32)
    return keep


def gather_digit(block, own, stride, size, axis, count):
    got = [block] + [exchange(block, e * stride, count) for e in range(1, size)]
    stacked = jnp.stack(got, axis)
    if size == 2:
        return jnp.where(own == 0, stacked, jnp.flip(stacked, axis))
    return jnp.stack([pick(stacked, own ^ at, axis) for at in range(size)], axis)


def split_digit(partial, own, size, axis):
    send = [pick(partial, own ^ e, axis).astype(bf16) for e in range(1, size)]
    return send, pick(partial, own, axis)


def product_of(fore, back):
    half = fore.shape[-1] // 2
    fore, back = fore.astype(f32), back.astype(f32)
    fore_re, fore_im = fore[..., :half], fore[..., half:]
    back_re, back_im = back[..., :half], back[..., half:]
    return back_re * fore_re + back_im * fore_im, back_re * fore_im - back_im * fore_re


def products_kernel(rows, fore_hbm, back_hbm, send_a, keep_a, send_b, keep_b, fore_ref, back_ref, sems):
    me = lax.axis_index("modes")
    low, high = me % 2 == 1, me // 2 % 2 == 1
    grid_size = fore_ref.shape[1] // 2
    half = grid_size // 2
    pair = 2 * rows
    groups = fore_ref.shape[0] // (4 * rows)
    copies = []
    for group in range(groups):
        at = pl.ds(group * 4 * rows, 4 * rows)
        for k, (hbm, ref) in enumerate(((fore_hbm, fore_ref), (back_hbm, back_ref))):
            copies.append(pltpu.make_async_copy(hbm.at[at], ref.at[at], sems.at[2 * group + k]))
    for copy in copies:
        copy.start()
    for group in range(groups):
        copies[2 * group].wait()
        copies[2 * group + 1].wait()
        at = pl.ds(group * 4 * rows, 4 * rows)
        out = pl.ds(group * pair, pair)
        for part in range(2):
            cols = [pl.ds(part * half, half), pl.ds(grid_size + part * half, half)]
            fore_re, fore_im = [fore_ref[at, c].astype(f32) for c in cols]
            back_re, back_im = [back_ref[at, c].astype(f32) for c in cols]
            values = (back_re * fore_re + back_im * fore_im, back_re * fore_im - back_im * fore_re)
            for k, v in enumerate(values):
                into = pl.ds(k * half, half)
                if part == 0:
                    first = jnp.concatenate([v[:rows], v[pair : pair + rows]], 0)
                    second = jnp.concatenate([v[rows:pair], v[pair + rows :]], 0)
                    send_a[out, into] = jnp.where(low, first, second).astype(bf16)
                    keep_a[out, into] = jnp.where(low, second, first)
                else:
                    first, second = v[:pair], v[pair:]
                    send_b[out, into] = jnp.where(high, first, second).astype(bf16)
                    keep_b[out, into] = jnp.where(high, second, first)


def times(one, two):
    return jnp.dot(one, two, preferred_element_type=f32)


def own_kernel(table_ref, shaped_ref, out_ref):
    out_ref[...] = times(table_ref[...], shaped_ref[...])


def other_kernel(table_ref, shaped_ref, own_ref, out_hbm, held, sems):
    half, piece = held.shape[0] // 2, held.shape[0] // 8
    copies = []
    for start in (0, half):
        at = pl.ds(start, half)
        held[at] = (own_ref[at] + times(table_ref[at], shaped_ref[...])).astype(bf16)
        for first in range(start, start + half, piece):
            rows = pl.ds(first, piece)
            copies.append(pltpu.make_async_copy(held.at[rows], out_hbm.at[rows], sems.at[len(copies)]))
            copies[-1].start()
    for copy in copies:
        copy.wait()


def fields_kernel(block_rows, columns_ref, re_ref, im_ref, out_ref):
    rows, grid_size = out_ref.shape[0], columns_ref.shape[1]
    by_re, by_im = times(columns_ref[...], re_ref[...]), times(columns_ref[...], im_ref[...])
    if block_rows % 8 == 0:
        step, block = 2 * block_rows, block_rows
    else:
        step, block = rows, rows
    for at in range(0, rows, step):
        pieces = [[], []]
        for start in range(2 * at, 2 * (at + step), 2 * block):
            real, imag = slice(start, start + block), slice(start + block, start + 2 * block)
            pieces[0].append(by_re[real] - by_im[imag])
            pieces[1].append(by_im[real] + by_re[imag])
        for k, piece in enumerate(pieces):
            out = jnp.concatenate(piece, 0).astype(bf16)
            out_ref[pl.ds(at, step), pl.ds(k * grid_size, grid_size)] = out


def targets_kernel(targets_ref, re_ref, im_ref, out_ref):
    rows = targets_ref.shape[0] // 2
    real, imag = targets_ref[:rows], targets_ref[rows:]
    c_re, c_im = re_ref[...], im_ref[...]
    out_ref[:rows] = (times(real, c_re) + times(imag, c_im)).astype(bf16)
    out_ref[rows:] = (times(imag, c_re) - times(real, c_im)).astype(bf16)


def exactly(one, two, dims):
    return lax.dot_general(
        one, two, (dims, ((), ())), precision=lax.Precision.HIGHEST, preferred_element_type=f32
    )


def coupling_kernel(block_rows, fields_ref, targets_ref, out_ref):
    modes = out_ref.shape[1]
    product = lax.dot_general(
        fields_ref[...], targets_ref[...], (((1,), (1,)), ((), ())), preferred_element_type=f32
    )
    left, right = product.shape
    col = lax.broadcasted_iota(jnp.int32, (1, right), 1) % block_rows

    def groups(size):
        member = lax.broadcasted_iota(jnp.int32, (size // block_rows, size), 1) // block_rows
        group = lax.broadcasted_iota(jnp.int32, (size // block_rows, size), 0)
        return jnp.where(member == group, 1.0, 0.0).astype(f32)

    if block_rows % 8 == 0:
        product = product.reshape(left // block_rows, block_rows, right)
        same = lax.broadcasted_iota(jnp.int32, (block_rows, right), 0) == col
        product = jnp.sum(jnp.where(same[None], product, 0.0), 1)
    else:
        same = lax.broadcasted_iota(jnp.int32, (left, 1), 0) % block_rows == col
        product = exactly(groups(left), jnp.where(same, product, 0.0), ((1,), (0,)))
    product = product.reshape(modes, 2, right)
    real, imag = product[:, 0], product[:, 1]
    right = right // 2
    both = jnp.concatenate(
        [real[:, :right] + imag[:, right:], imag[:, :right] - real[:, right:]], 0
    )
    out_ref[...] = exactly(both, groups(right), ((1,), (1,)))


def kernel_call(kernel, shape, dtype, flops, operands, grant=12, **more):
    place = pl.BlockSpec(memory_space=pltpu.VMEM)
    several = isinstance(dtype, list)
    if several:
        out_shape = [jax.ShapeDtypeStruct(s, d) for s, d in zip(shape, dtype)]
    else:
        out_shape = jax.ShapeDtypeStruct(shape, dtype)
    specs = dict(in_specs=[place] * len(operands), out_specs=[place] * len(shape) if several else place)
    return pl.pallas_call(
        kernel,
        out_shape=out_shape,
        compiler_params=pltpu.CompilerParams(vmem_limit_bytes=grant << 20),
        cost_estimate=pl.CostEstimate(flops=flops, bytes_accessed=4 << 20, transcendentals=0),
        **(specs | more),
    )(*operands)


def local(forward, backward, targets):
    modes_here, local_rows, double_width = forward.shape
    grid_size = double_width // 2
    count = lax.axis_size("modes")
    mode_total = modes_here * count
    block_rows = local_rows // count
    digits = stages(count)
    sizes = [size for _, size in reversed(digits)]
    half = grid_size // 2
    matmul = 2 * local_rows * double_width * double_width

    me = lax.axis_index("modes")
    owns = [me // stride % size for stride, size in digits]
    last = len(digits) - 1
    first = list(range(last))
    orders = [first, [1, 0] + first[2:]]
    kernel_first = block_rows % 8 == 0 and local_rows % (4 * block_rows) == 0
    if kernel_first:
        halves = kernel_call(
            lambda *refs: products_kernel(block_rows, *refs),
            [(local_rows // 2, grid_size)] * 4,
            [bf16, f32, bf16, f32],
            8 * local_rows * double_width,
            (forward[0], backward[0]),
            grant=52,
            in_specs=[pl.BlockSpec(memory_space=pltpu.HBM)] * 2,
            scratch_shapes=[pltpu.VMEM((local_rows, double_width), bf16)] * 2
            + [pltpu.SemaphoreType.DMA((2 * local_rows // (4 * block_rows),))],
        )
    else:
        product = product_of(forward[0], backward[0])
    kept = []
    for part, order in enumerate(orders):
        cols = slice(part * half, (part + 1) * half)
        axes = [last - d for d in range(len(digits))]
        if not kernel_first:
            partial = jnp.concatenate([p[:, cols] for p in product], -1)
            partial = partial.reshape(*sizes, block_rows, grid_size)
        for at, d in enumerate(order):
            stride, size = digits[d]
            left = sizes[: axes[d]] + sizes[axes[d] + 1 :] if at == 0 else None
            if at == 0 and kernel_first:
                send = [halves[2 * part].reshape(*left, block_rows, grid_size)]
                keep = halves[2 * part + 1].reshape(*left, block_rows, grid_size)
            else:
                send, keep = split_digit(partial, owns[d], size, axes[d])
            got = [exchange(v, (e + 1) * stride, count) for e, v in enumerate(send)]
            partial = reduce_digit(keep, got)
            axes = [a - (a > axes[d]) for a in axes]
        kept.append(partial)
    stride, size = digits[last]
    send, keep = split_digit(jnp.concatenate(kept, -1), owns[last], size, 0)
    got = [exchange(v, (e + 1) * stride, count) for e, v in enumerate(send)]
    summed = reduce_digit(keep, got)
    parts = []
    for part in range(2):
        over_re = summed[:, part * grid_size : part * grid_size + half]
        over_im = summed[:, part * grid_size + half : (part + 1) * grid_size]
        scale = lax.rsqrt(over_re * over_re + over_im * over_im + mode_total)
        parts += [over_re * scale, over_im * scale]
    block = jnp.concatenate(parts, -1).astype(bf16)

    block = gather_digit(block, owns[last], stride, size, 0, count)
    planes = []
    for part, order in enumerate(orders):
        piece = block[..., part * grid_size : (part + 1) * grid_size]
        done = [last]
        for d in reversed(order):
            axis = sum(1 for other in done if other > d)
            piece = gather_digit(piece, owns[d], *digits[d], axis, count)
            done.append(d)
        planes.append(piece.reshape(local_rows, grid_size))
    plane_re = jnp.concatenate([p[:, :half] for p in planes], -1)
    plane_im = jnp.concatenate([p[:, half:] for p in planes], -1)
    phase_plane = jnp.concatenate([plane_re, plane_im], -1)

    fore = forward[0].astype(f32)
    fore_re, fore_im = fore[:, :grid_size], fore[:, grid_size:]
    plane_re, plane_im = plane_re.astype(f32), plane_im.astype(f32)
    shaped = jnp.concatenate(
        [fore_re * plane_re - fore_im * plane_im, fore_re * plane_im + fore_im * plane_re], 0
    ).astype(bf16)
    other = lax.ppermute(shaped, "rows", [(0, 1), (1, 0)])

    c_re, c_im = propagator(grid_size)
    full_re, full_im = jnp.asarray(c_re, bf16), jnp.asarray(c_im, bf16)
    owners = count if block_rows % 8 == 0 else 1
    order = np.arange(local_rows).reshape(owners, -1)

    def table(cols):
        real, imag = c_re[:local_rows, cols], c_im[:local_rows, cols]
        rows = np.stack([np.concatenate([real, -imag], 1)[order], np.concatenate([imag, real], 1)[order]], 1)
        return jnp.asarray(rows.reshape(2 * local_rows, -1), bf16)

    column_shape = (2 * local_rows, grid_size)
    columns = kernel_call(
        own_kernel, column_shape, f32, matmul // 2, (table(slice(0, local_rows)), shaped)
    )
    columns, other = lax.optimization_barrier((columns, other))
    columns = kernel_call(
        other_kernel, column_shape, bf16, matmul // 2, (table(slice(local_rows, None)), other, columns),
        out_specs=pl.BlockSpec(memory_space=pltpu.HBM),
        scratch_shapes=[pltpu.VMEM(column_shape, bf16), pltpu.SemaphoreType.DMA((8,))],
    )
    blocks = columns.reshape(owners, 2, -1, block_rows, grid_size).transpose(0, 2, 1, 3, 4)
    blocks = blocks.reshape(count, 2 * block_rows, grid_size)
    pixels = lax.all_to_all(blocks, "modes", 0, 0, tiled=True)

    output_fields = kernel_call(
        lambda *refs: fields_kernel(block_rows, *refs),
        (local_rows, double_width),
        bf16,
        matmul,
        (columns, full_re, full_im),
    )
    target_re, target_im = targets.reshape(2, local_rows, grid_size)
    seen = jnp.concatenate(
        [
            times(target_re, full_re) + times(target_im, full_im),
            times(target_im, full_re) - times(target_re, full_im),
        ],
        0,
    ).astype(bf16)
    pixels, output_fields = lax.optimization_barrier((pixels, output_fields))
    term = kernel_call(
        lambda *refs: coupling_kernel(block_rows, *refs),
        (2 * mode_total, mode_total),
        f32,
        matmul,
        (pixels.reshape(column_shape), seen),
    )
    pieces = lax.all_to_all(term, ("modes", "rows"), 0, 0, tiled=True)
    coupling = jnp.sum(pieces, 0, keepdims=True)
    return (phase_plane, output_fields[None], coupling)


def solution(mesh):
    return jax.shard_map(
        local,
        mesh=mesh,
        in_specs=(
            P("modes", "rows", None),
            P("modes", "rows", None),
            P(None, None, ("rows", "modes"), None),
        ),
        out_specs=(P("rows", None), P("modes", "rows", None), P(("modes", "rows"), None)),
        check_vma=False,
    )
```

```python
import numpy as np

import jax
import jax.numpy as jnp
from jax import lax
from jax.experimental import pallas as pl
from jax.experimental.pallas import tpu as pltpu
from jax.sharding import PartitionSpec as P

bf16 = jnp.bfloat16
f32 = jnp.float32


def propagator(grid_size):
    index = np.arange(grid_size)
    centred = (index + grid_size // 2) % grid_size - grid_size // 2
    squared = centred * centred % (4 * grid_size)
    column = np.fft.ifft(np.exp(-2j * np.pi * squared / (4 * grid_size)))
    matrix = column[(index[:, None] - index[None, :]) % grid_size]
    return matrix.real, matrix.imag


def stages(count):
    digits, stride = [], 1
    while count // stride > 4:
        digits.append((stride, 2))
        stride *= 2
    digits.append((stride, count // stride))
    return digits


def exchange(values, offset, count):
    return lax.ppermute(values, "modes", [(i, i ^ offset) for i in range(count)])


def pick(values, index, axis):
    return lax.dynamic_index_in_dim(values, index, axis, keepdims=False)


def reduce_digit(keep, got):
    for g in got:
        keep = keep + g.astype(f32)
    return keep


def gather_digit(block, own, stride, size, axis, count):
    got = [block] + [exchange(block, e * stride, count) for e in range(1, size)]
    stacked = jnp.stack(got, axis)
    if size == 2:
        return jnp.where(own == 0, stacked, jnp.flip(stacked, axis))
    return jnp.stack([pick(stacked, own ^ at, axis) for at in range(size)], axis)


def split_digit(partial, own, size, axis):
    send = [pick(partial, own ^ e, axis).astype(bf16) for e in range(1, size)]
    return send, pick(partial, own, axis)


def product_of(fore, back):
    half = fore.shape[-1] // 2
    fore, back = fore.astype(f32), back.astype(f32)
    fore_re, fore_im = fore[..., :half], fore[..., half:]
    back_re, back_im = back[..., :half], back[..., half:]
    return back_re * fore_re + back_im * fore_im, back_re * fore_im - back_im * fore_re


def products_kernel(rows, fore_hbm, back_hbm, send_a, keep_a, send_b, keep_b, fore_ref, back_ref, sems):
    me = lax.axis_index("modes")
    low, high = me % 2 == 1, me // 2 % 2 == 1
    grid_size = fore_ref.shape[1] // 2
    half = grid_size // 2
    pair = 2 * rows
    groups = fore_ref.shape[0] // (4 * rows)
    copies = []
    for group in range(groups):
        at = pl.ds(group * 4 * rows, 4 * rows)
        for k, (hbm, ref) in enumerate(((fore_hbm, fore_ref), (back_hbm, back_ref))):
            copies.append(pltpu.make_async_copy(hbm.at[at], ref.at[at], sems.at[2 * group + k]))
    for copy in copies:
        copy.start()
    for group in range(groups):
        copies[2 * group].wait()
        copies[2 * group + 1].wait()
        at = pl.ds(group * 4 * rows, 4 * rows)
        out = pl.ds(group * pair, pair)
        for part in range(2):
            cols = [pl.ds(part * half, half), pl.ds(grid_size + part * half, half)]
            fore_re, fore_im = [fore_ref[at, c].astype(f32) for c in cols]
            back_re, back_im = [back_ref[at, c].astype(f32) for c in cols]
            values = (back_re * fore_re + back_im * fore_im, back_re * fore_im - back_im * fore_re)
            for k, v in enumerate(values):
                into = pl.ds(k * half, half)
                if part == 0:
                    first = jnp.concatenate([v[:rows], v[pair : pair + rows]], 0)
                    second = jnp.concatenate([v[rows:pair], v[pair + rows :]], 0)
                    send_a[out, into] = jnp.where(low, first, second).astype(bf16)
                    keep_a[out, into] = jnp.where(low, second, first)
                else:
                    first, second = v[:pair], v[pair:]
                    send_b[out, into] = jnp.where(high, first, second).astype(bf16)
                    keep_b[out, into] = jnp.where(high, second, first)


def times(one, two):
    return jnp.dot(one, two, preferred_element_type=f32)


def own_kernel(table_ref, shaped_ref, out_ref):
    out_ref[...] = times(table_ref[...], shaped_ref[...])


def other_kernel(table_ref, shaped_ref, own_ref, out_hbm, held, sems):
    half, piece = held.shape[0] // 2, held.shape[0] // 8
    copies = []
    for start in (0, half):
        at = pl.ds(start, half)
        held[at] = (own_ref[at] + times(table_ref[at], shaped_ref[...])).astype(bf16)
        for first in range(start, start + half, piece):
            rows = pl.ds(first, piece)
            copies.append(pltpu.make_async_copy(held.at[rows], out_hbm.at[rows], sems.at[len(copies)]))
            copies[-1].start()
    for copy in copies:
        copy.wait()


def fields_kernel(block_rows, columns_ref, re_ref, im_ref, out_ref):
    rows, grid_size = out_ref.shape[0], columns_ref.shape[1]
    by_re, by_im = times(columns_ref[...], re_ref[...]), times(columns_ref[...], im_ref[...])
    if block_rows % 8 == 0:
        step, block = 2 * block_rows, block_rows
    else:
        step, block = rows, rows
    for at in range(0, rows, step):
        pieces = [[], []]
        for start in range(2 * at, 2 * (at + step), 2 * block):
            real, imag = slice(start, start + block), slice(start + block, start + 2 * block)
            pieces[0].append(by_re[real] - by_im[imag])
            pieces[1].append(by_im[real] + by_re[imag])
        for k, piece in enumerate(pieces):
            out = jnp.concatenate(piece, 0).astype(bf16)
            out_ref[pl.ds(at, step), pl.ds(k * grid_size, grid_size)] = out


def targets_kernel(targets_ref, re_ref, im_ref, out_ref):
    rows = targets_ref.shape[0] // 2
    real, imag = targets_ref[:rows], targets_ref[rows:]
    c_re, c_im = re_ref[...], im_ref[...]
    out_ref[:rows] = (times(real, c_re) + times(imag, c_im)).astype(bf16)
    out_ref[rows:] = (times(imag, c_re) - times(real, c_im)).astype(bf16)


def exactly(one, two, dims):
    return lax.dot_general(
        one, two, (dims, ((), ())), precision=lax.Precision.HIGHEST, preferred_element_type=f32
    )


def coupling_kernel(block_rows, fields_ref, targets_ref, out_ref):
    modes = out_ref.shape[2]
    product = lax.dot_general(
        fields_ref[...], targets_ref[...], (((1,), (1,)), ((), ())), preferred_element_type=f32
    )
    left, right = product.shape
    col = lax.broadcasted_iota(jnp.int32, (1, right), 1) % block_rows

    def groups(size):
        member = lax.broadcasted_iota(jnp.int32, (size // block_rows, size), 1) // block_rows
        group = lax.broadcasted_iota(jnp.int32, (size // block_rows, size), 0)
        return jnp.where(member == group, 1.0, 0.0).astype(f32)

    if block_rows % 8 == 0:
        product = product.reshape(left // block_rows, block_rows, right)
        same = lax.broadcasted_iota(jnp.int32, (block_rows, right), 0) == col
        product = jnp.sum(jnp.where(same[None], product, 0.0), 1)
    else:
        same = lax.broadcasted_iota(jnp.int32, (left, 1), 0) % block_rows == col
        product = exactly(groups(left), jnp.where(same, product, 0.0), ((1,), (0,)))
    product = product.reshape(modes, 2, right)
    real, imag = product[:, 0], product[:, 1]
    right = right // 2
    both = jnp.concatenate(
        [real[:, :right] + imag[:, right:], imag[:, :right] - real[:, right:]], 0
    )
    total = exactly(both, groups(right), ((1,), (1,))).reshape(modes, 2, modes)
    out_ref[0], out_ref[1] = total[:, 0], total[:, 1]


def kernel_call(kernel, shape, dtype, flops, operands, grant=12, **more):
    place = pl.BlockSpec(memory_space=pltpu.VMEM)
    several = isinstance(dtype, list)
    if several:
        out_shape = [jax.ShapeDtypeStruct(s, d) for s, d in zip(shape, dtype)]
    else:
        out_shape = jax.ShapeDtypeStruct(shape, dtype)
    specs = dict(in_specs=[place] * len(operands), out_specs=[place] * len(shape) if several else place)
    return pl.pallas_call(
        kernel,
        out_shape=out_shape,
        compiler_params=pltpu.CompilerParams(vmem_limit_bytes=grant << 20),
        cost_estimate=pl.CostEstimate(flops=flops, bytes_accessed=4 << 20, transcendentals=0),
        **(specs | more),
    )(*operands)


def local(forward, backward, targets):
    modes_here, local_rows, double_width = forward.shape
    grid_size = double_width // 2
    count = lax.axis_size("modes")
    mode_total = modes_here * count
    block_rows = local_rows // count
    digits = stages(count)
    sizes = [size for _, size in reversed(digits)]
    half = grid_size // 2
    matmul = 2 * local_rows * double_width * double_width

    me = lax.axis_index("modes")
    owns = [me // stride % size for stride, size in digits]
    last = len(digits) - 1
    first = list(range(last))
    orders = [first, [1, 0] + first[2:]]
    kernel_first = block_rows % 8 == 0 and local_rows % (4 * block_rows) == 0
    if kernel_first:
        halves = kernel_call(
            lambda *refs: products_kernel(block_rows, *refs),
            [(local_rows // 2, grid_size)] * 4,
            [bf16, f32, bf16, f32],
            8 * local_rows * double_width,
            (forward[0], backward[0]),
            grant=52,
            in_specs=[pl.BlockSpec(memory_space=pltpu.HBM)] * 2,
            scratch_shapes=[pltpu.VMEM((local_rows, double_width), bf16)] * 2
            + [pltpu.SemaphoreType.DMA((2 * local_rows // (4 * block_rows),))],
        )
    else:
        product = product_of(forward[0], backward[0])
    kept = []
    for part, order in enumerate(orders):
        cols = slice(part * half, (part + 1) * half)
        axes = [last - d for d in range(len(digits))]
        if not kernel_first:
            partial = jnp.concatenate([p[:, cols] for p in product], -1)
            partial = partial.reshape(*sizes, block_rows, grid_size)
        for at, d in enumerate(order):
            stride, size = digits[d]
            left = sizes[: axes[d]] + sizes[axes[d] + 1 :] if at == 0 else None
            if at == 0 and kernel_first:
                send = [halves[2 * part].reshape(*left, block_rows, grid_size)]
                keep = halves[2 * part + 1].reshape(*left, block_rows, grid_size)
            else:
                send, keep = split_digit(partial, owns[d], size, axes[d])
            got = [exchange(v, (e + 1) * stride, count) for e, v in enumerate(send)]
            partial = reduce_digit(keep, got)
            axes = [a - (a > axes[d]) for a in axes]
        kept.append(partial)
    stride, size = digits[last]
    send, keep = split_digit(jnp.concatenate(kept, -1), owns[last], size, 0)
    got = [exchange(v, (e + 1) * stride, count) for e, v in enumerate(send)]
    summed = reduce_digit(keep, got)
    parts = []
    for part in range(2):
        over_re = summed[:, part * grid_size : part * grid_size + half]
        over_im = summed[:, part * grid_size + half : (part + 1) * grid_size]
        scale = lax.rsqrt(over_re * over_re + over_im * over_im + mode_total)
        parts += [over_re * scale, over_im * scale]
    block = jnp.concatenate(parts, -1).astype(bf16)

    block = gather_digit(block, owns[last], stride, size, 0, count)
    planes = []
    for part, order in enumerate(orders):
        piece = block[..., part * grid_size : (part + 1) * grid_size]
        done = [last]
        for d in reversed(order):
            axis = sum(1 for other in done if other > d)
            piece = gather_digit(piece, owns[d], *digits[d], axis, count)
            done.append(d)
        planes.append(piece.reshape(local_rows, grid_size))
    plane_re = jnp.concatenate([p[:, :half] for p in planes], -1)
    plane_im = jnp.concatenate([p[:, half:] for p in planes], -1)
    phase_plane = jnp.concatenate([plane_re, plane_im], -1)

    fore = forward[0].astype(f32)
    fore_re, fore_im = fore[:, :grid_size], fore[:, grid_size:]
    plane_re, plane_im = plane_re.astype(f32), plane_im.astype(f32)
    shaped = jnp.concatenate(
        [fore_re * plane_re - fore_im * plane_im, fore_re * plane_im + fore_im * plane_re], 0
    ).astype(bf16)
    other = lax.ppermute(shaped, "rows", [(0, 1), (1, 0)])

    c_re, c_im = propagator(grid_size)
    full_re, full_im = jnp.asarray(c_re, bf16), jnp.asarray(c_im, bf16)
    owners = count if block_rows % 8 == 0 else 1
    order = np.arange(local_rows).reshape(owners, -1)

    def table(cols):
        real, imag = c_re[:local_rows, cols], c_im[:local_rows, cols]
        rows = np.stack([np.concatenate([real, -imag], 1)[order], np.concatenate([imag, real], 1)[order]], 1)
        return jnp.asarray(rows.reshape(2 * local_rows, -1), bf16)

    column_shape = (2 * local_rows, grid_size)
    columns = kernel_call(
        own_kernel, column_shape, f32, matmul // 2, (table(slice(0, local_rows)), shaped)
    )
    columns, other = lax.optimization_barrier((columns, other))
    columns = kernel_call(
        other_kernel, column_shape, bf16, matmul // 2, (table(slice(local_rows, None)), other, columns),
        out_specs=pl.BlockSpec(memory_space=pltpu.HBM),
        scratch_shapes=[pltpu.VMEM(column_shape, bf16), pltpu.SemaphoreType.DMA((8,))],
    )
    blocks = columns.reshape(owners, 2, -1, block_rows, grid_size).transpose(0, 2, 1, 3, 4)
    blocks = blocks.reshape(count, 2 * block_rows, grid_size)
    pixels = lax.all_to_all(blocks, "modes", 0, 0, tiled=True)

    output_fields = kernel_call(
        lambda *refs: fields_kernel(block_rows, *refs),
        (local_rows, double_width),
        bf16,
        matmul,
        (columns, full_re, full_im),
    )
    target_re, target_im = targets.reshape(2, local_rows, grid_size)
    seen = jnp.concatenate(
        [
            times(target_re, full_re) + times(target_im, full_im),
            times(target_im, full_re) - times(target_re, full_im),
        ],
        0,
    ).astype(bf16)
    pixels, output_fields = lax.optimization_barrier((pixels, output_fields))
    term = kernel_call(
        lambda *refs: coupling_kernel(block_rows, *refs),
        (2, mode_total, mode_total),
        f32,
        matmul,
        (pixels.reshape(column_shape), seen),
    )
    core = lax.axis_index("rows")
    came = lax.ppermute(pick(term, 1 - core, 0), "rows", [(0, 1), (1, 0)])
    pieces = lax.all_to_all(pick(term, core, 0) + came, "modes", 0, 0, tiled=True)
    coupling = jnp.sum(pieces, 0, keepdims=True)
    return (phase_plane, output_fields[None], coupling)


def solution(mesh):
    return jax.shard_map(
        local,
        mesh=mesh,
        in_specs=(
            P("modes", "rows", None),
            P("modes", "rows", None),
            P(None, None, ("rows", "modes"), None),
        ),
        out_specs=(P("rows", None), P("modes", "rows", None), P(("modes", "rows"), None)),
        check_vma=False,
    )
```

```python
import numpy as np

import jax
import jax.numpy as jnp
from jax import lax
from jax.experimental import pallas as pl
from jax.experimental.pallas import tpu as pltpu
from jax.sharding import PartitionSpec as P

bf16 = jnp.bfloat16
f32 = jnp.float32


def propagator(grid_size):
    index = np.arange(grid_size)
    centred = (index + grid_size // 2) % grid_size - grid_size // 2
    squared = centred * centred % (4 * grid_size)
    column = np.fft.ifft(np.exp(-2j * np.pi * squared / (4 * grid_size)))
    matrix = column[(index[:, None] - index[None, :]) % grid_size]
    return matrix.real, matrix.imag


def stages(count):
    digits, stride = [], 1
    while count // stride > 4:
        digits.append((stride, 2))
        stride *= 2
    digits.append((stride, count // stride))
    return digits


def exchange(values, offset, count):
    return lax.ppermute(values, "modes", [(i, i ^ offset) for i in range(count)])


def pick(values, index, axis):
    return lax.dynamic_index_in_dim(values, index, axis, keepdims=False)


def reduce_digit(keep, got):
    for g in got:
        keep = keep + g.astype(f32)
    return keep


def gather_digit(block, own, stride, size, axis, count):
    got = [block] + [exchange(block, e * stride, count) for e in range(1, size)]
    stacked = jnp.stack(got, axis)
    if size == 2:
        return jnp.where(own == 0, stacked, jnp.flip(stacked, axis))
    return jnp.stack([pick(stacked, own ^ at, axis) for at in range(size)], axis)


def split_digit(partial, own, size, axis):
    send = [pick(partial, own ^ e, axis).astype(bf16) for e in range(1, size)]
    return send, pick(partial, own, axis)


def product_of(fore, back):
    half = fore.shape[-1] // 2
    fore, back = fore.astype(f32), back.astype(f32)
    fore_re, fore_im = fore[..., :half], fore[..., half:]
    back_re, back_im = back[..., :half], back[..., half:]
    return back_re * fore_re + back_im * fore_im, back_re * fore_im - back_im * fore_re


def products_kernel(rows, fore_hbm, back_hbm, send_a, keep_a, send_b, keep_b, fore_ref, back_ref, sems):
    me = lax.axis_index("modes")
    low, high = me % 2 == 1, me // 2 % 2 == 1
    grid_size = fore_ref.shape[1] // 2
    half = grid_size // 2
    pair = 2 * rows
    groups = fore_ref.shape[0] // (4 * rows)
    copies = []
    for group in range(groups):
        at = pl.ds(group * 4 * rows, 4 * rows)
        for k, (hbm, ref) in enumerate(((fore_hbm, fore_ref), (back_hbm, back_ref))):
            copies.append(pltpu.make_async_copy(hbm.at[at], ref.at[at], sems.at[2 * group + k]))
    for copy in copies:
        copy.start()
    for group in range(groups):
        copies[2 * group].wait()
        copies[2 * group + 1].wait()
        at = pl.ds(group * 4 * rows, 4 * rows)
        out = pl.ds(group * pair, pair)
        for part in range(2):
            cols = [pl.ds(part * half, half), pl.ds(grid_size + part * half, half)]
            fore_re, fore_im = [fore_ref[at, c].astype(f32) for c in cols]
            back_re, back_im = [back_ref[at, c].astype(f32) for c in cols]
            values = (back_re * fore_re + back_im * fore_im, back_re * fore_im - back_im * fore_re)
            for k, v in enumerate(values):
                into = pl.ds(k * half, half)
                if part == 0:
                    first = jnp.concatenate([v[:rows], v[pair : pair + rows]], 0)
                    second = jnp.concatenate([v[rows:pair], v[pair + rows :]], 0)
                    send_a[out, into] = jnp.where(low, first, second).astype(bf16)
                    keep_a[out, into] = jnp.where(low, second, first)
                else:
                    first, second = v[:pair], v[pair:]
                    send_b[out, into] = jnp.where(high, first, second).astype(bf16)
                    keep_b[out, into] = jnp.where(high, second, first)


def times(one, two):
    return jnp.dot(one, two, preferred_element_type=f32)


def own_kernel(table_ref, shaped_ref, out_ref):
    out_ref[...] = times(table_ref[...], shaped_ref[...])


def other_kernel(table_ref, shaped_ref, own_ref, out_hbm, held, sems):
    half, piece = held.shape[0] // 2, held.shape[0] // 8
    copies = []
    for start in (0, half):
        at = pl.ds(start, half)
        held[at] = (own_ref[at] + times(table_ref[at], shaped_ref[...])).astype(bf16)
        for first in range(start, start + half, piece):
            rows = pl.ds(first, piece)
            copies.append(pltpu.make_async_copy(held.at[rows], out_hbm.at[rows], sems.at[len(copies)]))
            copies[-1].start()
    for copy in copies:
        copy.wait()


def fields_kernel(block_rows, columns_ref, re_ref, im_ref, out_ref):
    rows, grid_size = out_ref.shape[0], columns_ref.shape[1]
    by_re, by_im = times(columns_ref[...], re_ref[...]), times(columns_ref[...], im_ref[...])
    if block_rows % 8 == 0:
        step, block = 2 * block_rows, block_rows
    else:
        step, block = rows, rows
    for at in range(0, rows, step):
        pieces = [[], []]
        for start in range(2 * at, 2 * (at + step), 2 * block):
            real, imag = slice(start, start + block), slice(start + block, start + 2 * block)
            pieces[0].append(by_re[real] - by_im[imag])
            pieces[1].append(by_im[real] + by_re[imag])
        for k, piece in enumerate(pieces):
            out = jnp.concatenate(piece, 0).astype(bf16)
            out_ref[pl.ds(at, step), pl.ds(k * grid_size, grid_size)] = out


def targets_kernel(targets_ref, re_ref, im_ref, out_ref):
    rows = targets_ref.shape[0] // 2
    real, imag = targets_ref[:rows], targets_ref[rows:]
    c_re, c_im = re_ref[...], im_ref[...]
    out_ref[:rows] = (times(real, c_re) + times(imag, c_im)).astype(bf16)
    out_ref[rows:] = (times(imag, c_re) - times(real, c_im)).astype(bf16)


def exactly(one, two, dims):
    return lax.dot_general(
        one, two, (dims, ((), ())), precision=lax.Precision.HIGHEST, preferred_element_type=f32
    )


def coupling_kernel(block_rows, fields_ref, targets_ref, out_ref):
    modes = out_ref.shape[2]
    product = lax.dot_general(
        fields_ref[...], targets_ref[...], (((1,), (1,)), ((), ())), preferred_element_type=f32
    )
    left, right = product.shape
    col = lax.broadcasted_iota(jnp.int32, (1, right), 1) % block_rows

    def groups(size):
        member = lax.broadcasted_iota(jnp.int32, (size // block_rows, size), 1) // block_rows
        group = lax.broadcasted_iota(jnp.int32, (size // block_rows, size), 0)
        return jnp.where(member == group, 1.0, 0.0).astype(f32)

    if block_rows % 8 == 0:
        product = product.reshape(left // block_rows, block_rows, right)
        same = lax.broadcasted_iota(jnp.int32, (block_rows, right), 0) == col
        product = jnp.sum(jnp.where(same[None], product, 0.0), 1)
    else:
        same = lax.broadcasted_iota(jnp.int32, (left, 1), 0) % block_rows == col
        product = exactly(groups(left), jnp.where(same, product, 0.0), ((1,), (0,)))
    product = product.reshape(modes, 2, right)
    real, imag = product[:, 0], product[:, 1]
    right = right // 2
    both = jnp.concatenate(
        [real[:, :right] + imag[:, right:], imag[:, :right] - real[:, right:]], 0
    )
    total = exactly(both, groups(right), ((1,), (1,))).reshape(modes, 2, modes)
    out_ref[0], out_ref[1] = total[:, 0], total[:, 1]


def kernel_call(kernel, shape, dtype, flops, operands, grant=12, **more):
    place = pl.BlockSpec(memory_space=pltpu.VMEM)
    several = isinstance(dtype, list)
    if several:
        out_shape = [jax.ShapeDtypeStruct(s, d) for s, d in zip(shape, dtype)]
    else:
        out_shape = jax.ShapeDtypeStruct(shape, dtype)
    specs = dict(in_specs=[place] * len(operands), out_specs=[place] * len(shape) if several else place)
    return pl.pallas_call(
        kernel,
        out_shape=out_shape,
        compiler_params=pltpu.CompilerParams(vmem_limit_bytes=grant << 20),
        cost_estimate=pl.CostEstimate(flops=flops, bytes_accessed=4 << 20, transcendentals=0),
        **(specs | more),
    )(*operands)


def local(forward, backward, targets):
    modes_here, local_rows, double_width = forward.shape
    grid_size = double_width // 2
    count = lax.axis_size("modes")
    mode_total = modes_here * count
    block_rows = local_rows // count
    digits = stages(count)
    sizes = [size for _, size in reversed(digits)]
    half = grid_size // 2
    matmul = 2 * local_rows * double_width * double_width

    me = lax.axis_index("modes")
    owns = [me // stride % size for stride, size in digits]
    last = len(digits) - 1
    first = list(range(last))
    orders = [first, [1, 0] + first[2:]]
    kernel_first = block_rows % 8 == 0 and local_rows % (4 * block_rows) == 0
    if kernel_first:
        halves = kernel_call(
            lambda *refs: products_kernel(block_rows, *refs),
            [(local_rows // 2, grid_size)] * 4,
            [bf16, f32, bf16, f32],
            8 * local_rows * double_width,
            (forward[0], backward[0]),
            grant=52,
            in_specs=[pl.BlockSpec(memory_space=pltpu.HBM)] * 2,
            scratch_shapes=[pltpu.VMEM((local_rows, double_width), bf16)] * 2
            + [pltpu.SemaphoreType.DMA((2 * local_rows // (4 * block_rows),))],
        )
    else:
        product = product_of(forward[0], backward[0])
    kept = []
    for part, order in enumerate(orders):
        cols = slice(part * half, (part + 1) * half)
        axes = [last - d for d in range(len(digits))]
        if not kernel_first:
            partial = jnp.concatenate([p[:, cols] for p in product], -1)
            partial = partial.reshape(*sizes, block_rows, grid_size)
        for at, d in enumerate(order):
            stride, size = digits[d]
            left = sizes[: axes[d]] + sizes[axes[d] + 1 :] if at == 0 else None
            if at == 0 and kernel_first:
                send = [halves[2 * part].reshape(*left, block_rows, grid_size)]
                keep = halves[2 * part + 1].reshape(*left, block_rows, grid_size)
            else:
                send, keep = split_digit(partial, owns[d], size, axes[d])
            got = [exchange(v, (e + 1) * stride, count) for e, v in enumerate(send)]
            partial = reduce_digit(keep, got)
            axes = [a - (a > axes[d]) for a in axes]
        kept.append(partial)
    stride, size = digits[last]
    send, keep = split_digit(jnp.concatenate(kept, -1), owns[last], size, 0)
    got = [exchange(v, (e + 1) * stride, count) for e, v in enumerate(send)]
    summed = reduce_digit(keep, got)
    parts = []
    for part in range(2):
        over_re = summed[:, part * grid_size : part * grid_size + half]
        over_im = summed[:, part * grid_size + half : (part + 1) * grid_size]
        scale = lax.rsqrt(over_re * over_re + over_im * over_im + mode_total)
        parts += [over_re * scale, over_im * scale]
    block = jnp.concatenate(parts, -1).astype(bf16)

    block = gather_digit(block, owns[last], stride, size, 0, count)
    planes = []
    for part, order in enumerate(orders):
        piece = block[..., part * grid_size : (part + 1) * grid_size]
        done = [last]
        for d in reversed(order):
            axis = sum(1 for other in done if other > d)
            piece = gather_digit(piece, owns[d], *digits[d], axis, count)
            done.append(d)
        planes.append(piece.reshape(local_rows, grid_size))
    plane_re = jnp.concatenate([p[:, :half] for p in planes], -1)
    plane_im = jnp.concatenate([p[:, half:] for p in planes], -1)
    phase_plane = jnp.concatenate([plane_re, plane_im], -1)

    fore = forward[0].astype(f32)
    fore_re, fore_im = fore[:, :grid_size], fore[:, grid_size:]
    plane_re, plane_im = plane_re.astype(f32), plane_im.astype(f32)
    shaped = jnp.concatenate(
        [fore_re * plane_re - fore_im * plane_im, fore_re * plane_im + fore_im * plane_re], 0
    ).astype(bf16)
    other = lax.ppermute(shaped, "rows", [(0, 1), (1, 0)])

    c_re, c_im = propagator(grid_size)
    full_re, full_im = jnp.asarray(c_re, bf16), jnp.asarray(c_im, bf16)
    owners = count if block_rows % 8 == 0 else 1
    order = np.arange(local_rows).reshape(owners, -1)

    def table(cols):
        real, imag = c_re[:local_rows, cols], c_im[:local_rows, cols]
        rows = np.stack([np.concatenate([real, -imag], 1)[order], np.concatenate([imag, real], 1)[order]], 1)
        return jnp.asarray(rows.reshape(2 * local_rows, -1), bf16)

    column_shape = (2 * local_rows, grid_size)
    columns = kernel_call(
        own_kernel, column_shape, f32, matmul // 2, (table(slice(0, local_rows)), shaped)
    )
    columns, other = lax.optimization_barrier((columns, other))
    columns = kernel_call(
        other_kernel, column_shape, bf16, matmul // 2, (table(slice(local_rows, None)), other, columns),
        out_specs=pl.BlockSpec(memory_space=pltpu.HBM),
        scratch_shapes=[pltpu.VMEM(column_shape, bf16), pltpu.SemaphoreType.DMA((8,))],
    )
    blocks = columns.reshape(owners, 2, -1, block_rows, grid_size).transpose(0, 2, 1, 3, 4)
    blocks = blocks.reshape(count, 2 * block_rows, grid_size)
    pixels = lax.all_to_all(blocks, "modes", 0, 0, tiled=True)

    output_fields = kernel_call(
        lambda *refs: fields_kernel(block_rows, *refs),
        (local_rows, double_width),
        bf16,
        matmul,
        (columns, full_re, full_im),
    )
    target_re, target_im = targets.reshape(2, local_rows, grid_size)
    seen = jnp.concatenate(
        [
            times(target_re, full_re) + times(target_im, full_im),
            times(target_im, full_re) - times(target_re, full_im),
        ],
        0,
    ).astype(bf16)
    pixels, output_fields, phase_plane = lax.optimization_barrier((pixels, output_fields, phase_plane))
    term = kernel_call(
        lambda *refs: coupling_kernel(block_rows, *refs),
        (2, mode_total, mode_total),
        f32,
        matmul,
        (pixels.reshape(column_shape), seen),
    )
    core = lax.axis_index("rows")
    total = pick(term, core, 0) + lax.ppermute(pick(term, 1 - core, 0), "rows", [(0, 1), (1, 0)])
    stride = count
    while stride > 1:
        stride //= 2
        own = me // stride % 2
        total = total.reshape(2, -1, mode_total)
        total = pick(total, own, 0) + exchange(pick(total, 1 - own, 0), stride, count)
    coupling = total.reshape(1, mode_total)
    return (phase_plane, output_fields[None], coupling)


def solution(mesh):
    return jax.shard_map(
        local,
        mesh=mesh,
        in_specs=(
            P("modes", "rows", None),
            P("modes", "rows", None),
            P(None, None, ("rows", "modes"), None),
        ),
        out_specs=(P("rows", None), P("modes", "rows", None), P(("modes", "rows"), None)),
        check_vma=False,
    )
```

```python
import numpy as np

import jax
import jax.numpy as jnp
from jax import lax
from jax.experimental import pallas as pl
from jax.experimental.pallas import tpu as pltpu
from jax.sharding import PartitionSpec as P

bf16 = jnp.bfloat16
f32 = jnp.float32


def propagator(grid_size):
    index = np.arange(grid_size)
    centred = (index + grid_size // 2) % grid_size - grid_size // 2
    squared = centred * centred % (4 * grid_size)
    column = np.fft.ifft(np.exp(-2j * np.pi * squared / (4 * grid_size)))
    matrix = column[(index[:, None] - index[None, :]) % grid_size]
    return matrix.real, matrix.imag


def stages(count):
    digits, stride = [], 1
    while count // stride > 4:
        digits.append((stride, 2))
        stride *= 2
    digits.append((stride, count // stride))
    return digits


def exchange(values, offset, count):
    return lax.ppermute(values, "modes", [(i, i ^ offset) for i in range(count)])


def pick(values, index, axis):
    return lax.dynamic_index_in_dim(values, index, axis, keepdims=False)


def reduce_digit(keep, got):
    for g in got:
        keep = keep + g.astype(f32)
    return keep


def gather_digit(block, own, stride, size, axis, count):
    got = [block] + [exchange(block, e * stride, count) for e in range(1, size)]
    stacked = jnp.stack(got, axis)
    if size == 2:
        return jnp.where(own == 0, stacked, jnp.flip(stacked, axis))
    return jnp.stack([pick(stacked, own ^ at, axis) for at in range(size)], axis)


def split_digit(partial, own, size, axis):
    send = [pick(partial, own ^ e, axis).astype(bf16) for e in range(1, size)]
    return send, pick(partial, own, axis)


def product_of(fore, back):
    half = fore.shape[-1] // 2
    fore, back = fore.astype(f32), back.astype(f32)
    fore_re, fore_im = fore[..., :half], fore[..., half:]
    back_re, back_im = back[..., :half], back[..., half:]
    return back_re * fore_re + back_im * fore_im, back_re * fore_im - back_im * fore_re


def products_kernel(rows, fore_hbm, back_hbm, send_a, keep_a, send_b, keep_b, fore_ref, back_ref, sems):
    me = lax.axis_index("modes")
    low, high = me % 2 == 1, me // 2 % 2 == 1
    grid_size = fore_ref.shape[1] // 2
    half = grid_size // 2
    pair = 2 * rows
    groups = fore_ref.shape[0] // (4 * rows)
    copies = []
    for group in range(groups):
        at = pl.ds(group * 4 * rows, 4 * rows)
        for k, (hbm, ref) in enumerate(((fore_hbm, fore_ref), (back_hbm, back_ref))):
            copies.append(pltpu.make_async_copy(hbm.at[at], ref.at[at], sems.at[2 * group + k]))
    for copy in copies:
        copy.start()
    for group in range(groups):
        copies[2 * group].wait()
        copies[2 * group + 1].wait()
        at = pl.ds(group * 4 * rows, 4 * rows)
        out = pl.ds(group * pair, pair)
        for part in range(2):
            cols = [pl.ds(part * half, half), pl.ds(grid_size + part * half, half)]
            fore_re, fore_im = [fore_ref[at, c].astype(f32) for c in cols]
            back_re, back_im = [back_ref[at, c].astype(f32) for c in cols]
            values = (back_re * fore_re + back_im * fore_im, back_re * fore_im - back_im * fore_re)
            for k, v in enumerate(values):
                into = pl.ds(k * half, half)
                if part == 0:
                    first = jnp.concatenate([v[:rows], v[pair : pair + rows]], 0)
                    second = jnp.concatenate([v[rows:pair], v[pair + rows :]], 0)
                    send_a[out, into] = jnp.where(low, first, second).astype(bf16)
                    keep_a[out, into] = jnp.where(low, second, first)
                else:
                    first, second = v[:pair], v[pair:]
                    send_b[out, into] = jnp.where(high, first, second).astype(bf16)
                    keep_b[out, into] = jnp.where(high, second, first)


def times(one, two):
    return jnp.dot(one, two, preferred_element_type=f32)


def own_kernel(table_ref, first_ref, second_ref, out_ref):
    half = first_ref.shape[1]
    out_ref[:, :half] = times(table_ref[...], first_ref[...])
    out_ref[:, half:] = times(table_ref[...], second_ref[...])


def other_kernel(table_ref, first_ref, second_ref, own_ref, out_ref):
    half = first_ref.shape[1]
    out_ref[:, :half] = (own_ref[:, :half] + times(table_ref[...], first_ref[...])).astype(bf16)
    out_ref[:, half:] = (own_ref[:, half:] + times(table_ref[...], second_ref[...])).astype(bf16)


def fields_kernel(block_rows, columns_ref, re_ref, im_ref, out_ref):
    rows, grid_size = out_ref.shape[0], columns_ref.shape[1]
    by_re, by_im = times(columns_ref[...], re_ref[...]), times(columns_ref[...], im_ref[...])
    if block_rows % 8 == 0:
        step, block = 2 * block_rows, block_rows
    else:
        step, block = rows, rows
    for at in range(0, rows, step):
        pieces = [[], []]
        for start in range(2 * at, 2 * (at + step), 2 * block):
            real, imag = slice(start, start + block), slice(start + block, start + 2 * block)
            pieces[0].append(by_re[real] - by_im[imag])
            pieces[1].append(by_im[real] + by_re[imag])
        for k, piece in enumerate(pieces):
            out = jnp.concatenate(piece, 0).astype(bf16)
            out_ref[pl.ds(at, step), pl.ds(k * grid_size, grid_size)] = out


def targets_kernel(targets_ref, re_ref, im_ref, out_ref):
    rows = targets_ref.shape[0] // 2
    real, imag = targets_ref[:rows], targets_ref[rows:]
    c_re, c_im = re_ref[...], im_ref[...]
    out_ref[:rows] = (times(real, c_re) + times(imag, c_im)).astype(bf16)
    out_ref[rows:] = (times(imag, c_re) - times(real, c_im)).astype(bf16)


def exactly(one, two, dims):
    return lax.dot_general(
        one, two, (dims, ((), ())), precision=lax.Precision.HIGHEST, preferred_element_type=f32
    )


def coupling_kernel(block_rows, fields_ref, targets_ref, out_ref):
    modes = out_ref.shape[1]
    product = lax.dot_general(
        fields_ref[...], targets_ref[...], (((1,), (1,)), ((), ())), preferred_element_type=f32
    )
    left, right = product.shape
    row = lax.broadcasted_iota(jnp.int32, (left, right), 0) % block_rows
    col = lax.broadcasted_iota(jnp.int32, (left, right), 1) % block_rows
    product = jnp.where(row == col, product, 0.0)

    def groups(size):
        member = lax.broadcasted_iota(jnp.int32, (size // block_rows, size), 1) // block_rows
        group = lax.broadcasted_iota(jnp.int32, (size // block_rows, size), 0)
        return jnp.where(member == group, 1.0, 0.0).astype(f32)

    if block_rows % 8 == 0:
        product = jnp.sum(product.reshape(left // block_rows, block_rows, right), 1)
    else:
        product = exactly(groups(left), product, ((1,), (0,)))
    product = product.reshape(modes, 2, right)
    real, imag = product[:, 0], product[:, 1]
    right = right // 2
    both = jnp.concatenate(
        [real[:, :right] + imag[:, right:], imag[:, :right] - real[:, right:]], 0
    )
    out_ref[...] = exactly(both, groups(right), ((1,), (1,)))


def kernel_call(kernel, shape, dtype, flops, operands, grant=12, **more):
    place = pl.BlockSpec(memory_space=pltpu.VMEM)
    several = isinstance(dtype, list)
    if several:
        out_shape = [jax.ShapeDtypeStruct(s, d) for s, d in zip(shape, dtype)]
    else:
        out_shape = jax.ShapeDtypeStruct(shape, dtype)
    specs = dict(in_specs=[place] * len(operands), out_specs=[place] * len(shape) if several else place)
    return pl.pallas_call(
        kernel,
        out_shape=out_shape,
        compiler_params=pltpu.CompilerParams(vmem_limit_bytes=grant << 20),
        cost_estimate=pl.CostEstimate(flops=flops, bytes_accessed=4 << 20, transcendentals=0),
        **(specs | more),
    )(*operands)


def local(forward, backward, targets):
    modes_here, local_rows, double_width = forward.shape
    grid_size = double_width // 2
    count = lax.axis_size("modes")
    mode_total = modes_here * count
    block_rows = local_rows // count
    digits = stages(count)
    sizes = [size for _, size in reversed(digits)]
    half = grid_size // 2
    matmul = 2 * local_rows * double_width * double_width

    me = lax.axis_index("modes")
    owns = [me // stride % size for stride, size in digits]
    last = len(digits) - 1
    first = list(range(last))
    orders = [first, [1, 0] + first[2:]]
    kernel_first = block_rows % 8 == 0 and local_rows % (4 * block_rows) == 0
    if kernel_first:
        halves = kernel_call(
            lambda *refs: products_kernel(block_rows, *refs),
            [(local_rows // 2, grid_size)] * 4,
            [bf16, f32, bf16, f32],
            8 * local_rows * double_width,
            (forward[0], backward[0]),
            grant=52,
            in_specs=[pl.BlockSpec(memory_space=pltpu.HBM)] * 2,
            scratch_shapes=[pltpu.VMEM((local_rows, double_width), bf16)] * 2
            + [pltpu.SemaphoreType.DMA((2 * local_rows // (4 * block_rows),))],
        )
    else:
        product = product_of(forward[0], backward[0])
    kept = []
    for part, order in enumerate(orders):
        cols = slice(part * half, (part + 1) * half)
        axes = [last - d for d in range(len(digits))]
        if not kernel_first:
            partial = jnp.concatenate([p[:, cols] for p in product], -1)
            partial = partial.reshape(*sizes, block_rows, grid_size)
        for at, d in enumerate(order):
            stride, size = digits[d]
            left = sizes[: axes[d]] + sizes[axes[d] + 1 :] if at == 0 else None
            if at == 0 and kernel_first:
                send = [halves[2 * part].reshape(*left, block_rows, grid_size)]
                keep = halves[2 * part + 1].reshape(*left, block_rows, grid_size)
            else:
                send, keep = split_digit(partial, owns[d], size, axes[d])
            got = [exchange(v, (e + 1) * stride, count) for e, v in enumerate(send)]
            partial = reduce_digit(keep, got)
            axes = [a - (a > axes[d]) for a in axes]
        kept.append(partial)
    stride, size = digits[last]
    send, keep = split_digit(jnp.concatenate(kept, -1), owns[last], size, 0)
    got = [exchange(v, (e + 1) * stride, count) for e, v in enumerate(send)]
    summed = reduce_digit(keep, got)
    parts = []
    for part in range(2):
        over_re = summed[:, part * grid_size : part * grid_size + half]
        over_im = summed[:, part * grid_size + half : (part + 1) * grid_size]
        scale = lax.rsqrt(over_re * over_re + over_im * over_im + mode_total)
        parts += [over_re * scale, over_im * scale]
    block = jnp.concatenate(parts, -1).astype(bf16)

    block = gather_digit(block, owns[last], stride, size, 0, count)
    planes = []
    for part, order in enumerate(orders):
        piece = block[..., part * grid_size : (part + 1) * grid_size]
        done = [last]
        for d in reversed(order):
            axis = sum(1 for other in done if other > d)
            piece = gather_digit(piece, owns[d], *digits[d], axis, count)
            done.append(d)
        planes.append(piece.reshape(local_rows, grid_size))
    plane_re = jnp.concatenate([p[:, :half] for p in planes], -1)
    plane_im = jnp.concatenate([p[:, half:] for p in planes], -1)
    phase_plane = jnp.concatenate([plane_re, plane_im], -1)

    fore = forward[0].astype(f32)
    fore_re, fore_im = fore[:, :grid_size], fore[:, grid_size:]
    shaped = []
    for part, plane in enumerate(planes):
        cols = slice(part * half, (part + 1) * half)
        real, imag = plane[:, :half].astype(f32), plane[:, half:].astype(f32)
        from_re, from_im = fore_re[:, cols], fore_im[:, cols]
        rows = [from_re * real - from_im * imag, from_re * imag + from_im * real]
        shaped.append(jnp.concatenate(rows, 0).astype(bf16))
    other = [lax.ppermute(s, "rows", [(0, 1), (1, 0)]) for s in shaped]

    c_re, c_im = propagator(grid_size)
    full_re, full_im = jnp.asarray(c_re, bf16), jnp.asarray(c_im, bf16)
    owners = count if block_rows % 8 == 0 else 1
    order = np.arange(local_rows).reshape(owners, -1)

    def table(cols):
        real, imag = c_re[:local_rows, cols], c_im[:local_rows, cols]
        rows = np.stack([np.concatenate([real, -imag], 1)[order], np.concatenate([imag, real], 1)[order]], 1)
        return jnp.asarray(rows.reshape(2 * local_rows, -1), bf16)

    column_shape = (2 * local_rows, grid_size)
    columns = kernel_call(
        own_kernel, column_shape, f32, matmul // 2, (table(slice(0, local_rows)), *shaped)
    )
    columns, *other = lax.optimization_barrier((columns, *other))
    columns = kernel_call(
        other_kernel, column_shape, bf16, matmul // 2, (table(slice(local_rows, None)), *other, columns)
    )
    blocks = columns.reshape(owners, 2, -1, block_rows, grid_size).transpose(0, 2, 1, 3, 4)
    blocks = blocks.reshape(count, 2 * block_rows, grid_size)
    pixels = lax.all_to_all(blocks, "modes", 0, 0, tiled=True)

    output_fields = kernel_call(
        lambda *refs: fields_kernel(block_rows, *refs),
        (local_rows, double_width),
        bf16,
        matmul,
        (columns, full_re, full_im),
    )
    target_re, target_im = targets.reshape(2, local_rows, grid_size)
    seen = jnp.concatenate(
        [
            times(target_re, full_re) + times(target_im, full_im),
            times(target_im, full_re) - times(target_re, full_im),
        ],
        0,
    ).astype(bf16)
    pixels, output_fields = lax.optimization_barrier((pixels, output_fields))
    term = kernel_call(
        lambda *refs: coupling_kernel(block_rows, *refs),
        (2 * mode_total, mode_total),
        f32,
        matmul,
        (pixels.reshape(column_shape), seen),
    )
    pieces = lax.all_to_all(term, ("modes", "rows"), 0, 0, tiled=True)
    coupling = jnp.sum(pieces, 0, keepdims=True)
    return (phase_plane, output_fields[None], coupling)


def solution(mesh):
    return jax.shard_map(
        local,
        mesh=mesh,
        in_specs=(
            P("modes", "rows", None),
            P("modes", "rows", None),
            P(None, None, ("rows", "modes"), None),
        ),
        out_specs=(P("rows", None), P("modes", "rows", None), P(("modes", "rows"), None)),
        check_vma=False,
    )
```

```python
import numpy as np

import jax
import jax.numpy as jnp
from jax import lax
from jax.experimental import pallas as pl
from jax.experimental.pallas import tpu as pltpu
from jax.sharding import PartitionSpec as P

bf16 = jnp.bfloat16
f32 = jnp.float32


def propagator(grid_size):
    index = np.arange(grid_size)
    centred = (index + grid_size // 2) % grid_size - grid_size // 2
    squared = centred * centred % (4 * grid_size)
    column = np.fft.ifft(np.exp(-2j * np.pi * squared / (4 * grid_size)))
    matrix = column[(index[:, None] - index[None, :]) % grid_size]
    return matrix.real, matrix.imag


def stages(count):
    digits, stride = [], 1
    while count // stride > 4:
        digits.append((stride, 2))
        stride *= 2
    digits.append((stride, count // stride))
    return digits


def exchange(values, offset, count):
    return lax.ppermute(values, "modes", [(i, i ^ offset) for i in range(count)])


def pick(values, index, axis):
    return lax.dynamic_index_in_dim(values, index, axis, keepdims=False)


def reduce_digit(keep, got):
    for g in got:
        keep = keep + g.astype(f32)
    return keep


def gather_digit(block, own, stride, size, axis, count):
    got = [block] + [exchange(block, e * stride, count) for e in range(1, size)]
    stacked = jnp.stack(got, axis)
    if size == 2:
        return jnp.where(own == 0, stacked, jnp.flip(stacked, axis))
    return jnp.stack([pick(stacked, own ^ at, axis) for at in range(size)], axis)


def split_digit(partial, own, size, axis):
    send = [pick(partial, own ^ e, axis).astype(bf16) for e in range(1, size)]
    return send, pick(partial, own, axis)


def product_of(fore, back):
    half = fore.shape[-1] // 2
    fore, back = fore.astype(f32), back.astype(f32)
    fore_re, fore_im = fore[..., :half], fore[..., half:]
    back_re, back_im = back[..., :half], back[..., half:]
    return back_re * fore_re + back_im * fore_im, back_re * fore_im - back_im * fore_re


def products_kernel(rows, fore_hbm, back_hbm, send_a, keep_a, send_b, keep_b, fore_ref, back_ref, sems):
    me = lax.axis_index("modes")
    low, high = me % 2 == 1, me // 2 % 2 == 1
    grid_size = fore_ref.shape[1] // 2
    half = grid_size // 2
    pair = 2 * rows
    groups = fore_ref.shape[0] // (4 * rows)
    copies = []
    for group in range(groups):
        at = pl.ds(group * 4 * rows, 4 * rows)
        for k, (hbm, ref) in enumerate(((fore_hbm, fore_ref), (back_hbm, back_ref))):
            copies.append(pltpu.make_async_copy(hbm.at[at], ref.at[at], sems.at[2 * group + k]))
    for copy in copies:
        copy.start()
    for group in range(groups):
        copies[2 * group].wait()
        copies[2 * group + 1].wait()
        at = pl.ds(group * 4 * rows, 4 * rows)
        out = pl.ds(group * pair, pair)
        for part in range(2):
            cols = [pl.ds(part * half, half), pl.ds(grid_size + part * half, half)]
            fore_re, fore_im = [fore_ref[at, c].astype(f32) for c in cols]
            back_re, back_im = [back_ref[at, c].astype(f32) for c in cols]
            values = (back_re * fore_re + back_im * fore_im, back_re * fore_im - back_im * fore_re)
            for k, v in enumerate(values):
                into = pl.ds(k * half, half)
                if part == 0:
                    first = jnp.concatenate([v[:rows], v[pair : pair + rows]], 0)
                    second = jnp.concatenate([v[rows:pair], v[pair + rows :]], 0)
                    send_a[out, into] = jnp.where(low, first, second).astype(bf16)
                    keep_a[out, into] = jnp.where(low, second, first)
                else:
                    first, second = v[:pair], v[pair:]
                    send_b[out, into] = jnp.where(high, first, second).astype(bf16)
                    keep_b[out, into] = jnp.where(high, second, first)


def times(one, two):
    return jnp.dot(one, two, preferred_element_type=f32)


def own_kernel(table_ref, first_ref, second_ref, out_ref):
    half = first_ref.shape[1]
    out_ref[:, :half] = times(table_ref[...], first_ref[...])
    out_ref[:, half:] = times(table_ref[...], second_ref[...])


def other_kernel(table_ref, first_ref, second_ref, own_ref, out_ref):
    half = first_ref.shape[1]
    out_ref[:, :half] = (own_ref[:, :half] + times(table_ref[...], first_ref[...])).astype(bf16)
    out_ref[:, half:] = (own_ref[:, half:] + times(table_ref[...], second_ref[...])).astype(bf16)


def fields_kernel(block_rows, columns_ref, re_ref, im_ref, out_ref):
    rows, grid_size = out_ref.shape[0], columns_ref.shape[1]
    by_re, by_im = times(columns_ref[...], re_ref[...]), times(columns_ref[...], im_ref[...])
    if block_rows % 8 == 0:
        step, block = 2 * block_rows, block_rows
    else:
        step, block = rows, rows
    for at in range(0, rows, step):
        pieces = [[], []]
        for start in range(2 * at, 2 * (at + step), 2 * block):
            real, imag = slice(start, start + block), slice(start + block, start + 2 * block)
            pieces[0].append(by_re[real] - by_im[imag])
            pieces[1].append(by_im[real] + by_re[imag])
        for k, piece in enumerate(pieces):
            out = jnp.concatenate(piece, 0).astype(bf16)
            out_ref[pl.ds(at, step), pl.ds(k * grid_size, grid_size)] = out


def targets_kernel(targets_ref, re_ref, im_ref, out_ref):
    rows = targets_ref.shape[0] // 2
    real, imag = targets_ref[:rows], targets_ref[rows:]
    c_re, c_im = re_ref[...], im_ref[...]
    out_ref[:rows] = (times(real, c_re) + times(imag, c_im)).astype(bf16)
    out_ref[rows:] = (times(imag, c_re) - times(real, c_im)).astype(bf16)


def exactly(one, two, dims):
    return lax.dot_general(
        one, two, (dims, ((), ())), precision=lax.Precision.HIGHEST, preferred_element_type=f32
    )


def coupling_kernel(block_rows, fields_ref, targets_ref, out_ref):
    modes = out_ref.shape[1]
    product = lax.dot_general(
        fields_ref[...], targets_ref[...], (((1,), (1,)), ((), ())), preferred_element_type=f32
    )
    left, right = product.shape
    row = lax.broadcasted_iota(jnp.int32, (left, right), 0) % block_rows
    col = lax.broadcasted_iota(jnp.int32, (left, right), 1) % block_rows
    product = jnp.where(row == col, product, 0.0)

    def groups(size):
        member = lax.broadcasted_iota(jnp.int32, (size // block_rows, size), 1) // block_rows
        group = lax.broadcasted_iota(jnp.int32, (size // block_rows, size), 0)
        return jnp.where(member == group, 1.0, 0.0).astype(f32)

    if block_rows % 8 == 0:
        product = jnp.sum(product.reshape(left // block_rows, block_rows, right), 1)
    else:
        product = exactly(groups(left), product, ((1,), (0,)))
    product = product.reshape(modes, 2, right)
    real, imag = product[:, 0], product[:, 1]
    right = right // 2
    both = jnp.concatenate(
        [real[:, :right] + imag[:, right:], imag[:, :right] - real[:, right:]], 0
    )
    out_ref[...] = exactly(both, groups(right), ((1,), (1,)))


def kernel_call(kernel, shape, dtype, flops, operands, grant=12, **more):
    place = pl.BlockSpec(memory_space=pltpu.VMEM)
    several = isinstance(dtype, list)
    if several:
        out_shape = [jax.ShapeDtypeStruct(s, d) for s, d in zip(shape, dtype)]
    else:
        out_shape = jax.ShapeDtypeStruct(shape, dtype)
    specs = dict(in_specs=[place] * len(operands), out_specs=[place] * len(shape) if several else place)
    return pl.pallas_call(
        kernel,
        out_shape=out_shape,
        compiler_params=pltpu.CompilerParams(vmem_limit_bytes=grant << 20),
        cost_estimate=pl.CostEstimate(flops=flops, bytes_accessed=4 << 20, transcendentals=0),
        **(specs | more),
    )(*operands)


def local(forward, backward, targets):
    modes_here, local_rows, double_width = forward.shape
    grid_size = double_width // 2
    count = lax.axis_size("modes")
    mode_total = modes_here * count
    block_rows = local_rows // count
    digits = stages(count)
    sizes = [size for _, size in reversed(digits)]
    half = grid_size // 2
    matmul = 2 * local_rows * double_width * double_width

    me = lax.axis_index("modes")
    owns = [me // stride % size for stride, size in digits]
    last = len(digits) - 1
    first = list(range(last))
    orders = [first, [1, 0] + first[2:]]
    kernel_first = block_rows % 8 == 0 and local_rows % (4 * block_rows) == 0
    if kernel_first:
        halves = kernel_call(
            lambda *refs: products_kernel(block_rows, *refs),
            [(local_rows // 2, grid_size)] * 4,
            [bf16, f32, bf16, f32],
            8 * local_rows * double_width,
            (forward[0], backward[0]),
            grant=52,
            in_specs=[pl.BlockSpec(memory_space=pltpu.HBM)] * 2,
            scratch_shapes=[pltpu.VMEM((local_rows, double_width), bf16)] * 2
            + [pltpu.SemaphoreType.DMA((2 * local_rows // (4 * block_rows),))],
        )
    else:
        product = product_of(forward[0], backward[0])
    kept = []
    for part, order in enumerate(orders):
        cols = slice(part * half, (part + 1) * half)
        axes = [last - d for d in range(len(digits))]
        if not kernel_first:
            partial = jnp.concatenate([p[:, cols] for p in product], -1)
            partial = partial.reshape(*sizes, block_rows, grid_size)
        for at, d in enumerate(order):
            stride, size = digits[d]
            left = sizes[: axes[d]] + sizes[axes[d] + 1 :] if at == 0 else None
            if at == 0 and kernel_first:
                send = [halves[2 * part].reshape(*left, block_rows, grid_size)]
                keep = halves[2 * part + 1].reshape(*left, block_rows, grid_size)
            else:
                send, keep = split_digit(partial, owns[d], size, axes[d])
            got = [exchange(v, (e + 1) * stride, count) for e, v in enumerate(send)]
            partial = reduce_digit(keep, got)
            axes = [a - (a > axes[d]) for a in axes]
        kept.append(partial)
    stride, size = digits[last]
    send, keep = split_digit(jnp.concatenate(kept, -1), owns[last], size, 0)
    got = [exchange(v, (e + 1) * stride, count) for e, v in enumerate(send)]
    summed = reduce_digit(keep, got)
    parts = []
    for part in range(2):
        over_re = summed[:, part * grid_size : part * grid_size + half]
        over_im = summed[:, part * grid_size + half : (part + 1) * grid_size]
        scale = lax.rsqrt(over_re * over_re + over_im * over_im + mode_total)
        parts += [over_re * scale, over_im * scale]
    block = jnp.concatenate(parts, -1).astype(bf16)

    block = gather_digit(block, owns[last], stride, size, 0, count)
    planes = []
    for part, order in enumerate(orders):
        piece = block[..., part * grid_size : (part + 1) * grid_size]
        done = [last]
        for d in reversed(order):
            axis = sum(1 for other in done if other > d)
            piece = gather_digit(piece, owns[d], *digits[d], axis, count)
            done.append(d)
        planes.append(piece.reshape(local_rows, grid_size))
    plane_re = jnp.concatenate([p[:, :half] for p in planes], -1)
    plane_im = jnp.concatenate([p[:, half:] for p in planes], -1)
    phase_plane = jnp.concatenate([plane_re, plane_im], -1)

    fore = forward[0].astype(f32)
    fore_re, fore_im = fore[:, :grid_size], fore[:, grid_size:]
    shaped = []
    for part, plane in enumerate(planes):
        cols = slice(part * half, (part + 1) * half)
        real, imag = plane[:, :half].astype(f32), plane[:, half:].astype(f32)
        from_re, from_im = fore_re[:, cols], fore_im[:, cols]
        rows = [from_re * real - from_im * imag, from_re * imag + from_im * real]
        shaped.append(jnp.concatenate(rows, 0).astype(bf16))
    other = [lax.ppermute(s, "rows", [(0, 1), (1, 0)]) for s in shaped]

    c_re, c_im = propagator(grid_size)
    full_re, full_im = jnp.asarray(c_re, bf16), jnp.asarray(c_im, bf16)
    owners = count if block_rows % 8 == 0 else 1
    order = np.arange(local_rows).reshape(owners, -1)

    def table(cols):
        real, imag = c_re[:local_rows, cols], c_im[:local_rows, cols]
        rows = np.stack([np.concatenate([real, -imag], 1)[order], np.concatenate([imag, real], 1)[order]], 1)
        return jnp.asarray(rows.reshape(2 * local_rows, -1), bf16)

    column_shape = (2 * local_rows, grid_size)
    columns = kernel_call(
        own_kernel, column_shape, f32, matmul // 2, (table(slice(0, local_rows)), *shaped)
    )
    columns, *other = lax.optimization_barrier((columns, *other))
    columns = kernel_call(
        other_kernel, column_shape, bf16, matmul // 2, (table(slice(local_rows, None)), *other, columns)
    )
    blocks = columns.reshape(owners, 2, -1, block_rows, grid_size).transpose(0, 2, 1, 3, 4)
    blocks = blocks.reshape(count, 2 * block_rows, grid_size)
    pixels = lax.all_to_all(blocks, "modes", 0, 0, tiled=True)

    output_fields = kernel_call(
        lambda *refs: fields_kernel(block_rows, *refs),
        (local_rows, double_width),
        bf16,
        matmul,
        (columns, full_re, full_im),
    )
    target_re, target_im = targets.reshape(2, local_rows, grid_size)
    seen = jnp.concatenate(
        [
            times(target_re, full_re) + times(target_im, full_im),
            times(target_im, full_re) - times(target_re, full_im),
        ],
        0,
    ).astype(bf16)
    pixels, output_fields, phase_plane = lax.optimization_barrier((pixels, output_fields, phase_plane))
    term = kernel_call(
        lambda *refs: coupling_kernel(block_rows, *refs),
        (2 * mode_total, mode_total),
        f32,
        matmul,
        (pixels.reshape(column_shape), seen),
    )
    pieces = lax.all_to_all(term, ("modes", "rows"), 0, 0, tiled=True)
    coupling = jnp.sum(pieces, 0, keepdims=True)
    return (phase_plane, output_fields[None], coupling)


def solution(mesh):
    return jax.shard_map(
        local,
        mesh=mesh,
        in_specs=(
            P("modes", "rows", None),
            P("modes", "rows", None),
            P(None, None, ("rows", "modes"), None),
        ),
        out_specs=(P("rows", None), P("modes", "rows", None), P(("modes", "rows"), None)),
        check_vma=False,
    )
```
